32 devices in a mesh: dp: 8 (over z, y), tensor: 4 (over x, core).
Axes of the slice: x: 2, y: 2, z: 4, core: 2. Of those that a mesh axis runs over, the one named last changes fastest.
Arguments:
- word_vectors: bfloat16 [16384, 768], P(('dp', 'tensor')), may hold values from -6 to 6
- position_table: bfloat16 [512, 768], P(('dp', 'tensor')), may hold values from -3 to 3
- horizontal_table: bfloat16 [1024, 768], P(('dp', 'tensor')), may hold values from -3 to 3
- vertical_table: bfloat16 [1024, 768], P(('dp', 'tensor')), may hold values from -3 to 3
- height_table: bfloat16 [1024, 768], P(('dp', 'tensor')), may hold values from -3 to 3
- width_table: bfloat16 [1024, 768], P(('dp', 'tensor')), may hold values from -3 to 3
- embed_gain: float32 [768], replicated, may hold values from 0.25 to 1.75
- embed_shift: float32 [768], replicated, may hold values from -3 to 3
- w_query: bfloat16 [768, 768], P('tensor'), may hold values from -0.21875 to 0.21875
- b_query: float32 [768], P('tensor'), may hold values from -3 to 3
- w_key: bfloat16 [768, 768], P('tensor'), may hold values from -0.21875 to 0.21875
- w_value: bfloat16 [768, 768], P('tensor'), may hold values from -0.21875 to 0.21875
- b_value: float32 [768], P('tensor'), may hold values from -3 to 3
- w_out: bfloat16 [768, 768], P('tensor'), may hold values from -1.25 to 1.25
- b_out: float32 [768], replicated, may hold values from -3 to 3
- attn_gain: float32 [768], replicated, may hold values from 0.25 to 1.75
- attn_shift: float32 [768], replicated, may hold values from -3 to 3
- w_in: bfloat16 [768, 3072], P(None, 'tensor'), may hold values from -0.21875 to 0.21875
- b_in: float32 [3072], P('tensor'), may hold values from -3 to 3
- w_down: bfloat16 [3072, 768], P('tensor'), may hold values from -0.109375 to 0.109375
- b_down: float32 [768], replicated, may hold values from -3 to 3
- ffn_gain: float32 [768], replicated, may hold values from 0.25 to 1.75
- ffn_shift: float32 [768], replicated, may hold values from -3 to 3
- boxes: int32 [4, 16384], P(None, ('dp', 'tensor')), may hold values from 0 to 1023
- segments: int32 [32, 512], P('dp'), may hold values from 0 to 7, never falling along the last dimension, each value on 1 to 128 neighbouring positions
- offsets: int32 [32, 8], P('dp'), may hold values from 0 to 384
- cotangent: float32 [16384, 768], P(('dp', 'tensor')), may hold values from -6 to 6
Outputs:
- layer_out: float32 [16384, 768], P(('dp', 'tensor'))
- grad_word: float32 [16384, 768], P(('dp', 'tensor'))
- grad_position_table: float32 [512, 768], P(('dp', 'tensor'))
- grad_horizontal_table: float32 [1024, 768], P(('dp', 'tensor'))
- grad_vertical_table: float32 [1024, 768], P(('dp', 'tensor'))
- grad_height_table: float32 [1024, 768], P(('dp', 'tensor'))
- grad_width_table: float32 [1024, 768], P(('dp', 'tensor'))
- grad_embed_gain: float32 [768], replicated
- grad_embed_shift: float32 [768], replicated
- grad_w_query: float32 [768, 768], P('tensor')
- grad_b_query: float32 [768], P('tensor')
- grad_w_key: float32 [768, 768], P('tensor')
- grad_w_value: float32 [768, 768], P('tensor')
- grad_b_value: float32 [768], P('tensor')
- grad_w_out: float32 [768, 768], P('tensor')
- grad_b_out: float32 [768], replicated
- grad_attn_gain: float32 [768], replicated
- grad_attn_shift: float32 [768], replicated
- grad_w_in: float32 [768, 3072], P(None, 'tensor')
- grad_b_in: float32 [3072], P('tensor')
- grad_w_down: float32 [3072, 768], P('tensor')
- grad_b_down: float32 [768], replicated
- grad_ffn_gain: float32 [768], replicated
- grad_ffn_shift: float32 [768], replicated
The draws below stay inside these ranges and needn't reach their ends.
Inputs may be any that keep to these rules, and one draw needn't show every extreme that they name: `segments`: in each sequence page ids start at 0 and never fall; each of the 8 pages holds 1 to 128 tokens.
All inputs are finite; a program needn't handle non-finite values.
Results may differ from the reference program's by a relative error of at most 0.014.
Values may be sent and summed in bfloat16 or wider, within the bound.
A program may use at most 128 MiB of HBM per device.

```python
import math
import jax
import jax.numpy as jnp
import numpy as np
from jax import lax

D = 768
HEADS = 12
HEAD = 64
FF = 3072
POS_ROWS = 512
COORD = 1024
SEQ_LEN = 512
PAGES = 8
PAGE_MOST = 128
SEQS = 32
TOKENS = 16384


def set_ends(drawn, rng, low, top_value):
    dims = drawn.shape
    place = [jax.random.randint(jax.random.fold_in(rng, axis), (), 0, dims[axis]) for axis in range(len(dims))]
    drawn = drawn.at[tuple(place)].set(low)
    longest = dims.index(max(dims))
    place[longest] = (place[longest] + 1) % dims[longest]
    return drawn.at[tuple(place)].set(top_value)


def shard_levels(key, dims, shards, low, largest):
    level = 1.0
    for axis_at, shards_of in shards:
        draws = jax.random.uniform(jax.random.fold_in(jax.random.fold_in(key, 6), axis_at), (shards_of,), jnp.float32, low / len(shards), largest / len(shards))
        level = level * jnp.repeat(jnp.exp(draws), dims[axis_at] // shards_of).reshape((-1,) + (1,) * (len(dims) - 1 - axis_at))
    return level


def profile(count, total, limit, skew):
    portions = [(1 << 20) // math.isqrt(grade ** skew) + 1 for grade in range(2, count + 1)]
    rest, holding = total - limit - (count - 1), [1] * (count - 1)
    while rest > 0:
        candidates = [i for i in range(count - 1) if holding[i] < limit]
        pool, remaining = sum([portions[i] for i in candidates]), rest
        for i in candidates:
            extra = min(limit - holding[i], max(1, remaining * portions[i] // pool), rest)
            holding[i] = holding[i] + extra
            rest = rest - extra
    return np.array([limit] + holding)


def ragged(stream_key, amount, total, limit, slope):
    if amount == 2:
        one = jax.random.randint(stream_key, (), max(1, total - limit), min(limit, total - 1) + 1)
        return jnp.stack([one, total - one])
    tallies = jnp.asarray(profile(amount, total, limit, slope), jnp.int32)
    couples = (amount - 1) // 2
    giver, taker = tallies[1:1 + 2 * couples:2], tallies[2:2 + 2 * couples:2]
    margin = jnp.minimum(giver - 1, limit - taker)
    passed = jax.random.randint(jax.random.fold_in(stream_key, 1), (couples,), 0, 1 << 20) % (margin + 1)
    tallies = tallies.at[1:1 + 2 * couples:2].set(giver - passed).at[2:2 + 2 * couples:2].set(taker + passed)
    return tallies[jax.random.permutation(jax.random.fold_in(stream_key, 2), amount)]


def scatter_about(key, dims, spread, reach, cuts=(), held_as=jnp.bfloat16):
    values = spread * jax.random.normal(key, dims, jnp.float32)
    if cuts:
        values = values * shard_levels(key, dims, cuts, -0.22, 0.18)
    return jnp.clip(values, -reach, reach).astype(held_as)


def setup_inputs(seed: int = 0) -> dict:
    seeds = jax.random.split(jax.random.key(seed), 28)
    return {
        "word_vectors": scatter_about(seeds[0], (TOKENS, D), 1.0, 6.0, ((0, 32),)),
        "position_table": scatter_about(seeds[1], (POS_ROWS, D), 0.5, 3.0, ((0, 32),)),
        "horizontal_table": scatter_about(seeds[2], (COORD, D), 0.5, 3.0, ((0, 32),)),
        "vertical_table": scatter_about(seeds[3], (COORD, D), 0.5, 3.0, ((0, 32),)),
        "height_table": scatter_about(seeds[4], (COORD, D), 0.5, 3.0, ((0, 32),)),
        "width_table": scatter_about(seeds[5], (COORD, D), 0.5, 3.0, ((0, 32),)),
        "embed_gain": jnp.clip(1.0 + 0.15 * jax.random.normal(seeds[6], (D,), jnp.float32), 0.25, 1.75),
        "embed_shift": scatter_about(seeds[7], (D,), 0.5, 3.0, (), jnp.float32),
        "w_query": scatter_about(seeds[8], (D, D), D ** -0.5, 0.21875, ((0, 4),)),
        "b_query": scatter_about(seeds[9], (D,), 0.5, 3.0, ((0, 4),), jnp.float32),
        "w_key": scatter_about(seeds[10], (D, D), D ** -0.5, 0.21875, ((0, 4),)),
        "w_value": scatter_about(seeds[11], (D, D), D ** -0.5, 0.21875, ((0, 4),)),
        "b_value": scatter_about(seeds[12], (D,), 0.5, 3.0, ((0, 4),), jnp.float32),
        "w_out": scatter_about(seeds[13], (D, D), (D // 32) ** -0.5, 1.25, ((0, 4),)),
        "b_out": scatter_about(seeds[14], (D,), 0.5, 3.0, (), jnp.float32),
        "attn_gain": jnp.clip(1.0 + 0.15 * jax.random.normal(seeds[15], (D,), jnp.float32), 0.25, 1.75),
        "attn_shift": scatter_about(seeds[16], (D,), 0.5, 3.0, (), jnp.float32),
        "w_in": scatter_about(seeds[17], (D, FF), D ** -0.5, 0.21875, ((1, 4),)),
        "b_in": scatter_about(seeds[18], (FF,), 0.5, 3.0, ((0, 4),), jnp.float32),
        "w_down": scatter_about(seeds[19], (FF, D), FF ** -0.5, 0.109375, ((0, 4),)),
        "b_down": scatter_about(seeds[20], (D,), 0.5, 3.0, (), jnp.float32),
        "ffn_gain": jnp.clip(1.0 + 0.15 * jax.random.normal(seeds[21], (D,), jnp.float32), 0.25, 1.75),
        "ffn_shift": scatter_about(seeds[22], (D,), 0.5, 3.0, (), jnp.float32),
        "boxes": set_ends(jax.random.randint(seeds[23], (4, TOKENS), 0, COORD), jax.random.fold_in(seeds[23], 1), 0, COORD - 1).astype(jnp.int32),
        "segments": jax.vmap(lambda own: jnp.searchsorted(jnp.cumsum(ragged(own, PAGES, SEQ_LEN, PAGE_MOST, 2)), jnp.arange(SEQ_LEN), side="right"))(jax.random.split(seeds[24], SEQS)).reshape((SEQS, SEQ_LEN)).astype(jnp.int32),
        "offsets": set_ends(jax.random.randint(seeds[25], (SEQS, PAGES), 0, POS_ROWS - PAGE_MOST + 1), jax.random.fold_in(seeds[25], 1), 0, POS_ROWS - PAGE_MOST).astype(jnp.int32),
        "cotangent": scatter_about(seeds[26], (TOKENS, D), 1.0, 6.0, ((0, 32),), jnp.float32),
    }


@jax.custom_vjp
def low(v):
    return lax.optimization_barrier(v.astype(jnp.bfloat16)).astype(jnp.float32)

@jax.custom_vjp
def low_back(v):
    return v

def low_keep(v):
    return (low(v), None)

def low_pass(kept, grad):
    return (grad,)

def back_keep(v):
    return (v, None)

def back_low(kept, grad):
    return (low(grad),)
low.defvjp(low_keep, low_pass)
low_back.defvjp(back_keep, back_low)
highest = lax.Precision.HIGHEST
epsilon = 1e-06
masked_score = -1e+30

def matmul(left, right):
    return jnp.dot(left, right, precision=highest, preferred_element_type=jnp.float32)

def page_positions(segments, offsets):
    length = segments.shape[1]
    places = jnp.arange(length, dtype=jnp.int32)
    labels = jnp.arange(offsets.shape[1], dtype=jnp.int32)
    member = segments[:, :, None] == labels[None, None, :]
    starts = lax.optimization_barrier(jnp.min(jnp.where(member, places[None, :, None], length), axis=1))
    page_begin = lax.optimization_barrier(jnp.sum(jnp.where(member, starts[:, None, :], 0), axis=2))
    page_shift = lax.optimization_barrier(jnp.sum(jnp.where(member, offsets[:, None, :], 0), axis=2))
    return (places[None, :] - page_begin + page_shift).astype(jnp.int32)

def layer_norm(values, norm_gain, norm_shift):
    row_mean = lax.optimization_barrier(jnp.mean(values, axis=-1, keepdims=True))
    row_var = lax.optimization_barrier(jnp.mean(values * values, axis=-1, keepdims=True)) - row_mean * row_mean
    return (values - row_mean) * lax.rsqrt(row_var + epsilon) * norm_gain + norm_shift

def attend_group(pieces):
    queries, keys_all, values_all, segments = pieces
    scores = jnp.einsum('sqhd,skhd->shqk', queries, keys_all, precision=highest) * HEAD ** (-0.5)
    same_page = (segments[:, :, None] == segments[:, None, :])[:, None]
    scores = low_back(jnp.where(same_page, scores, masked_score))
    row_peak = lax.optimization_barrier(jnp.max(scores, axis=-1, keepdims=True))
    exponent = jnp.exp(scores - row_peak)
    attention = low(exponent / lax.optimization_barrier(jnp.sum(exponent, axis=-1, keepdims=True)))
    return jnp.einsum('shqk,skhd->sqhd', attention, values_all, precision=highest)

def layer_forward(params, boxes, positions, segments):
    word, position_table, horizontal_table, vertical_table, height_table, width_table, embed_gain, embed_shift, w_query, b_query, w_key, w_value, b_value, w_out, b_out, attn_gain, attn_shift, w_in, b_in, w_down, b_down, ffn_gain, ffn_shift = params
    embedded = word + jnp.take(position_table, positions, axis=0)
    embedded = embedded + jnp.take(horizontal_table, boxes[0], axis=0) + jnp.take(vertical_table, boxes[1], axis=0)
    embedded = embedded + jnp.take(horizontal_table, boxes[2], axis=0) + jnp.take(vertical_table, boxes[3], axis=0)
    embedded = embedded + jnp.take(height_table, jnp.abs(boxes[3] - boxes[1]), axis=0)
    embedded = embedded + jnp.take(width_table, jnp.abs(boxes[2] - boxes[0]), axis=0)
    normed_in = layer_norm(embedded, embed_gain, embed_shift)
    inputs_low = low(normed_in)
    queries = low(low_back(matmul(inputs_low, w_query.T) + b_query))
    keys_all = low(low_back(matmul(inputs_low, w_key.T)))
    values_all = low(low_back(matmul(inputs_low, w_value.T) + b_value))
    grouped = (queries.reshape(SEQS // 4, 4, SEQ_LEN, HEADS, HEAD), keys_all.reshape(SEQS // 4, 4, SEQ_LEN, HEADS, HEAD), values_all.reshape(SEQS // 4, 4, SEQ_LEN, HEADS, HEAD), segments.reshape(SEQS // 4, 4, SEQ_LEN))
    mixed_heads = lax.map(jax.checkpoint(attend_group), grouped).reshape(-1, D)
    mixed_low = low(low_back(mixed_heads))
    attn_branch = low_back(matmul(mixed_low, w_out))
    normed_mid = layer_norm(attn_branch + b_out + normed_in, attn_gain, attn_shift)
    mid_low = low(normed_mid)
    hidden_pre = low_back(matmul(mid_low, w_in) + b_in)
    hidden = low(jax.nn.gelu(hidden_pre, approximate=False))
    ffn_branch = low_back(matmul(hidden, w_down))
    return layer_norm(ffn_branch + b_down + normed_mid, ffn_gain, ffn_shift)

def reference(word_vectors, position_table, horizontal_table, vertical_table, height_table, width_table, embed_gain, embed_shift, w_query, b_query, w_key, w_value, b_value, w_out, b_out, attn_gain, attn_shift, w_in, b_in, w_down, b_down, ffn_gain, ffn_shift, boxes, segments, offsets, cotangent):
    weights = tuple((array.astype(jnp.float32) for array in (word_vectors, position_table, horizontal_table, vertical_table, height_table, width_table, embed_gain, embed_shift, w_query, b_query, w_key, w_value, b_value, w_out, b_out, attn_gain, attn_shift, w_in, b_in, w_down, b_down, ffn_gain, ffn_shift)))
    positions = page_positions(segments, offsets).reshape(-1)

    def forward(*params):
        return layer_forward(params, boxes, positions, segments)
    layer_out, pullback = jax.vjp(forward, *weights)
    gradients = pullback(cotangent.astype(jnp.float32))
    return (layer_out, gradients[0], gradients[1], gradients[2], gradients[3], gradients[4], gradients[5], gradients[6], gradients[7], gradients[8], gradients[9], gradients[10], gradients[11], gradients[12], gradients[13], gradients[14], gradients[15], gradients[16], gradients[17], gradients[18], gradients[19], gradients[20], gradients[21], gradients[22])
```

```python
import functools

import jax
import jax.numpy as jnp
from jax import lax
from jax.experimental import pallas as pl
from jax.experimental.pallas import tpu as pltpu
from jax.sharding import PartitionSpec as P

HEAD = 64
MESH = pl.DeviceIdType.MESH
BF16 = jnp.bfloat16
F32 = jnp.float32

epsilon = 1e-06
masked_score = -1e30


class Place:
    def __init__(self, bits):
        self.bits = bits
        self.dp = lax.axis_index("dp")
        self.t = lax.axis_index("tensor")
        self.core = self.t % 2
        self.half = self.t // 2

    def bit(self, i):
        return (self.dp // 2**i) % 2

    def dp_flip(self, mask):
        dp = self.dp
        for i in range(self.bits):
            if mask & (1 << i):
                dp = dp + 2**i - 2 * 2**i * self.bit(i)
        return dp

    def t_flip(self, mask):
        t = self.t
        if mask & 1:
            t = t + 1 - 2 * self.core
        if mask & 2:
            t = t + 2 - 4 * self.half
        return t

    def partner(self, way):
        if way == "core":
            return (self.dp, self.t_flip(1))
        if way == "half":
            return (self.dp, self.t_flip(2))
        return (self.dp_flip(1 << way), self.t)

    def greet(self):
        barrier = pltpu.get_barrier_semaphore()
        ways = ["core", "half"] + list(range(self.bits))
        for way in ways:
            pl.semaphore_signal(
                barrier, inc=1, device_id=self.partner(way), device_id_type=MESH
            )
        pl.semaphore_wait(barrier, len(ways))


class Links:
    def __init__(self, place, send_sems):
        self.place = place
        self.send_sems = send_sems
        self.sent = []
        self.count = 0

    def send(self, way, src, dst, recv_sem):
        copy = pltpu.make_async_remote_copy(
            src_ref=src,
            dst_ref=dst,
            send_sem=self.send_sems.at[self.count],
            recv_sem=recv_sem,
            device_id=self.place.partner(way),
            device_id_type=MESH,
        )
        copy.start()
        self.count += 1
        self.sent.append(copy)
        return copy

    def arrived(self, way, dst, recv_sem):
        pltpu.make_async_remote_copy(
            src_ref=dst,
            dst_ref=dst,
            send_sem=recv_sem,
            recv_sem=recv_sem,
            device_id=self.place.partner(way),
            device_id_type=MESH,
        ).wait_recv()

    def finish(self):
        for copy in self.sent:
            copy.wait_send()


def interleave(*steps):
    live = list(steps)
    while live:
        for step in list(live):
            try:
                next(step)
            except StopIteration:
                live.remove(step)


def tables_gather(place, links, own, full, sems):
    bits = place.bits
    line_masks = [2 * k for k in range(2 ** (bits - 1))]
    line_sem, half_sem, row_sem, cross_sem, core_sem = sems

    def at(dp_mask, t_mask):
        return full.at[place.dp_flip(dp_mask) * 4 + place.t_flip(t_mask)]

    def to_core(slab, key):
        links.send("core", slab, slab, core_sem.at[key])

    def onward(mask, slab_source, below):
        for b in range(below - 1, 0, -1):
            links.send(b, slab_source, at(mask, 0), line_sem.at[(mask | (1 << b)) // 2])
        links.send("half", slab_source, at(mask, 0), half_sem.at[mask // 2])
        links.send(0, slab_source, at(mask, 0), row_sem.at[mask // 2])
        links.send("core", slab_source, at(mask, 0), core_sem.at[mask * 2])

    onward(0, own, bits)
    yield
    order = []
    held = [0]
    for b in range(bits - 1, 0, -1):
        fresh = [m | (1 << b) for m in held]
        for m in fresh:
            order.append((m, b))
        held = held + fresh
    for mask, b in order:
        links.arrived(b, at(mask, 0), line_sem.at[mask // 2])
        onward(mask, at(mask, 0), b)
        yield
    low = place.bit(1)
    for pair in range(len(line_masks) // 2):
        base = 4 * pair
        for mask in (base, base + 2):
            links.arrived("half", at(mask, 2), half_sem.at[mask // 2])
            to_core(at(mask, 2), mask * 2 + 1)
            links.arrived(0, at(mask + 1, 0), row_sem.at[mask // 2])
            to_core(at(mask + 1, 0), (mask + 1) * 2)
        yield
        dp_other = place.dp_flip(base)
        clear = dp_other - 2 * low
        here_clear = clear * 4 + place.t_flip(2)
        links.send(0, full.at[here_clear], full.at[here_clear], cross_sem.at[2 * pair + low])
        row_dp = place.dp_flip(base + 1)
        raised = row_dp + 2 * (1 - low)
        here_raised = raised * 4 + place.t
        links.send(
            "half", full.at[here_raised], full.at[here_raised], cross_sem.at[2 * pair + 1 - low]
        )
        yield
    for pair in range(len(line_masks) // 2):
        base = 4 * pair
        dp_cross = place.dp_flip(base + 1)
        clear = (dp_cross - 2 * low) * 4 + place.t_flip(2)
        links.arrived(0, full.at[clear], cross_sem.at[2 * pair + low])
        links.send("core", full.at[clear], full.at[clear], core_sem.at[(base + 2 * low + 1) * 2 + 1])
        raised = (dp_cross + 2 * (1 - low)) * 4 + place.t_flip(2)
        links.arrived("half", full.at[raised], cross_sem.at[2 * pair + 1 - low])
        links.send(
            "core", full.at[raised], full.at[raised], core_sem.at[(base + 2 * (1 - low) + 1) * 2 + 1]
        )
        yield
    for mask in range(2**bits):
        for t_mask in (0, 2):
            links.arrived(
                "core", at(mask, t_mask + 1), core_sem.at[mask * 2 + t_mask // 2]
            )
    yield


def weight_gather(place, links, own, full, sems, local_sem):
    rows = own.shape[0] // 2
    near = pl.ds(pl.multiple_of(place.bit(0) * rows, rows), rows)
    far = pl.ds(pl.multiple_of((1 - place.bit(0)) * rows, rows), rows)
    other = place.t_flip(2)
    links.send("half", own.at[near], full.at[place.t, near], sems.at[0])
    links.send("core", own, full.at[place.t], sems.at[2])
    local = pltpu.make_async_copy(own, full.at[place.t], local_sem)
    local.start()
    yield
    links.arrived("half", full.at[other, near], sems.at[0])
    links.send(0, full.at[other, near], full.at[other, near], sems.at[1])
    links.send("core", full.at[other, near], full.at[other, near], sems.at[3])
    yield
    links.arrived(0, full.at[other, far], sems.at[1])
    links.send("core", full.at[other, far], full.at[other, far], sems.at[4])
    yield
    links.arrived("core", full.at[place.t_flip(1)], sems.at[2])
    links.arrived("core", full.at[place.t_flip(3), near], sems.at[3])
    links.arrived("core", full.at[place.t_flip(3), far], sems.at[4])
    local.wait()
    yield


def gather_kernel(
    bits,
    slab,
    square,
    wide,
    tall,
    tables,
    square_full,
    wide_full,
    tall_full,
    send_sems,
    line_sem,
    half_sem,
    row_sem,
    cross_sem,
    core_sem,
    weight_sems,
    local_sems,
):
    place = Place(bits)
    place.greet()
    links = Links(place, send_sems)
    local = pltpu.make_async_copy(
        slab, tables.at[place.dp * 4 + place.t], local_sems.at[3]
    )
    local.start()
    gathers = [
        weight_gather(place, links, own, full, weight_sems.at[i], local_sems.at[i])
        for i, (own, full) in enumerate(
            ((square, square_full), (wide, wide_full), (tall, tall_full))
        )
    ]
    interleave(
        tables_gather(
            place, links, slab, tables, (line_sem, half_sem, row_sem, cross_sem, core_sem)
        ),
        *gathers,
    )
    local.wait()
    links.finish()


def gather_all(devices, slab, square, wide, tall):
    bits = (devices // 4).bit_length() - 1
    lines = 2 ** (bits - 1)
    width = slab.shape[1]
    anywhere = pl.BlockSpec(memory_space=pl.ANY)
    full = jax.ShapeDtypeStruct((4,) + square.shape, BF16)
    return pl.pallas_call(
        functools.partial(gather_kernel, bits),
        out_shape=[jax.ShapeDtypeStruct((devices,) + slab.shape, BF16), full, full, full],
        in_specs=[anywhere] * 4,
        out_specs=[anywhere] * 4,
        scratch_shapes=[
            pltpu.SemaphoreType.DMA((10 * lines + 40 + lines * bits,)),
            pltpu.SemaphoreType.DMA((lines,)),
            pltpu.SemaphoreType.DMA((lines,)),
            pltpu.SemaphoreType.DMA((lines,)),
            pltpu.SemaphoreType.DMA((lines,)),
            pltpu.SemaphoreType.DMA((4 * lines,)),
            pltpu.SemaphoreType.DMA((3, 5)),
            pltpu.SemaphoreType.DMA((4,)),
        ],
        name="gather_all",
        compiler_params=pltpu.CompilerParams(collective_id=0, has_side_effects=True),
    )(slab, square, wide, tall)


def added(left, right):
    return (left.astype(F32) + right.astype(F32)).astype(BF16)


def ladder(rows, bits):
    left = [rows]
    for _ in range(bits):
        left.append(left[-1] // 2 if left[-1] % 32 == 0 else left[-1])
    return left


def weight_reduce(place, links, terms, total, from_core, from_half, from_dp, sems):
    t, other = place.t, place.t_flip(2)
    left = ladder(terms.shape[1], place.bits)
    links.send("core", terms.at[place.t_flip(3)], from_core.at[1], sems.at[1])
    links.send("core", terms.at[place.t_flip(1)], from_core.at[0], sems.at[0])
    yield
    links.arrived("core", from_core.at[1], sems.at[1])
    terms[other] = added(terms[other], from_core[1])
    links.send("half", terms.at[other], from_half, sems.at[2])
    yield
    links.arrived("core", from_core.at[0], sems.at[0])
    terms[t] = added(terms[t], from_core[0])
    yield
    links.arrived("half", from_half, sems.at[2])
    terms[t] = added(terms[t], from_half[...])
    start = 0
    starts = [0]
    used = 0
    for b in range(place.bits):
        rows = left[b + 1]
        halved = rows < left[b]
        mine = start + place.bit(b) * rows if halved else start
        theirs = start + (1 - place.bit(b)) * rows if halved else start
        mine = pl.ds(pl.multiple_of(mine, 16), rows)
        theirs = pl.ds(pl.multiple_of(theirs, 16), rows)
        landing = from_dp.at[pl.ds(used, rows)]
        copy = links.send(b, terms.at[t, theirs], landing, sems.at[3 + b])
        yield
        links.arrived(b, landing, sems.at[3 + b])
        if not halved:
            copy.wait_send()
            links.sent = [other for other in links.sent if other is not copy]
        terms[t, mine] = added(terms[t, mine], from_dp[pl.ds(used, rows)])
        used += rows
        if halved:
            start = start + place.bit(b) * rows
        starts.append(start)
    own = pl.ds(pl.multiple_of(start, 16), left[-1])
    total[own] = terms[t, own]
    for b in range(place.bits - 1, -1, -1):
        rows = left[b + 1]
        if rows == left[b]:
            continue
        mine = pl.ds(pl.multiple_of(starts[b] + place.bit(b) * rows, 16), rows)
        theirs = pl.ds(pl.multiple_of(starts[b] + (1 - place.bit(b)) * rows, 16), rows)
        links.send(b, total.at[mine], total.at[mine], sems.at[3 + place.bits + b])
        yield
        links.arrived(b, total.at[theirs], sems.at[3 + place.bits + b])
    yield


def table_reduce(place, links, terms, columns, order, halves, lines, half_sems, dp_sems):
    bits, core = place.bits, place.core

    def slab(mask, half):
        return terms.at[place.dp_flip(mask), half, core, :, columns]

    def add(mask, half, landed):
        dp = place.dp_flip(mask)
        terms[dp, half, core, :, columns] = added(
            terms[dp, half, core, :, columns], landed[...]
        )

    def lowest(mask):
        return (mask & -mask).bit_length() - 1 if mask else bits

    mine, theirs = place.half, 1 - place.half
    masks = sorted(range(2**bits), key=lambda m: (lowest(m), m))
    slot = 0
    base = {}
    for b in range(bits):
        for h in range(2 if (b == 0 and order == "row") else 1):
            base[b, h] = slot
            slot += 2 ** (bits - 1 - b)

    def index(b, h, mask):
        return base[b, h] + (mask >> (b + 1))

    def send_dp(b, mask, half, h):
        i = index(b, h, mask ^ (1 << b))
        links.send(b, slab(mask, half), lines.at[i], dp_sems.at[i])

    def take_dp(b, mask, half, h):
        i = index(b, h, mask)
        links.arrived(b, lines.at[i], dp_sems.at[i])
        add(mask, half, lines.at[i])

    if order == "half":
        for mask in masks:
            links.send("half", slab(mask, theirs), halves.at[mask], half_sems.at[mask])
        yield
        for mask in masks:
            links.arrived("half", halves.at[mask], half_sems.at[mask])
            add(mask, mine, halves.at[mask])
            if mask & 1:
                send_dp(0, mask, mine, 0)
            yield
    else:
        for h, half in ((1, theirs), (0, mine)):
            for mask in masks:
                if mask & 1:
                    send_dp(0, mask, half, h)
        yield
        kept = [m for m in masks if not m & 1]
        for mask in kept:
            take_dp(0, mask, theirs, 1)
            links.send("half", slab(mask, theirs), halves.at[mask], half_sems.at[mask])
            yield
        for mask in kept:
            take_dp(0, mask, mine, 0)
            yield
        for mask in kept:
            links.arrived("half", halves.at[mask], half_sems.at[mask])
            add(mask, mine, halves.at[mask])
            if bits > 1 and mask & 2:
                send_dp(1, mask, mine, 0)
            yield
    for b in range(0 if order == "half" else 1, bits):
        for mask in masks:
            if mask % (2 << b):
                continue
            take_dp(b, mask, mine, 0)
            if b + 1 < bits and mask & (2 << b):
                send_dp(b + 1, mask, mine, 0)
            yield


def vector_reduce(place, links, vectors, landing, sems):
    for i, way in enumerate(["core", "half"] + list(range(place.bits))):
        copy = links.send(way, vectors.at[i], landing.at[i], sems.at[i])
        yield
        links.arrived(way, landing.at[i], sems.at[i])
        vectors[i + 1] = vectors[i] + landing[i]


def reduce_kernel(
    bits,
    square,
    wide,
    tall,
    tables,
    vectors_in,
    square_sum,
    wide_sum,
    tall_sum,
    table_sum,
    vector_sum,
    from_core,
    from_half,
    from_dp,
    table_core,
    halves,
    lines_half,
    lines_row,
    vectors,
    vector_land,
    send_sems,
    weight_sems,
    core_sems,
    half_sems,
    line_half_sems,
    line_row_sems,
    vector_sems,
):
    place = Place(bits)
    place.greet()
    links = Links(place, send_sems)
    vectors[0] = vectors_in[...]
    split = tables.shape[-1] // 2

    def tables_all():
        theirs, mine = 1 - place.half, place.half
        for i, half in enumerate((theirs, mine)):
            links.send(
                "core",
                tables.at[:, half, 1 - place.core],
                table_core.at[i],
                core_sems.at[i],
            )
        yield
        for i, half in enumerate((theirs, mine)):
            links.arrived("core", table_core.at[i], core_sems.at[i])

            def add(d, carry):
                tables[d, half, place.core] = added(
                    tables[d, half, place.core], table_core[i, d]
                )
                return carry

            lax.fori_loop(0, 2**bits, add, 0)
        yield
        left = table_reduce(
            place,
            links,
            tables,
            pl.ds(0, split),
            "half",
            halves.at[0],
            lines_half,
            half_sems.at[0],
            line_half_sems,
        )
        right = table_reduce(
            place,
            links,
            tables,
            pl.ds(split, split),
            "row",
            halves.at[1],
            lines_row,
            half_sems.at[1],
            line_row_sems,
        )
        live = [left, right]
        while live:
            for step in list(live):
                try:
                    next(step)
                except StopIteration:
                    live.remove(step)
            yield
        table_sum[...] = tables[place.dp, place.half, place.core]

    steps = [
        weight_reduce(
            place,
            links,
            terms,
            total,
            from_core.at[i],
            from_half.at[i],
            from_dp.at[i],
            weight_sems.at[i],
        )
        for i, (terms, total) in enumerate(
            ((square, square_sum), (wide, wide_sum), (tall, tall_sum))
        )
    ]
    interleave(
        tables_all(), *steps, vector_reduce(place, links, vectors, vector_land, vector_sems)
    )
    links.finish()
    vector_sum[...] = vectors[bits + 2]


def reduce_all(devices, square, wide, tall, tables, vectors):
    bits = (devices // 4).bit_length() - 1
    dps = 2**bits
    rows, width = square.shape[1:]
    slab = tables.shape[3]
    landing = sum(ladder(rows, bits)[1:])
    in_vmem = pl.BlockSpec(memory_space=pltpu.VMEM)
    quarter = jax.ShapeDtypeStruct((rows, width), BF16)
    half_lines = dps - 1
    row_lines = dps - 1 + dps // 2
    return pl.pallas_call(
        functools.partial(reduce_kernel, bits),
        out_shape=[
            quarter,
            quarter,
            quarter,
            jax.ShapeDtypeStruct((slab, width), BF16),
            jax.ShapeDtypeStruct(vectors.shape, F32),
        ],
        in_specs=[in_vmem] * 5,
        out_specs=[in_vmem] * 5,
        scratch_shapes=[
            pltpu.VMEM((3, 2, rows, width), BF16),
            pltpu.VMEM((3, rows, width), BF16),
            pltpu.VMEM((3, landing, width), BF16),
            pltpu.VMEM((2, dps, slab, width), BF16),
            pltpu.VMEM((2, dps, slab, width // 2), BF16),
            pltpu.VMEM((half_lines, slab, width // 2), BF16),
            pltpu.VMEM((row_lines, slab, width // 2), BF16),
            pltpu.VMEM((bits + 3,) + vectors.shape, F32),
            pltpu.VMEM((bits + 2,) + vectors.shape, F32),
            pltpu.SemaphoreType.DMA((6 * dps + 60 + 8 * bits,)),
            pltpu.SemaphoreType.DMA((3, 3 + 2 * bits)),
            pltpu.SemaphoreType.DMA((2,)),
            pltpu.SemaphoreType.DMA((2, dps)),
            pltpu.SemaphoreType.DMA((half_lines,)),
            pltpu.SemaphoreType.DMA((row_lines,)),
            pltpu.SemaphoreType.DMA((bits + 2,)),
        ],
        name="reduce_all",
        compiler_params=pltpu.CompilerParams(
            collective_id=1, has_side_effects=True, vmem_limit_bytes=60 * 2**20
        ),
    )(square, wide, tall, tables, vectors)


def product(left, right):
    return jnp.dot(left, right, preferred_element_type=F32)


def inner_rows(left, right):
    return lax.dot_general(left, right, (((0,), (0,)), ((), ())), preferred_element_type=F32)


def against_rows(left, right):
    return lax.dot_general(left, right, (((1,), (1,)), ((), ())), preferred_element_type=F32)


def page_positions(segments, offsets):
    length = segments.shape[1]
    places = jnp.arange(length, dtype=jnp.int32)
    labels = jnp.arange(offsets.shape[1], dtype=jnp.int32)
    member = segments[:, :, None] == labels[None, None, :]
    starts = jnp.min(jnp.where(member, places[None, :, None], length), axis=1)
    page_begin = jnp.sum(jnp.where(member, starts[:, None, :], 0), axis=2)
    page_shift = jnp.sum(jnp.where(member, offsets[:, None, :], 0), axis=2)
    return places[None, :] - page_begin + page_shift


def exact_gelu(values):
    return jax.nn.gelu(values, approximate=False)


def norm_forward(values, norm_gain, norm_shift):
    row_mean = jnp.mean(values, axis=1, keepdims=True)
    row_var = jnp.mean(values * values, axis=1, keepdims=True) - row_mean * row_mean
    scaled = lax.rsqrt(row_var + epsilon)
    centered = (values - row_mean) * scaled
    return (centered * norm_gain + norm_shift, centered, scaled)


def norm_backward(grad_out, centered, scaled, norm_gain):
    grad_centered = grad_out * norm_gain
    first_mean = jnp.mean(grad_centered, axis=1, keepdims=True)
    second_mean = jnp.mean(grad_centered * centered, axis=1, keepdims=True)
    grad_in = scaled * (grad_centered - first_mean - centered * second_mean)
    return (grad_in, jnp.sum(grad_out * centered, axis=0), jnp.sum(grad_out, axis=0))


def split_heads(values):
    return values.reshape(values.shape[0], -1, HEAD)


def page_scores(head_queries, head_keys, same_page):
    scores = jnp.einsum(
        "qhd,khd->hqk", head_queries, head_keys, preferred_element_type=F32
    ) * HEAD ** (-0.5)
    return jnp.where(same_page, scores, masked_score)


def body(
    devices,
    word_vectors,
    position_table,
    horizontal_table,
    vertical_table,
    height_table,
    width_table,
    embed_gain,
    embed_shift,
    w_query,
    b_query,
    w_key,
    w_value,
    b_value,
    w_out,
    b_out,
    attn_gain,
    attn_shift,
    w_in,
    b_in,
    w_down,
    b_down,
    ffn_gain,
    ffn_shift,
    boxes,
    segments,
    offsets,
    cotangent,
):
    own_rows, width = word_vectors.shape
    t = lax.axis_index("tensor")
    owned = (position_table, horizontal_table, vertical_table, height_table, width_table)
    slab_rows = sum(table.shape[0] for table in owned)
    slab_padded = -(-slab_rows // 16) * 16
    slab = jnp.concatenate(owned, axis=0)
    slab = jnp.pad(slab, ((0, slab_padded - slab_rows), (0, 0)))
    square = jnp.concatenate((w_query, w_key, w_value, w_out), axis=0)
    tables, square_full, wide_full, tall_full = gather_all(
        devices, slab, square, w_in, w_down
    )
    tables = tables.reshape(devices * slab_padded, width)
    fourth = w_query.shape[0]
    query_rows, key_rows, value_rows, out_rows = (
        square_full[:, i * fourth : (i + 1) * fourth].reshape(width, width) for i in range(4)
    )
    in_rows = wide_full.transpose(1, 0, 2).reshape(width, -1)
    down_rows = tall_full.reshape(-1, width)
    query_bias, value_bias, in_bias = (
        lax.all_gather(bias, "tensor", axis=0, tiled=True) for bias in (b_query, b_value, b_in)
    )
    own_segments = lax.dynamic_slice_in_dim(segments, t, 1, 0)
    own_offsets = lax.dynamic_slice_in_dim(offsets, t, 1, 0)
    positions = page_positions(own_segments, own_offsets)[0]
    left_edge, top_edge, right_edge, bottom_edge = boxes
    lookups = (
        (0, positions),
        (1, left_edge),
        (2, top_edge),
        (1, right_edge),
        (2, bottom_edge),
        (3, jnp.abs(bottom_edge - top_edge)),
        (4, jnp.abs(right_edge - left_edge)),
    )
    first = [0]
    for table in owned:
        first.append(first[-1] + table.shape[0])
    counts = 0.0
    slots = jnp.arange(devices * slab_padded, dtype=jnp.int32)
    for k, rows in lookups:
        own = owned[k].shape[0]
        row_slots = rows // own * slab_padded + first[k] + rows % own
        counts = counts + (row_slots[:, None] == slots[None, :]).astype(F32)
    counts = counts.astype(BF16)
    embedded = word_vectors.astype(F32) + product(counts, tables)
    normed_in, centered_in, scaled_in = norm_forward(embedded, embed_gain, embed_shift)
    inputs_low = normed_in.astype(BF16)
    queries = (against_rows(inputs_low, query_rows) + query_bias).astype(BF16)
    keys_all = against_rows(inputs_low, key_rows).astype(BF16)
    values_all = (against_rows(inputs_low, value_rows) + value_bias).astype(BF16)
    same_page = own_segments[0][:, None] == own_segments[0][None, :]
    head_queries, head_keys, head_values = (
        split_heads(v) for v in (queries, keys_all, values_all)
    )
    scores = page_scores(head_queries, head_keys, same_page)
    row_peak = jnp.max(scores, axis=-1, keepdims=True)
    exponent = jnp.exp(scores - row_peak)
    row_total = jnp.sum(exponent, axis=-1, keepdims=True)
    again = exponent / row_total
    attention = again.astype(BF16)
    mixed_heads = jnp.einsum("hqk,khd->qhd", attention, head_values, preferred_element_type=F32)
    mixed_low = mixed_heads.reshape(own_rows, -1).astype(BF16)
    normed_mid, centered_mid, scaled_mid = norm_forward(
        product(mixed_low, out_rows) + b_out + normed_in, attn_gain, attn_shift
    )
    mid_low = normed_mid.astype(BF16)
    hidden_pre = product(mid_low, in_rows) + in_bias
    hidden_act, gelu_back = jax.vjp(exact_gelu, hidden_pre)
    hidden = hidden_act.astype(BF16)
    layer_out, centered_out, scaled_out = norm_forward(
        product(hidden, down_rows) + b_down + normed_mid, ffn_gain, ffn_shift
    )
    grad_ffn_sum, grad_ffn_gain, grad_ffn_shift = norm_backward(
        cotangent, centered_out, scaled_out, ffn_gain
    )
    grad_b_down = jnp.sum(grad_ffn_sum, axis=0)
    ffn_low = grad_ffn_sum.astype(BF16)
    grad_hidden = against_rows(ffn_low, down_rows)
    grad_w_down = inner_rows(hidden, ffn_low)
    grad_pre = gelu_back(grad_hidden)[0].astype(BF16)
    grad_b_in = jnp.sum(grad_pre.astype(F32), axis=0)
    grad_w_in = inner_rows(mid_low, grad_pre)
    grad_mid = grad_ffn_sum + against_rows(grad_pre, in_rows)
    grad_attn_sum, grad_attn_gain, grad_attn_shift = norm_backward(
        grad_mid, centered_mid, scaled_mid, attn_gain
    )
    grad_b_out = jnp.sum(grad_attn_sum, axis=0)
    attn_low = grad_attn_sum.astype(BF16)
    grad_mixed = against_rows(attn_low, out_rows)
    grad_w_out = inner_rows(mixed_low, attn_low)
    grad_heads = split_heads(grad_mixed.astype(BF16))
    grad_attention = jnp.einsum(
        "qhd,khd->hqk", grad_heads, head_values, preferred_element_type=F32
    )
    grad_values = jnp.einsum("hqk,qhd->khd", attention, grad_heads, preferred_element_type=F32)
    row_inner = jnp.sum(grad_attention * again, axis=-1, keepdims=True)
    grad_scores = (again * (grad_attention - row_inner)).astype(BF16)
    grad_queries = jnp.einsum(
        "hqk,khd->qhd", grad_scores, head_keys, preferred_element_type=F32
    ) * HEAD ** (-0.5)
    grad_keys = jnp.einsum(
        "hqk,qhd->khd", grad_scores, head_queries, preferred_element_type=F32
    ) * HEAD ** (-0.5)
    grad_queries, grad_keys, grad_values = (
        v.reshape(own_rows, -1).astype(BF16) for v in (grad_queries, grad_keys, grad_values)
    )
    grad_b_query = jnp.sum(grad_queries.astype(F32), axis=0)
    grad_b_value = jnp.sum(grad_values.astype(F32), axis=0)
    grad_square = jnp.stack(
        [
            v.reshape(4, fourth, width)
            for v in (
                inner_rows(grad_queries, inputs_low),
                inner_rows(grad_keys, inputs_low),
                inner_rows(grad_values, inputs_low),
                grad_w_out,
            )
        ],
        axis=1,
    ).reshape(4, width, width)
    grad_in_sum = (
        grad_attn_sum
        + product(grad_queries, query_rows)
        + product(grad_keys, key_rows)
        + product(grad_values, value_rows)
    )
    grad_word, grad_embed_gain, grad_embed_shift = norm_backward(
        grad_in_sum, centered_in, scaled_in, embed_gain
    )
    table_terms = inner_rows(counts, grad_word.astype(BF16)).astype(BF16)
    vectors = jnp.concatenate(
        [
            v.reshape(-1, width)
            for v in (
                grad_embed_gain,
                grad_embed_shift,
                grad_attn_gain,
                grad_attn_shift,
                grad_ffn_gain,
                grad_ffn_shift,
                grad_b_out,
                grad_b_down,
                grad_b_query,
                grad_b_value,
                grad_b_in,
            )
        ],
        axis=0,
    )
    vectors = jnp.pad(vectors, ((0, -vectors.shape[0] % 8), (0, 0)))
    square_sum, wide_sum, tall_sum, table_sum, vector_sum = reduce_all(
        devices,
        grad_square.astype(BF16),
        grad_w_in.reshape(width, 4, -1).transpose(1, 0, 2).astype(BF16),
        grad_w_down.reshape(4, -1, width).astype(BF16),
        table_terms.reshape(devices // 4, 2, 2, slab_padded, width),
        vectors,
    )
    square_sum = square_sum.astype(F32)
    table_sum = table_sum.astype(F32)
    bias_in = lax.dynamic_slice_in_dim(vector_sum[10:14].reshape(-1), t * b_in.shape[0], b_in.shape[0])
    bias_query, bias_value = (
        lax.dynamic_slice_in_dim(vector_sum[i], t * fourth, fourth) for i in (8, 9)
    )
    return (
        layer_out,
        grad_word,
        *(table_sum[first[k] : first[k + 1]] for k in range(5)),
        vector_sum[0],
        vector_sum[1],
        square_sum[:fourth],
        bias_query,
        square_sum[fourth : 2 * fourth],
        square_sum[2 * fourth : 3 * fourth],
        bias_value,
        square_sum[3 * fourth :],
        vector_sum[6],
        vector_sum[2],
        vector_sum[3],
        wide_sum.astype(F32),
        bias_in,
        tall_sum.astype(F32),
        vector_sum[7],
        vector_sum[4],
        vector_sum[5],
    )


def solution(mesh):
    devices = mesh.shape["dp"] * mesh.shape["tensor"]
    both = P(("dp", "tensor"), None)
    rows = P("tensor", None)
    return jax.shard_map(
        functools.partial(body, devices),
        mesh=mesh,
        in_specs=(
            *(both,) * 6,
            P(),
            P(),
            rows,
            P("tensor"),
            rows,
            rows,
            P("tensor"),
            rows,
            P(),
            P(),
            P(),
            P(None, "tensor"),
            P("tensor"),
            rows,
            P(),
            P(),
            P(),
            P(None, ("dp", "tensor")),
            P("dp", None),
            P("dp", None),
            both,
        ),
        out_specs=(
            *(both,) * 7,
            P(),
            P(),
            rows,
            P("tensor"),
            rows,
            rows,
            P("tensor"),
            rows,
            P(),
            P(),
            P(),
            P(None, "tensor"),
            P("tensor"),
            rows,
            P(),
            P(),
            P(),
        ),
        check_vma=False,
    )
```

```python
import functools

import jax
import jax.numpy as jnp
from jax import lax
from jax.experimental import pallas as pl
from jax.experimental.pallas import tpu as pltpu
from jax.sharding import PartitionSpec as P

HEAD = 64
MESH = pl.DeviceIdType.MESH
BF16 = jnp.bfloat16
F32 = jnp.float32

epsilon = 1e-06
masked_score = -1e30


class Place:
    def __init__(self, bits):
        self.bits = bits
        self.dp = lax.axis_index("dp")
        self.t = lax.axis_index("tensor")
        self.core = self.t % 2
        self.half = self.t // 2

    def bit(self, i):
        return (self.dp // 2**i) % 2

    def dp_flip(self, mask):
        dp = self.dp
        for i in range(self.bits):
            if mask & (1 << i):
                dp = dp + 2**i - 2 * 2**i * self.bit(i)
        return dp

    def t_flip(self, mask):
        t = self.t
        if mask & 1:
            t = t + 1 - 2 * self.core
        if mask & 2:
            t = t + 2 - 4 * self.half
        return t

    def partner(self, way):
        if way == "core":
            return (self.dp, self.t_flip(1))
        if way == "half":
            return (self.dp, self.t_flip(2))
        return (self.dp_flip(1 << way), self.t)

    def greet(self):
        barrier = pltpu.get_barrier_semaphore()
        ways = ["core", "half"] + list(range(self.bits))
        for way in ways:
            pl.semaphore_signal(
                barrier, inc=1, device_id=self.partner(way), device_id_type=MESH
            )
        pl.semaphore_wait(barrier, len(ways))


class Links:
    def __init__(self, place, send_sems):
        self.place = place
        self.send_sems = send_sems
        self.sent = []
        self.count = 0

    def send(self, way, src, dst, recv_sem):
        copy = pltpu.make_async_remote_copy(
            src_ref=src,
            dst_ref=dst,
            send_sem=self.send_sems.at[self.count],
            recv_sem=recv_sem,
            device_id=self.place.partner(way),
            device_id_type=MESH,
        )
        copy.start()
        self.count += 1
        self.sent.append(copy)
        return copy

    def arrived(self, way, dst, recv_sem):
        pltpu.make_async_remote_copy(
            src_ref=dst,
            dst_ref=dst,
            send_sem=recv_sem,
            recv_sem=recv_sem,
            device_id=self.place.partner(way),
            device_id_type=MESH,
        ).wait_recv()

    def finish(self):
        for copy in self.sent:
            copy.wait_send()


def interleave(*steps):
    live = list(steps)
    while live:
        for step in list(live):
            try:
                next(step)
            except StopIteration:
                live.remove(step)


def tables_gather(place, links, own, full, sems):
    bits = place.bits
    line_masks = [2 * k for k in range(2 ** (bits - 1))]
    line_sem, half_sem, row_sem, cross_sem, core_sem = sems

    def at(dp_mask, t_mask):
        return full.at[place.dp_flip(dp_mask) * 4 + place.t_flip(t_mask)]

    def to_core(slab, key):
        links.send("core", slab, slab, core_sem.at[key])

    def onward(mask, slab_source, below):
        for b in range(below - 1, 0, -1):
            links.send(b, slab_source, at(mask, 0), line_sem.at[(mask | (1 << b)) // 2])
        links.send("half", slab_source, at(mask, 0), half_sem.at[mask // 2])
        links.send(0, slab_source, at(mask, 0), row_sem.at[mask // 2])
        links.send("core", slab_source, at(mask, 0), core_sem.at[mask * 2])

    onward(0, own, bits)
    yield
    order = []
    held = [0]
    for b in range(bits - 1, 0, -1):
        fresh = [m | (1 << b) for m in held]
        for m in fresh:
            order.append((m, b))
        held = held + fresh
    for mask, b in order:
        links.arrived(b, at(mask, 0), line_sem.at[mask // 2])
        onward(mask, at(mask, 0), b)
        yield
    low = place.bit(1)
    for pair in range(len(line_masks) // 2):
        base = 4 * pair
        for mask in (base, base + 2):
            links.arrived("half", at(mask, 2), half_sem.at[mask // 2])
            to_core(at(mask, 2), mask * 2 + 1)
            links.arrived(0, at(mask + 1, 0), row_sem.at[mask // 2])
            to_core(at(mask + 1, 0), (mask + 1) * 2)
        yield
        dp_other = place.dp_flip(base)
        clear = dp_other - 2 * low
        here_clear = clear * 4 + place.t_flip(2)
        links.send(0, full.at[here_clear], full.at[here_clear], cross_sem.at[2 * pair + low])
        row_dp = place.dp_flip(base + 1)
        raised = row_dp + 2 * (1 - low)
        here_raised = raised * 4 + place.t
        links.send(
            "half", full.at[here_raised], full.at[here_raised], cross_sem.at[2 * pair + 1 - low]
        )
        yield
    def core_arrivals(row):
        for mask in line_masks:
            for t_mask in (0, 2):
                links.arrived(
                    "core",
                    at(mask + row, t_mask + 1),
                    core_sem.at[(mask + row) * 2 + t_mask // 2],
                )

    core_arrivals(0)
    yield "near"
    for pair in range(len(line_masks) // 2):
        base = 4 * pair
        dp_cross = place.dp_flip(base + 1)
        clear = (dp_cross - 2 * low) * 4 + place.t_flip(2)
        links.arrived(0, full.at[clear], cross_sem.at[2 * pair + low])
        links.send("core", full.at[clear], full.at[clear], core_sem.at[(base + 2 * low + 1) * 2 + 1])
        raised = (dp_cross + 2 * (1 - low)) * 4 + place.t_flip(2)
        links.arrived("half", full.at[raised], cross_sem.at[2 * pair + 1 - low])
        links.send(
            "core", full.at[raised], full.at[raised], core_sem.at[(base + 2 * (1 - low) + 1) * 2 + 1]
        )
        yield
    core_arrivals(1)
    yield


def added(left, right):
    return (left.astype(F32) + right.astype(F32)).astype(BF16)


def ladder(rows, bits):
    left = [rows]
    for _ in range(bits):
        left.append(left[-1] // 2 if left[-1] % 32 == 0 else left[-1])
    return left


def weight_reduce(place, links, terms, total, from_core, from_half, from_dp, sems):
    t, other = place.t, place.t_flip(2)
    left = ladder(terms.shape[1], place.bits)
    links.send("core", terms.at[place.t_flip(3)], from_core.at[1], sems.at[1])
    links.send("core", terms.at[place.t_flip(1)], from_core.at[0], sems.at[0])
    yield
    links.arrived("core", from_core.at[1], sems.at[1])
    terms[other] = added(terms[other], from_core[1])
    links.send("half", terms.at[other], from_half, sems.at[2])
    yield
    links.arrived("core", from_core.at[0], sems.at[0])
    terms[t] = added(terms[t], from_core[0])
    yield
    links.arrived("half", from_half, sems.at[2])
    terms[t] = added(terms[t], from_half[...])
    start = 0
    starts = [0]
    used = 0
    for b in range(place.bits):
        rows = left[b + 1]
        halved = rows < left[b]
        mine = start + place.bit(b) * rows if halved else start
        theirs = start + (1 - place.bit(b)) * rows if halved else start
        mine = pl.ds(pl.multiple_of(mine, 16), rows)
        theirs = pl.ds(pl.multiple_of(theirs, 16), rows)
        landing = from_dp.at[pl.ds(used, rows)]
        copy = links.send(b, terms.at[t, theirs], landing, sems.at[3 + b])
        yield
        links.arrived(b, landing, sems.at[3 + b])
        if not halved:
            copy.wait_send()
            links.sent = [other for other in links.sent if other is not copy]
        terms[t, mine] = added(terms[t, mine], from_dp[pl.ds(used, rows)])
        used += rows
        if halved:
            start = start + place.bit(b) * rows
        starts.append(start)
    own = pl.ds(pl.multiple_of(start, 16), left[-1])
    total[own] = terms[t, own]
    for b in range(place.bits - 1, -1, -1):
        rows = left[b + 1]
        if rows == left[b]:
            continue
        mine = pl.ds(pl.multiple_of(starts[b] + place.bit(b) * rows, 16), rows)
        theirs = pl.ds(pl.multiple_of(starts[b] + (1 - place.bit(b)) * rows, 16), rows)
        links.send(b, total.at[mine], total.at[mine], sems.at[3 + place.bits + b])
        yield
        links.arrived(b, total.at[theirs], sems.at[3 + place.bits + b])
    yield


def table_reduce(place, links, terms, columns, order, halves, lines, half_sems, dp_sems):
    bits, core = place.bits, place.core

    def slab(mask, half):
        return terms.at[place.dp_flip(mask), half, core, :, columns]

    def add(mask, half, landed):
        dp = place.dp_flip(mask)
        terms[dp, half, core, :, columns] = added(
            terms[dp, half, core, :, columns], landed[...]
        )

    def lowest(mask):
        return (mask & -mask).bit_length() - 1 if mask else bits

    mine, theirs = place.half, 1 - place.half
    masks = sorted(range(2**bits), key=lambda m: (lowest(m), m))
    slot = 0
    base = {}
    for b in range(bits):
        for h in range(2 if (b == 0 and order == "row") else 1):
            base[b, h] = slot
            slot += 2 ** (bits - 1 - b)

    def index(b, h, mask):
        return base[b, h] + (mask >> (b + 1))

    def send_dp(b, mask, half, h):
        i = index(b, h, mask ^ (1 << b))
        links.send(b, slab(mask, half), lines.at[i], dp_sems.at[i])

    def take_dp(b, mask, half, h):
        i = index(b, h, mask)
        links.arrived(b, lines.at[i], dp_sems.at[i])
        add(mask, half, lines.at[i])

    if order == "half":
        for mask in masks:
            links.send("half", slab(mask, theirs), halves.at[mask], half_sems.at[mask])
        yield
        for mask in masks:
            links.arrived("half", halves.at[mask], half_sems.at[mask])
            add(mask, mine, halves.at[mask])
            if mask & 1:
                send_dp(0, mask, mine, 0)
            yield
    else:
        for h, half in ((1, theirs), (0, mine)):
            for mask in masks:
                if mask & 1:
                    send_dp(0, mask, half, h)
        yield
        kept = [m for m in masks if not m & 1]
        for mask in kept:
            take_dp(0, mask, theirs, 1)
            links.send("half", slab(mask, theirs), halves.at[mask], half_sems.at[mask])
            yield
        for mask in kept:
            take_dp(0, mask, mine, 0)
            yield
        for mask in kept:
            links.arrived("half", halves.at[mask], half_sems.at[mask])
            add(mask, mine, halves.at[mask])
            if bits > 1 and mask & 2:
                send_dp(1, mask, mine, 0)
            yield
    for b in range(0 if order == "half" else 1, bits):
        for mask in masks:
            if mask % (2 << b):
                continue
            take_dp(b, mask, mine, 0)
            if b + 1 < bits and mask & (2 << b):
                send_dp(b + 1, mask, mine, 0)
            yield


def vector_reduce(place, links, vectors, landing, sems):
    for i, way in enumerate(["core", "half"] + list(range(place.bits))):
        copy = links.send(way, vectors.at[i], landing.at[i], sems.at[i])
        yield
        links.arrived(way, landing.at[i], sems.at[i])
        vectors[i + 1] = vectors[i] + landing[i]


def reduce_kernel(
    bits,
    square,
    wide,
    tall,
    tables,
    vectors_in,
    square_sum,
    wide_sum,
    tall_sum,
    table_sum,
    vector_sum,
    from_core,
    from_half,
    from_dp,
    table_core,
    halves,
    lines_half,
    lines_row,
    vectors,
    vector_land,
    send_sems,
    weight_sems,
    core_sems,
    half_sems,
    line_half_sems,
    line_row_sems,
    vector_sems,
):
    place = Place(bits)
    place.greet()
    links = Links(place, send_sems)
    vectors[0] = vectors_in[...]
    split = tables.shape[-1] // 2

    def tables_all():
        theirs, mine = 1 - place.half, place.half
        for i, half in enumerate((theirs, mine)):
            links.send(
                "core",
                tables.at[:, half, 1 - place.core],
                table_core.at[i],
                core_sems.at[i],
            )
        yield
        for i, half in enumerate((theirs, mine)):
            links.arrived("core", table_core.at[i], core_sems.at[i])

            def add(d, carry):
                tables[d, half, place.core] = added(
                    tables[d, half, place.core], table_core[i, d]
                )
                return carry

            lax.fori_loop(0, 2**bits, add, 0)
        yield
        left = table_reduce(
            place,
            links,
            tables,
            pl.ds(0, split),
            "half",
            halves.at[0],
            lines_half,
            half_sems.at[0],
            line_half_sems,
        )
        right = table_reduce(
            place,
            links,
            tables,
            pl.ds(split, split),
            "row",
            halves.at[1],
            lines_row,
            half_sems.at[1],
            line_row_sems,
        )
        live = [left, right]
        while live:
            for step in list(live):
                try:
                    next(step)
                except StopIteration:
                    live.remove(step)
            yield
        table_sum[...] = tables[place.dp, place.half, place.core]

    steps = [
        weight_reduce(
            place,
            links,
            terms,
            total,
            from_core.at[i],
            from_half.at[i],
            from_dp.at[i],
            weight_sems.at[i],
        )
        for i, (terms, total) in enumerate(
            ((square, square_sum), (wide, wide_sum), (tall, tall_sum))
        )
    ]
    interleave(
        tables_all(), *steps, vector_reduce(place, links, vectors, vector_land, vector_sems)
    )
    links.finish()
    vector_sum[...] = vectors[bits + 2]


def reduce_all(devices, square, wide, tall, tables, vectors):
    bits = (devices // 4).bit_length() - 1
    dps = 2**bits
    rows, width = square.shape[1:]
    slab = tables.shape[3]
    landing = sum(ladder(rows, bits)[1:])
    in_vmem = pl.BlockSpec(memory_space=pltpu.VMEM)
    quarter = jax.ShapeDtypeStruct((rows, width), BF16)
    half_lines = dps - 1
    row_lines = dps - 1 + dps // 2
    return pl.pallas_call(
        functools.partial(reduce_kernel, bits),
        out_shape=[
            quarter,
            quarter,
            quarter,
            jax.ShapeDtypeStruct((slab, width), BF16),
            jax.ShapeDtypeStruct(vectors.shape, F32),
        ],
        in_specs=[in_vmem] * 5,
        out_specs=[in_vmem] * 5,
        scratch_shapes=[
            pltpu.VMEM((3, 2, rows, width), BF16),
            pltpu.VMEM((3, rows, width), BF16),
            pltpu.VMEM((3, landing, width), BF16),
            pltpu.VMEM((2, dps, slab, width), BF16),
            pltpu.VMEM((2, dps, slab, width // 2), BF16),
            pltpu.VMEM((half_lines, slab, width // 2), BF16),
            pltpu.VMEM((row_lines, slab, width // 2), BF16),
            pltpu.VMEM((bits + 3,) + vectors.shape, F32),
            pltpu.VMEM((bits + 2,) + vectors.shape, F32),
            pltpu.SemaphoreType.DMA((6 * dps + 60 + 8 * bits,)),
            pltpu.SemaphoreType.DMA((3, 3 + 2 * bits)),
            pltpu.SemaphoreType.DMA((2,)),
            pltpu.SemaphoreType.DMA((2, dps)),
            pltpu.SemaphoreType.DMA((half_lines,)),
            pltpu.SemaphoreType.DMA((row_lines,)),
            pltpu.SemaphoreType.DMA((bits + 2,)),
        ],
        name="reduce_all",
        compiler_params=pltpu.CompilerParams(
            collective_id=1, has_side_effects=True, vmem_limit_bytes=60 * 2**20
        ),
    )(square, wide, tall, tables, vectors)


def product(left, right):
    return jnp.dot(left, right, preferred_element_type=F32)


def inner_rows(left, right):
    return lax.dot_general(left, right, (((0,), (0,)), ((), ())), preferred_element_type=F32)


def against_rows(left, right):
    return lax.dot_general(left, right, (((1,), (1,)), ((), ())), preferred_element_type=F32)


CHUNKS = 2


def chunk_rows(place, weights, j, near):
    side = weights.shape[2] // 2
    rows = side // CHUNKS
    row_bit = place.bit(0) if near else 1 - place.bit(0)
    start = row_bit * side + (j % CHUNKS) * rows
    return j // CHUNKS, pl.ds(pl.multiple_of(start, rows), rows)


class Weights:
    def __init__(self, place, weights, send_sems, recv_sems, own_send, own_recv):
        self.place = place
        self.weights = weights
        self.send_sems = send_sems
        self.recv_sems = recv_sems
        self.own_send = own_send
        self.own_recv = own_recv

    def copy(self, way, lane, j, t, near, to=None):
        matrix, rows = chunk_rows(self.place, self.weights, j, near)
        block = self.weights.at[matrix, t, rows]
        return pltpu.make_async_remote_copy(
            src_ref=block,
            dst_ref=block,
            send_sem=self.send_sems.at[lane, j],
            recv_sem=self.recv_sems.at[lane, j],
            device_id=self.place.partner(way),
            device_id_type=MESH,
        )

    def own(self, i):
        block = self.weights.at[i, self.place.t]
        return pltpu.make_async_remote_copy(
            src_ref=block,
            dst_ref=block,
            send_sem=self.own_send.at[i],
            recv_sem=self.own_recv.at[i],
            device_id=self.place.partner("core"),
            device_id_type=MESH,
        )

    def own_arrived(self, i):
        block = self.weights.at[i, self.place.t_flip(1)]
        pltpu.make_async_remote_copy(
            src_ref=block,
            dst_ref=block,
            send_sem=self.own_send.at[i],
            recv_sem=self.own_recv.at[i],
            device_id=self.place.partner("core"),
            device_id_type=MESH,
        ).wait_recv()

    def issue(self, j):
        self.copy("half", 0, j, self.place.t, True).start()

    def take_half(self, j):
        other = self.place.t_flip(2)
        self.copy("half", 0, j, other, True).wait_recv()
        self.copy(0, 1, j, other, True).start()
        self.copy("core", 2, j, other, True).start()

    def take_row(self, j):
        other = self.place.t_flip(2)
        self.copy(0, 1, j, other, False).wait_recv()
        self.copy("core", 3, j, other, False).start()

    def settle(self, j):
        cross = self.place.t_flip(3)
        self.copy("core", 2, j, cross, True).wait_recv()
        self.copy("core", 3, j, cross, False).wait_recv()

    def finish(self, count):
        for i in range(3):
            self.own(i).wait_send()

        def one(j, carry):
            self.copy("half", 0, j, self.place.t, True).wait_send()
            self.copy(0, 1, j, self.place.t_flip(2), True).wait_send()
            self.copy("core", 2, j, self.place.t_flip(2), True).wait_send()
            self.copy("core", 3, j, self.place.t_flip(2), False).wait_send()
            return carry

        lax.fori_loop(0, count, one, 0)


def row_counts(lookup_rows, device, owns, slab_rows, tokens):
    by_table = ((0, (0,)), (1, (1, 3)), (2, (2, 4)), (3, (5,)), (4, (6,)))
    if all(own % 16 == 0 for own in owns):
        pieces = []
        for k, which in by_table:
            at = lax.broadcasted_iota(jnp.int32, (owns[k], tokens), 0) + device * owns[k]
            piece = sum(jnp.where(at == lookup_rows[w], 1.0, 0.0) for w in which)
            pieces.append(piece.astype(BF16))
        spare = slab_rows - sum(owns)
        if spare:
            pieces.append(jnp.zeros((spare, tokens), BF16))
        return jnp.concatenate(pieces, axis=0)
    at = lax.broadcasted_iota(jnp.int32, (slab_rows, tokens), 0)
    total = jnp.zeros((slab_rows, tokens), F32)
    first = 0
    for k, which in by_table:
        for w in which:
            local = lookup_rows[w] - device * owns[k]
            inside = (local >= 0) & (local < owns[k])
            total = total + jnp.where(at == jnp.where(inside, local + first, -1), 1.0, 0.0)
        first += owns[k]
    return total.astype(BF16)


def lookup_rows_of(boxes, segments, offsets, t):
    tokens = segments.shape[1]
    pages = offsets.shape[1]
    seg = segments[pl.ds(t, 1), :]
    label = lax.broadcasted_iota(jnp.int32, (pages, tokens), 0)
    place_in = lax.broadcasted_iota(jnp.int32, (pages, tokens), 1).astype(F32)
    member = label == seg
    starts = jnp.min(jnp.where(member, place_in, float(tokens)), axis=1, keepdims=True)
    shift_row = offsets[pl.ds(t, 1), :].astype(F32)
    eye = lax.broadcasted_iota(jnp.int32, (pages, pages), 0) == lax.broadcasted_iota(
        jnp.int32, (pages, pages), 1
    )
    shift = jnp.sum(jnp.where(eye, shift_row, 0.0), axis=1, keepdims=True)
    moved = jnp.sum(jnp.where(member, place_in - starts + shift, 0.0), axis=0, keepdims=True)
    positions = moved.astype(jnp.int32)
    x0, y0, x1, y1 = (boxes[i : i + 1, :] for i in range(4))
    return (positions, x0, y0, x1, y1, jnp.abs(y1 - y0), jnp.abs(x1 - x0)), seg


def norm_parts(values):
    width = values.shape[1]
    row_mean = jnp.sum(values, axis=1, keepdims=True) * (1.0 / width)
    row_var = jnp.sum(values * values, axis=1, keepdims=True) * (1.0 / width) - row_mean * row_mean
    scaled = lax.rsqrt(row_var + epsilon)
    return (values - row_mean) * scaled, scaled


ROWS = 64


def by_rows(count, step):
    def one(i, carry):
        step(pl.ds(pl.multiple_of(i * ROWS, ROWS), ROWS))
        return carry

    lax.fori_loop(0, count // ROWS, one, 0)


def head_blocks(tokens):
    half, reach = tokens // 2, 128
    return ((0, half, 0, half + reach), (half, half, half - reach, half + reach))


def mask_pages(segments_row, masks):
    tokens = segments_row.shape[1]
    rows = jnp.broadcast_to(segments_row.astype(F32), (8, tokens))
    columns = jnp.transpose(rows)
    for i, (q, nq, k, nk) in enumerate(head_blocks(tokens)):
        same = columns[k : k + nk, 0:1] == rows[0:1, q : q + nq]
        masks[i] = jnp.where(same, 0.0, masked_score)


def forward_kernel(
    bits,
    owns,
    slab,
    square,
    wide,
    tall,
    vectors,
    word,
    boxes,
    segments,
    offsets,
    cotangent,
    layer_out,
    grad_sum,
    grad_vectors,
    weights_out,
    inputs_low,
    centered_in,
    scaled_in,
    projected,
    mixed,
    stats,
    mid_low,
    centered_mid,
    scaled_mid,
    hidden,
    slopes,
    tables,
    counts,
    weights,
    biases,
    normed,
    total,
    masks,
    send_sems,
    line_sem,
    half_sem,
    row_sem,
    cross_sem,
    core_sem,
    weight_send,
    weight_recv,
    own_send,
    own_recv,
    bias_sems,
    local_sems,
):
    place = Place(bits)
    tokens, width = word.shape
    dps = 2**bits
    slab_rows = slab.shape[0]
    t = place.t
    place.greet()
    links = Links(place, send_sems)
    flow = Weights(place, weights, weight_send, weight_recv, own_send, own_recv)
    chunks = 3 * CHUNKS
    local = pltpu.make_async_copy(slab, tables.at[place.dp * 4 + t], local_sems.at[3])
    local.start()
    owned = [
        pltpu.make_async_copy(source, weights.at[i, t], local_sems.at[i])
        for i, source in enumerate((square, wide, tall))
    ]
    for copy in owned:
        copy.start()
    gather = tables_gather(
        place, links, slab, tables, (line_sem, half_sem, row_sem, cross_sem, core_sem)
    )
    next(gather)
    bias = vectors.at[pl.ds(8, 8)]
    biases[t] = vectors[8:16]
    links.send("core", bias, biases.at[t], bias_sems.at[0])
    links.send("half", bias, biases.at[t], bias_sems.at[1])
    for i, copy in enumerate(owned):
        copy.wait()
        flow.own(i).start()
    flow.issue(0)
    flow.issue(1)

    lookup, seg = lookup_rows_of(boxes, segments, offsets, t)

    def count_dp(dp, carry):
        for j in range(4):
            counts[dp, j * slab_rows : (j + 1) * slab_rows, :] = row_counts(
                lookup, dp * 4 + j, owns, slab_rows, tokens
            )
        return carry

    lax.fori_loop(0, dps, count_dp, 0)
    mask_pages(seg, masks)
    total[...] = word[...].astype(F32)
    local.wait()

    def embed(row_bit):
        def one(i, carry):
            dp = 2 * i + row_bit
            rows = tables[pl.ds(dp * 4, 4)].reshape(4 * slab_rows, width)
            total[...] += inner_rows(counts[dp], rows)
            return carry

        lax.fori_loop(0, dps // 2, one, 0)

    for step in gather:
        if step == "near":
            break
    links.arrived("half", biases.at[place.t_flip(2)], bias_sems.at[1])
    links.send("core", biases.at[place.t_flip(2)], biases.at[place.t_flip(2)], bias_sems.at[2])
    flow.take_half(0)
    flow.issue(2)
    embed(place.bit(0))
    flow.take_half(1)
    flow.issue(3)
    for step in gather:
        pass
    flow.take_row(0)
    embed(1 - place.bit(0))
    flow.take_row(1)

    def norm_in(rows):
        centered, scaled = norm_parts(total[rows])
        centered_in[rows] = centered
        scaled_in[rows] = scaled
        result = centered * vectors[0:1] + vectors[1:2]
        normed[rows] = result
        inputs_low[rows] = result.astype(BF16)

    by_rows(tokens, norm_in)
    links.arrived("core", biases.at[place.t_flip(1)], bias_sems.at[0])
    links.arrived("core", biases.at[place.t_flip(3)], bias_sems.at[2])
    flow.own_arrived(0)
    flow.settle(0)
    flow.settle(1)
    fourth = width // 4

    def project(j, carry):
        columns = jnp.transpose(biases[j])
        zeros = jnp.zeros((fourth, 1), F32)
        column = jnp.concatenate(
            [columns[0:fourth, 1:2], zeros, columns[fourth : 2 * fourth, 1:2]], axis=0
        )
        projected[j] = (
            against_rows(weights[0, j, : 3 * fourth, :], inputs_low[...]) + column
        ).astype(BF16)
        return carry

    lax.fori_loop(0, 4, project, 0)
    flow.take_half(2)
    flow.issue(4)

    def attend(j, carry):
        for h in range(fourth // HEAD):
            rows = slice(h * HEAD, (h + 1) * HEAD)
            key_rows = slice(fourth + h * HEAD, fourth + (h + 1) * HEAD)
            value_rows = slice(2 * fourth + h * HEAD, 2 * fourth + (h + 1) * HEAD)
            for i, (q, nq, k, nk) in enumerate(head_blocks(tokens)):
                scores = (
                    inner_rows(
                        projected[j, key_rows, k : k + nk], projected[j, rows, q : q + nq]
                    )
                    * HEAD ** (-0.5)
                    + masks[i]
                )
                peak = jnp.max(scores, axis=0, keepdims=True)
                exponent = jnp.exp(scores - peak)
                all_of = jnp.sum(exponent, axis=0, keepdims=True)
                stats[j, h : h + 1, q : q + nq] = peak + jnp.log(all_of)
                share = (exponent * (1.0 / all_of)).astype(BF16)
                mixed[j, rows, q : q + nq] = product(
                    projected[j, value_rows, k : k + nk], share
                ).astype(BF16)
        return carry

    def attend_and_pass(j, carry):
        attend(j, carry)

        @pl.when(j < 2)
        def _():
            flow.take_row(j + 2)

        @pl.when(j < 2)
        def _():
            flow.take_half(j + 3)

        @pl.when(j < 1)
        def _():
            flow.issue(j + 5)

        return carry

    lax.fori_loop(0, 4, attend_and_pass, 0)
    out_rows = weights[0, :, 3 * fourth :, :].reshape(width, width)
    total[...] = inner_rows(mixed[...].reshape(width, tokens), out_rows)
    flow.take_row(4)
    flow.take_half(5)

    def norm_mid(rows):
        centered, scaled = norm_parts(total[rows] + vectors[2:3] + normed[rows])
        centered_mid[rows] = centered
        scaled_mid[rows] = scaled
        result = centered * vectors[3:4] + vectors[4:5]
        normed[rows] = result
        mid_low[rows] = result.astype(BF16)

    by_rows(tokens, norm_mid)
    total[...] = jnp.zeros_like(total)
    columns = 256

    def feed(j):
        def one(n, carry):
            at = pl.ds(pl.multiple_of(n * columns, columns), columns)
            before = product(mid_low[...], weights[1, j, :, at]) + biases[j, 0:1, at]
            share = 0.5 * (1.0 + lax.erf(before * 0.5**0.5))
            hidden[j, :, at] = (before * share).astype(BF16)
            density = jnp.exp(before * before * -0.5) * 0.3989422804014327
            slopes[j, :, at] = (share + before * density).astype(BF16)
            return carry

        lax.fori_loop(0, width // columns, one, 0)
        total[...] += product(hidden[j], weights[2, j])

    flow.own_arrived(1)
    flow.own_arrived(2)

    def feed_near(i, carry):
        feed(t + i * (1 - 2 * place.core))
        return carry

    lax.fori_loop(0, 2, feed_near, 0)
    flow.take_row(5)
    for j in range(CHUNKS, chunks):
        flow.settle(j)
    out_copy = pltpu.make_async_copy(weights, weights_out, local_sems.at[0])
    out_copy.start()

    def feed_far(i, carry):
        feed(place.t_flip(2) + i * (1 - 2 * place.core))
        return carry

    lax.fori_loop(0, 2, feed_far, 0)
    grad_vectors[...] = jnp.zeros_like(grad_vectors)

    def norm_out(rows):
        centered, scaled = norm_parts(total[rows] + vectors[5:6] + normed[rows])
        layer_out[rows] = centered * vectors[6:7] + vectors[7:8]
        grad = cotangent[rows]
        grad_sum[rows] = norm_back(grad, centered, scaled, vectors[6:7])
        grad_vectors[0:1] += jnp.sum(grad * centered, axis=0, keepdims=True)
        grad_vectors[1:2] += jnp.sum(grad, axis=0, keepdims=True)
        grad_vectors[2:3] += jnp.sum(grad_sum[rows], axis=0, keepdims=True)

    by_rows(tokens, norm_out)
    out_copy.wait()
    links.finish()
    flow.finish(chunks)


def norm_back(grad_out, centered, scaled, norm_gain):
    width = grad_out.shape[1]
    grad_centered = grad_out * norm_gain
    first_mean = jnp.sum(grad_centered, axis=1, keepdims=True) * (1.0 / width)
    second_mean = jnp.sum(grad_centered * centered, axis=1, keepdims=True) * (1.0 / width)
    return scaled * (grad_centered - first_mean - centered * second_mean)


def forward_all(
    devices, owns, slab, square, wide, tall, vectors, word, boxes, segments, offsets, cotangent
):
    bits = (devices // 4).bit_length() - 1
    dps = 2**bits
    lines = 2 ** (bits - 1)
    tokens, width = word.shape
    anywhere = pl.BlockSpec(memory_space=pl.ANY)
    in_vmem = pl.BlockSpec(memory_space=pltpu.VMEM)
    slab_rows = slab.shape[0]
    fourth = width // 4
    shape = jax.ShapeDtypeStruct
    return pl.pallas_call(
        functools.partial(forward_kernel, bits, owns),
        out_shape=[
            shape((tokens, width), F32),
            shape((tokens, width), F32),
            shape((8, width), F32),
            shape((3, 4, width, width), BF16),
            shape((tokens, width), BF16),
            shape((tokens, width), F32),
            shape((tokens, 1), F32),
            shape((4, 3 * fourth, tokens), BF16),
            shape((4, fourth, tokens), BF16),
            shape((4, 8, tokens), F32),
            shape((tokens, width), BF16),
            shape((tokens, width), F32),
            shape((tokens, 1), F32),
            shape((4, tokens, width), BF16),
            shape((4, tokens, width), BF16),
        ],
        in_specs=[anywhere] * 4 + [in_vmem] * 6,
        out_specs=[in_vmem] * 3 + [anywhere] + [in_vmem] * 11,
        scratch_shapes=[
            pltpu.VMEM((devices, slab_rows, width), BF16),
            pltpu.VMEM((dps, 4 * slab_rows, tokens), BF16),
            pltpu.VMEM((3, 4, width, width), BF16),
            pltpu.VMEM((4, 8, width), F32),
            pltpu.VMEM((tokens, width), F32),
            pltpu.VMEM((tokens, width), F32),
            pltpu.VMEM((2, tokens // 2 + 128, tokens // 2), F32),
            pltpu.SemaphoreType.DMA((10 * lines + 40 + lines * bits,)),
            pltpu.SemaphoreType.DMA((lines,)),
            pltpu.SemaphoreType.DMA((lines,)),
            pltpu.SemaphoreType.DMA((lines,)),
            pltpu.SemaphoreType.DMA((lines,)),
            pltpu.SemaphoreType.DMA((4 * lines,)),
            pltpu.SemaphoreType.DMA((4, 3 * CHUNKS)),
            pltpu.SemaphoreType.DMA((4, 3 * CHUNKS)),
            pltpu.SemaphoreType.DMA((3,)),
            pltpu.SemaphoreType.DMA((3,)),
            pltpu.SemaphoreType.DMA((3,)),
            pltpu.SemaphoreType.DMA((4,)),
        ],
        name="forward_all",
        compiler_params=pltpu.CompilerParams(
            collective_id=0, has_side_effects=True, vmem_limit_bytes=60 * 2**20
        ),
    )(slab, square, wide, tall, vectors, word, boxes, segments, offsets, cotangent)


def page_positions(segments, offsets):
    length = segments.shape[1]
    places = jnp.arange(length, dtype=jnp.int32)
    labels = jnp.arange(offsets.shape[1], dtype=jnp.int32)
    member = segments[:, :, None] == labels[None, None, :]
    starts = jnp.min(jnp.where(member, places[None, :, None], length), axis=1)
    page_begin = jnp.sum(jnp.where(member, starts[:, None, :], 0), axis=2)
    page_shift = jnp.sum(jnp.where(member, offsets[:, None, :], 0), axis=2)
    return places[None, :] - page_begin + page_shift


def norm_backward(grad_out, centered, scaled, norm_gain):
    grad_in = norm_back(grad_out, centered, scaled, norm_gain)
    return (grad_in, jnp.sum(grad_out * centered, axis=0), jnp.sum(grad_out, axis=0))


def body(
    devices,
    word_vectors,
    position_table,
    horizontal_table,
    vertical_table,
    height_table,
    width_table,
    embed_gain,
    embed_shift,
    w_query,
    b_query,
    w_key,
    w_value,
    b_value,
    w_out,
    b_out,
    attn_gain,
    attn_shift,
    w_in,
    b_in,
    w_down,
    b_down,
    ffn_gain,
    ffn_shift,
    boxes,
    segments,
    offsets,
    cotangent,
):
    own_rows, width = word_vectors.shape
    t = lax.axis_index("tensor")
    owned = (position_table, horizontal_table, vertical_table, height_table, width_table)
    slab_rows = sum(table.shape[0] for table in owned)
    slab_padded = -(-slab_rows // 16) * 16
    slab = jnp.concatenate(owned, axis=0)
    slab = jnp.pad(slab, ((0, slab_padded - slab_rows), (0, 0)))
    square = jnp.concatenate((w_query, w_key, w_value, w_out), axis=0)
    fourth = w_query.shape[0]
    bias_rows = jnp.concatenate([b_query, b_value, jnp.zeros((2 * fourth,), F32)])
    vectors_in = jnp.stack(
        [embed_gain, embed_shift, b_out, attn_gain, attn_shift, b_down, ffn_gain, ffn_shift]
        + [b_in, bias_rows]
        + [jnp.zeros_like(b_in)] * 6
    )
    (
        layer_out,
        grad_ffn_sum,
        ffn_vectors,
        weights,
        inputs_low,
        centered_in,
        scaled_in,
        projected,
        mixed,
        stats,
        mid_low,
        centered_mid,
        scaled_mid,
        hidden,
        slopes,
    ) = forward_all(
        devices,
        tuple(table.shape[0] for table in owned),
        slab,
        square,
        w_in,
        w_down,
        vectors_in,
        word_vectors,
        boxes,
        segments,
        offsets,
        cotangent,
    )
    own_segments = lax.dynamic_slice_in_dim(segments, t, 1, 0)
    own_offsets = lax.dynamic_slice_in_dim(offsets, t, 1, 0)
    positions = page_positions(own_segments, own_offsets)[0]
    left_edge, top_edge, right_edge, bottom_edge = boxes
    lookups = (
        (0, positions),
        (1, left_edge),
        (2, top_edge),
        (1, right_edge),
        (2, bottom_edge),
        (3, jnp.abs(bottom_edge - top_edge)),
        (4, jnp.abs(right_edge - left_edge)),
    )
    first = [0]
    for table in owned:
        first.append(first[-1] + table.shape[0])
    counts = 0.0
    slots = jnp.arange(devices * slab_padded, dtype=jnp.int32)
    for k, rows in lookups:
        own = owned[k].shape[0]
        row_slots = rows // own * slab_padded + first[k] + rows % own
        counts = counts + (row_slots[:, None] == slots[None, :]).astype(F32)
    counts = counts.astype(BF16)
    ffn_low = grad_ffn_sum.astype(BF16)
    grad_hidden = jnp.einsum("qd,jfd->jqf", ffn_low, weights[2], preferred_element_type=F32)
    grad_w_down = jnp.einsum("jqf,qd->jfd", hidden, ffn_low, preferred_element_type=F32)
    grad_pre = (grad_hidden * slopes.astype(F32)).astype(BF16)
    grad_b_in = jnp.sum(grad_pre.astype(F32), axis=1).reshape(-1)
    grad_w_in = jnp.einsum("qd,jqf->jdf", mid_low, grad_pre, preferred_element_type=F32)
    grad_mid = grad_ffn_sum + jnp.einsum(
        "jqf,jdf->qd", grad_pre, weights[1], preferred_element_type=F32
    )
    grad_attn_sum, grad_attn_gain, grad_attn_shift = norm_backward(
        grad_mid, centered_mid, scaled_mid, attn_gain
    )
    grad_b_out = jnp.sum(grad_attn_sum, axis=0)
    attn_low = grad_attn_sum.astype(BF16)
    grad_mixed = jnp.einsum(
        "jrd,qd->jrq", weights[0][:, 3 * fourth :], attn_low, preferred_element_type=F32
    ).astype(BF16)
    grad_w_out = jnp.einsum("jrq,qd->jrd", mixed, attn_low, preferred_element_type=F32)
    heads = projected.reshape(4, 3, 3, HEAD, own_rows)
    hq, hk, hv = (heads[:, i].reshape(12, HEAD, own_rows) for i in range(3))
    hm = grad_mixed.reshape(12, HEAD, own_rows)
    same_page = own_segments[0][:, None] == own_segments[0][None, :]
    scores = jnp.einsum("hdk,hdq->hkq", hk, hq, preferred_element_type=F32) * HEAD ** (-0.5)
    again = jnp.exp(
        jnp.where(same_page, scores, masked_score) - stats[:, :3].reshape(12, 1, own_rows)
    )
    grad_att = jnp.einsum("hdk,hdq->hkq", hv, hm, preferred_element_type=F32)
    row_inner = jnp.sum(again * grad_att, axis=1, keepdims=True)
    grad_scores = (again * (grad_att - row_inner)).astype(BF16)
    gq = jnp.einsum("hdk,hkq->hdq", hk, grad_scores, preferred_element_type=F32) * HEAD ** (-0.5)
    gk = jnp.einsum("hdq,hkq->hdk", hq, grad_scores, preferred_element_type=F32) * HEAD ** (-0.5)
    gv = jnp.einsum("hdq,hkq->hdk", hm, again.astype(BF16), preferred_element_type=F32)
    gqkv = jnp.stack([v.reshape(4, fourth, own_rows) for v in (gq, gk, gv)], axis=1)
    gqkv = gqkv.reshape(4, 3 * fourth, own_rows).astype(BF16)
    bias_sums = jnp.sum(gqkv.astype(F32), axis=2)
    grad_b_query = bias_sums[:, :fourth].reshape(-1)
    grad_b_value = bias_sums[:, 2 * fourth :].reshape(-1)
    grad_square = jnp.concatenate(
        [jnp.einsum("jrq,qd->jrd", gqkv, inputs_low, preferred_element_type=F32), grad_w_out], axis=1
    )
    grad_in_sum = grad_attn_sum + jnp.einsum(
        "jrq,jrd->qd", gqkv, weights[0][:, : 3 * fourth], preferred_element_type=F32
    )
    grad_ffn_gain, grad_ffn_shift, grad_b_down = (ffn_vectors[i] for i in range(3))
    grad_word, grad_embed_gain, grad_embed_shift = norm_backward(
        grad_in_sum, centered_in, scaled_in, embed_gain
    )
    table_terms = inner_rows(counts, grad_word.astype(BF16)).astype(BF16)
    vectors = jnp.concatenate(
        [
            v.reshape(-1, width)
            for v in (
                grad_embed_gain,
                grad_embed_shift,
                grad_attn_gain,
                grad_attn_shift,
                grad_ffn_gain,
                grad_ffn_shift,
                grad_b_out,
                grad_b_down,
                grad_b_query,
                grad_b_value,
                grad_b_in,
            )
        ],
        axis=0,
    )
    vectors = jnp.pad(vectors, ((0, -vectors.shape[0] % 8), (0, 0)))
    square_sum, wide_sum, tall_sum, table_sum, vector_sum = reduce_all(
        devices,
        grad_square.astype(BF16),
        grad_w_in.astype(BF16),
        grad_w_down.astype(BF16),
        table_terms.reshape(devices // 4, 2, 2, slab_padded, width),
        vectors,
    )
    square_sum = square_sum.astype(F32)
    table_sum = table_sum.astype(F32)
    bias_in = lax.dynamic_slice_in_dim(vector_sum[10:14].reshape(-1), t * b_in.shape[0], b_in.shape[0])
    bias_query, bias_value = (
        lax.dynamic_slice_in_dim(vector_sum[i], t * fourth, fourth) for i in (8, 9)
    )
    return (
        layer_out,
        grad_word,
        *(table_sum[first[k] : first[k + 1]] for k in range(5)),
        vector_sum[0],
        vector_sum[1],
        square_sum[:fourth],
        bias_query,
        square_sum[fourth : 2 * fourth],
        square_sum[2 * fourth : 3 * fourth],
        bias_value,
        square_sum[3 * fourth :],
        vector_sum[6],
        vector_sum[2],
        vector_sum[3],
        wide_sum.astype(F32),
        bias_in,
        tall_sum.astype(F32),
        vector_sum[7],
        vector_sum[4],
        vector_sum[5],
    )


def solution(mesh):
    devices = mesh.shape["dp"] * mesh.shape["tensor"]
    both = P(("dp", "tensor"), None)
    rows = P("tensor", None)
    return jax.shard_map(
        functools.partial(body, devices),
        mesh=mesh,
        in_specs=(
            *(both,) * 6,
            P(),
            P(),
            rows,
            P("tensor"),
            rows,
            rows,
            P("tensor"),
            rows,
            P(),
            P(),
            P(),
            P(None, "tensor"),
            P("tensor"),
            rows,
            P(),
            P(),
            P(),
            P(None, ("dp", "tensor")),
            P("dp", None),
            P("dp", None),
            both,
        ),
        out_specs=(
            *(both,) * 7,
            P(),
            P(),
            rows,
            P("tensor"),
            rows,
            rows,
            P("tensor"),
            rows,
            P(),
            P(),
            P(),
            P(None, "tensor"),
            P("tensor"),
            rows,
            P(),
            P(),
            P(),
        ),
        check_vma=False,
    )
```

```python
import functools

import jax
import jax.numpy as jnp
from jax import lax
from jax.experimental import pallas as pl
from jax.experimental.pallas import tpu as pltpu
from jax.sharding import PartitionSpec as P

HEAD = 64
MESH = pl.DeviceIdType.MESH
BF16 = jnp.bfloat16
F32 = jnp.float32

epsilon = 1e-06
masked_score = -1e30


class Place:
    def __init__(self, bits):
        self.bits = bits
        self.dp = lax.axis_index("dp")
        self.t = lax.axis_index("tensor")
        self.core = self.t % 2
        self.half = self.t // 2

    def bit(self, i):
        return (self.dp // 2**i) % 2

    def dp_flip(self, mask):
        dp = self.dp
        for i in range(self.bits):
            if mask & (1 << i):
                dp = dp + 2**i - 2 * 2**i * self.bit(i)
        return dp

    def t_flip(self, mask):
        t = self.t
        if mask & 1:
            t = t + 1 - 2 * self.core
        if mask & 2:
            t = t + 2 - 4 * self.half
        return t

    def partner(self, way):
        if way == "core":
            return (self.dp, self.t_flip(1))
        if way == "half":
            return (self.dp, self.t_flip(2))
        return (self.dp_flip(1 << way), self.t)

    def greet(self):
        barrier = pltpu.get_barrier_semaphore()
        ways = ["core", "half"] + list(range(self.bits))
        for way in ways:
            pl.semaphore_signal(
                barrier, inc=1, device_id=self.partner(way), device_id_type=MESH
            )
        pl.semaphore_wait(barrier, len(ways))


class Links:
    def __init__(self, place, send_sems):
        self.place = place
        self.send_sems = send_sems
        self.sent = []
        self.count = 0

    def send(self, way, src, dst, recv_sem):
        copy = pltpu.make_async_remote_copy(
            src_ref=src,
            dst_ref=dst,
            send_sem=self.send_sems.at[self.count],
            recv_sem=recv_sem,
            device_id=self.place.partner(way),
            device_id_type=MESH,
        )
        copy.start()
        self.count += 1
        self.sent.append(copy)
        return copy

    def arrived(self, way, dst, recv_sem):
        pltpu.make_async_remote_copy(
            src_ref=dst,
            dst_ref=dst,
            send_sem=recv_sem,
            recv_sem=recv_sem,
            device_id=self.place.partner(way),
            device_id_type=MESH,
        ).wait_recv()

    def finish(self):
        for copy in self.sent:
            copy.wait_send()


def interleave(*steps):
    live = list(steps)
    while live:
        for step in list(live):
            try:
                next(step)
            except StopIteration:
                live.remove(step)


def tables_gather(place, links, own, full, sems):
    bits = place.bits
    line_masks = [2 * k for k in range(2 ** (bits - 1))]
    line_sem, half_sem, row_sem, cross_sem, core_sem = sems

    def at(dp_mask, t_mask):
        return full.at[place.dp_flip(dp_mask) * 4 + place.t_flip(t_mask)]

    def to_core(slab, key):
        links.send("core", slab, slab, core_sem.at[key])

    def onward(mask, slab_source, below):
        for b in range(below - 1, 0, -1):
            links.send(b, slab_source, at(mask, 0), line_sem.at[(mask | (1 << b)) // 2])
        links.send("half", slab_source, at(mask, 0), half_sem.at[mask // 2])
        links.send(0, slab_source, at(mask, 0), row_sem.at[mask // 2])
        links.send("core", slab_source, at(mask, 0), core_sem.at[mask * 2])

    onward(0, own, bits)
    yield
    order = []
    held = [0]
    for b in range(bits - 1, 0, -1):
        fresh = [m | (1 << b) for m in held]
        for m in fresh:
            order.append((m, b))
        held = held + fresh
    for mask, b in order:
        links.arrived(b, at(mask, 0), line_sem.at[mask // 2])
        onward(mask, at(mask, 0), b)
        yield
    low = place.bit(1)
    for pair in range(len(line_masks) // 2):
        base = 4 * pair
        for mask in (base, base + 2):
            links.arrived("half", at(mask, 2), half_sem.at[mask // 2])
            to_core(at(mask, 2), mask * 2 + 1)
            links.arrived(0, at(mask + 1, 0), row_sem.at[mask // 2])
            to_core(at(mask + 1, 0), (mask + 1) * 2)
        yield
        dp_other = place.dp_flip(base)
        clear = dp_other - 2 * low
        here_clear = clear * 4 + place.t_flip(2)
        links.send(0, full.at[here_clear], full.at[here_clear], cross_sem.at[2 * pair + low])
        row_dp = place.dp_flip(base + 1)
        raised = row_dp + 2 * (1 - low)
        here_raised = raised * 4 + place.t
        links.send(
            "half", full.at[here_raised], full.at[here_raised], cross_sem.at[2 * pair + 1 - low]
        )
        yield
    def core_arrivals(row):
        for mask in line_masks:
            for t_mask in (0, 2):
                links.arrived(
                    "core",
                    at(mask + row, t_mask + 1),
                    core_sem.at[(mask + row) * 2 + t_mask // 2],
                )

    core_arrivals(0)
    yield "near"
    for pair in range(len(line_masks) // 2):
        base = 4 * pair
        dp_cross = place.dp_flip(base + 1)
        clear = (dp_cross - 2 * low) * 4 + place.t_flip(2)
        links.arrived(0, full.at[clear], cross_sem.at[2 * pair + low])
        links.send("core", full.at[clear], full.at[clear], core_sem.at[(base + 2 * low + 1) * 2 + 1])
        raised = (dp_cross + 2 * (1 - low)) * 4 + place.t_flip(2)
        links.arrived("half", full.at[raised], cross_sem.at[2 * pair + 1 - low])
        links.send(
            "core", full.at[raised], full.at[raised], core_sem.at[(base + 2 * (1 - low) + 1) * 2 + 1]
        )
        yield
    core_arrivals(1)
    yield


def added(left, right):
    return (left.astype(F32) + right.astype(F32)).astype(BF16)


def product(left, right):
    return jnp.dot(left, right, preferred_element_type=F32)


def inner_rows(left, right):
    return lax.dot_general(left, right, (((0,), (0,)), ((), ())), preferred_element_type=F32)


def against_rows(left, right):
    return lax.dot_general(left, right, (((1,), (1,)), ((), ())), preferred_element_type=F32)


CHUNKS = 2


def chunk_rows(place, weights, j, near):
    side = weights.shape[2] // 2
    rows = side // CHUNKS
    row_bit = place.bit(0) if near else 1 - place.bit(0)
    start = row_bit * side + (j % CHUNKS) * rows
    return j // CHUNKS, pl.ds(pl.multiple_of(start, rows), rows)


class Weights:
    def __init__(self, place, weights, send_sems, recv_sems, own_send, own_recv):
        self.place = place
        self.weights = weights
        self.send_sems = send_sems
        self.recv_sems = recv_sems
        self.own_send = own_send
        self.own_recv = own_recv

    def copy(self, way, lane, j, t, near, to=None):
        matrix, rows = chunk_rows(self.place, self.weights, j, near)
        block = self.weights.at[matrix, t, rows]
        return pltpu.make_async_remote_copy(
            src_ref=block,
            dst_ref=block,
            send_sem=self.send_sems.at[lane, j],
            recv_sem=self.recv_sems.at[lane, j],
            device_id=self.place.partner(way),
            device_id_type=MESH,
        )

    def own(self, i):
        block = self.weights.at[i, self.place.t]
        return pltpu.make_async_remote_copy(
            src_ref=block,
            dst_ref=block,
            send_sem=self.own_send.at[i],
            recv_sem=self.own_recv.at[i],
            device_id=self.place.partner("core"),
            device_id_type=MESH,
        )

    def own_arrived(self, i):
        block = self.weights.at[i, self.place.t_flip(1)]
        pltpu.make_async_remote_copy(
            src_ref=block,
            dst_ref=block,
            send_sem=self.own_send.at[i],
            recv_sem=self.own_recv.at[i],
            device_id=self.place.partner("core"),
            device_id_type=MESH,
        ).wait_recv()

    def issue(self, j):
        self.copy("half", 0, j, self.place.t, True).start()

    def take_half(self, j):
        other = self.place.t_flip(2)
        self.copy("half", 0, j, other, True).wait_recv()
        self.copy(0, 1, j, other, True).start()
        self.copy("core", 2, j, other, True).start()

    def take_row(self, j):
        other = self.place.t_flip(2)
        self.copy(0, 1, j, other, False).wait_recv()
        self.copy("core", 3, j, other, False).start()

    def settle(self, j):
        cross = self.place.t_flip(3)
        self.copy("core", 2, j, cross, True).wait_recv()
        self.copy("core", 3, j, cross, False).wait_recv()

    def finish(self, count):
        for i in range(3):
            self.own(i).wait_send()

        def one(j, carry):
            self.copy("half", 0, j, self.place.t, True).wait_send()
            self.copy(0, 1, j, self.place.t_flip(2), True).wait_send()
            self.copy("core", 2, j, self.place.t_flip(2), True).wait_send()
            self.copy("core", 3, j, self.place.t_flip(2), False).wait_send()
            return carry

        lax.fori_loop(0, count, one, 0)


def row_counts(lookup_rows, device, owns, slab_rows, tokens):
    by_table = ((0, (0,)), (1, (1, 3)), (2, (2, 4)), (3, (5,)), (4, (6,)))
    if all(own % 16 == 0 for own in owns):
        pieces = []
        for k, which in by_table:
            at = lax.broadcasted_iota(jnp.int32, (owns[k], tokens), 0) + device * owns[k]
            piece = sum(jnp.where(at == lookup_rows[w], 1.0, 0.0) for w in which)
            pieces.append(piece.astype(BF16))
        spare = slab_rows - sum(owns)
        if spare:
            pieces.append(jnp.zeros((spare, tokens), BF16))
        return jnp.concatenate(pieces, axis=0)
    at = lax.broadcasted_iota(jnp.int32, (slab_rows, tokens), 0)
    total = jnp.zeros((slab_rows, tokens), F32)
    first = 0
    for k, which in by_table:
        for w in which:
            local = lookup_rows[w] - device * owns[k]
            inside = (local >= 0) & (local < owns[k])
            total = total + jnp.where(at == jnp.where(inside, local + first, -1), 1.0, 0.0)
        first += owns[k]
    return total.astype(BF16)


def lookup_rows_of(boxes, segments, offsets, t):
    tokens = segments.shape[1]
    pages = offsets.shape[1]
    seg = segments[pl.ds(t, 1), :]
    label = lax.broadcasted_iota(jnp.int32, (pages, tokens), 0)
    place_in = lax.broadcasted_iota(jnp.int32, (pages, tokens), 1).astype(F32)
    member = label == seg
    starts = jnp.min(jnp.where(member, place_in, float(tokens)), axis=1, keepdims=True)
    shift_row = offsets[pl.ds(t, 1), :].astype(F32)
    eye = lax.broadcasted_iota(jnp.int32, (pages, pages), 0) == lax.broadcasted_iota(
        jnp.int32, (pages, pages), 1
    )
    shift = jnp.sum(jnp.where(eye, shift_row, 0.0), axis=1, keepdims=True)
    moved = jnp.sum(jnp.where(member, place_in - starts + shift, 0.0), axis=0, keepdims=True)
    positions = moved.astype(jnp.int32)
    x0, y0, x1, y1 = (boxes[i : i + 1, :] for i in range(4))
    return (positions, x0, y0, x1, y1, jnp.abs(y1 - y0), jnp.abs(x1 - x0)), seg


def norm_parts(values):
    width = values.shape[1]
    row_mean = jnp.sum(values, axis=1, keepdims=True) * (1.0 / width)
    row_var = jnp.sum(values * values, axis=1, keepdims=True) * (1.0 / width) - row_mean * row_mean
    scaled = lax.rsqrt(row_var + epsilon)
    return (values - row_mean) * scaled, scaled


ROWS = 64


def by_rows(count, step):
    def one(i, carry):
        step(pl.ds(pl.multiple_of(i * ROWS, ROWS), ROWS))
        return carry

    lax.fori_loop(0, count // ROWS, one, 0)


def head_blocks(tokens):
    half, reach = tokens // 2, 128
    return ((0, half, 0, half + reach), (half, half, half - reach, half + reach))


def mask_pages(segments_row, masks):
    tokens = segments_row.shape[1]
    rows = jnp.broadcast_to(segments_row.astype(F32), (8, tokens))
    columns = jnp.transpose(rows)
    for i, (q, nq, k, nk) in enumerate(head_blocks(tokens)):
        same = columns[k : k + nk, 0:1] == rows[0:1, q : q + nq]
        masks[i] = jnp.where(same, 0.0, masked_score).astype(masks.dtype)


def forward_kernel(
    bits,
    owns,
    slab,
    square,
    wide,
    tall,
    vectors,
    word,
    boxes,
    segments,
    offsets,
    cotangent,
    layer_out,
    grad_sum,
    grad_vectors,
    weights_out,
    inputs_low,
    centered_in,
    scaled_in,
    projected,
    mixed,
    stats,
    mid_low,
    centered_mid,
    scaled_mid,
    hidden,
    slopes,
    tables,
    counts,
    weights,
    biases,
    normed,
    total,
    masks,
    send_sems,
    line_sem,
    half_sem,
    row_sem,
    cross_sem,
    core_sem,
    weight_send,
    weight_recv,
    own_send,
    own_recv,
    bias_sems,
    local_sems,
):
    place = Place(bits)
    tokens, width = word.shape
    dps = 2**bits
    slab_rows = slab.shape[0]
    t = place.t
    place.greet()
    links = Links(place, send_sems)
    flow = Weights(place, weights, weight_send, weight_recv, own_send, own_recv)
    chunks = 3 * CHUNKS
    local = pltpu.make_async_copy(slab, tables.at[place.dp * 4 + t], local_sems.at[3])
    local.start()
    owned = [
        pltpu.make_async_copy(source, weights.at[i, t], local_sems.at[i])
        for i, source in enumerate((square, wide, tall))
    ]
    for copy in owned:
        copy.start()
    gather = tables_gather(
        place, links, slab, tables, (line_sem, half_sem, row_sem, cross_sem, core_sem)
    )
    next(gather)
    bias = vectors.at[pl.ds(8, 8)]
    biases[t] = vectors[8:16]
    links.send("core", bias, biases.at[t], bias_sems.at[0])
    links.send("half", bias, biases.at[t], bias_sems.at[1])
    for i, copy in enumerate(owned):
        copy.wait()
        flow.own(i).start()
    flow.issue(0)
    flow.issue(1)

    lookup, seg = lookup_rows_of(boxes, segments, offsets, t)

    def count_dp(dp, carry):
        for j in range(4):
            counts[dp, j * slab_rows : (j + 1) * slab_rows, :] = row_counts(
                lookup, dp * 4 + j, owns, slab_rows, tokens
            )
        return carry

    lax.fori_loop(0, dps, count_dp, 0)
    mask_pages(seg, masks)
    total[...] = word[...].astype(F32)
    local.wait()

    def embed(row_bit):
        def one(i, carry):
            dp = 2 * i + row_bit
            rows = tables[pl.ds(dp * 4, 4)].reshape(4 * slab_rows, width)
            total[...] += inner_rows(counts[dp], rows)
            return carry

        lax.fori_loop(0, dps // 2, one, 0)

    for step in gather:
        if step == "near":
            break
    links.arrived("half", biases.at[place.t_flip(2)], bias_sems.at[1])
    links.send("core", biases.at[place.t_flip(2)], biases.at[place.t_flip(2)], bias_sems.at[2])
    flow.take_half(0)
    flow.issue(2)
    embed(place.bit(0))
    flow.take_half(1)
    flow.issue(3)
    for step in gather:
        pass
    flow.take_row(0)
    embed(1 - place.bit(0))
    flow.take_row(1)

    def norm_in(rows):
        centered, scaled = norm_parts(total[rows])
        centered_in[rows] = centered.astype(BF16)
        scaled_in[rows] = scaled
        result = centered * vectors[0:1] + vectors[1:2]
        normed[rows] = result
        inputs_low[rows] = result.astype(BF16)

    by_rows(tokens, norm_in)
    links.arrived("core", biases.at[place.t_flip(1)], bias_sems.at[0])
    links.arrived("core", biases.at[place.t_flip(3)], bias_sems.at[2])
    flow.own_arrived(0)
    flow.settle(0)
    flow.settle(1)
    fourth = width // 4

    def project(j, carry):
        columns = jnp.transpose(biases[j])
        zeros = jnp.zeros((fourth, 1), F32)
        column = jnp.concatenate(
            [columns[0:fourth, 1:2], zeros, columns[fourth : 2 * fourth, 1:2]], axis=0
        )
        projected[j] = (
            against_rows(weights[0, j, : 3 * fourth, :], inputs_low[...]) + column
        ).astype(BF16)
        return carry

    lax.fori_loop(0, 4, project, 0)
    flow.take_half(2)
    flow.issue(4)

    def attend(j, carry):
        for h in range(fourth // HEAD):
            rows = slice(h * HEAD, (h + 1) * HEAD)
            key_rows = slice(fourth + h * HEAD, fourth + (h + 1) * HEAD)
            value_rows = slice(2 * fourth + h * HEAD, 2 * fourth + (h + 1) * HEAD)
            for i, (q, nq, k, nk) in enumerate(head_blocks(tokens)):
                scores = (
                    inner_rows(
                        projected[j, key_rows, k : k + nk], projected[j, rows, q : q + nq]
                    )
                    * HEAD ** (-0.5)
                    + masks[i]
                )
                peak = jnp.max(scores, axis=0, keepdims=True)
                exponent = jnp.exp(scores - peak)
                all_of = jnp.sum(exponent, axis=0, keepdims=True)
                stats[j, h : h + 1, q : q + nq] = peak + jnp.log(all_of)
                share = (exponent * (1.0 / all_of)).astype(BF16)
                mixed[j, rows, q : q + nq] = product(
                    projected[j, value_rows, k : k + nk], share
                ).astype(BF16)
        return carry

    def attend_and_pass(j, carry):
        attend(j, carry)

        @pl.when(j < 2)
        def _():
            flow.take_row(j + 2)

        @pl.when(j < 2)
        def _():
            flow.take_half(j + 3)

        @pl.when(j < 1)
        def _():
            flow.issue(j + 5)

        return carry

    lax.fori_loop(0, 4, attend_and_pass, 0)
    out_rows = weights[0, :, 3 * fourth :, :].reshape(width, width)
    total[...] = inner_rows(mixed[...].reshape(width, tokens), out_rows)
    flow.take_row(4)
    flow.take_half(5)

    def norm_mid(rows):
        centered, scaled = norm_parts(total[rows] + vectors[2:3] + normed[rows])
        centered_mid[rows] = centered.astype(BF16)
        scaled_mid[rows] = scaled
        result = centered * vectors[3:4] + vectors[4:5]
        normed[rows] = result
        mid_low[rows] = result.astype(BF16)

    by_rows(tokens, norm_mid)
    total[...] = jnp.zeros_like(total)
    columns = 256

    def feed(j):
        def one(n, carry):
            at = pl.ds(pl.multiple_of(n * columns, columns), columns)
            before = product(mid_low[...], weights[1, j, :, at]) + biases[j, 0:1, at]
            share = 0.5 * (1.0 + lax.erf(before * 0.5**0.5))
            hidden[j, :, at] = (before * share).astype(BF16)
            density = jnp.exp(before * before * -0.5) * 0.3989422804014327
            slopes[j, :, at] = (share + before * density).astype(BF16)
            return carry

        lax.fori_loop(0, width // columns, one, 0)
        total[...] += product(hidden[j], weights[2, j])

    flow.own_arrived(1)
    flow.own_arrived(2)

    def feed_near(i, carry):
        feed(t + i * (1 - 2 * place.core))
        return carry

    lax.fori_loop(0, 2, feed_near, 0)
    flow.take_row(5)
    for j in range(CHUNKS, chunks):
        flow.settle(j)
    out_copy = pltpu.make_async_copy(weights, weights_out, local_sems.at[0])
    out_copy.start()

    def feed_far(i, carry):
        feed(place.t_flip(2) + i * (1 - 2 * place.core))
        return carry

    lax.fori_loop(0, 2, feed_far, 0)
    grad_vectors[...] = jnp.zeros_like(grad_vectors)

    def norm_out(rows):
        centered, scaled = norm_parts(total[rows] + vectors[5:6] + normed[rows])
        layer_out[rows] = centered * vectors[6:7] + vectors[7:8]
        grad = cotangent[rows]
        grad_sum[rows] = norm_back(grad, centered, scaled, vectors[6:7])
        grad_vectors[0:1] += jnp.sum(grad * centered, axis=0, keepdims=True)
        grad_vectors[1:2] += jnp.sum(grad, axis=0, keepdims=True)
        grad_vectors[2:3] += jnp.sum(grad_sum[rows], axis=0, keepdims=True)

    by_rows(tokens, norm_out)
    out_copy.wait()
    links.finish()
    flow.finish(chunks)


def norm_back(grad_out, centered, scaled, norm_gain):
    width = grad_out.shape[1]
    grad_centered = grad_out * norm_gain
    first_mean = jnp.sum(grad_centered, axis=1, keepdims=True) * (1.0 / width)
    second_mean = jnp.sum(grad_centered * centered, axis=1, keepdims=True) * (1.0 / width)
    return scaled * (grad_centered - first_mean - centered * second_mean)


def forward_all(
    devices, owns, slab, square, wide, tall, vectors, word, boxes, segments, offsets, cotangent
):
    bits = (devices // 4).bit_length() - 1
    dps = 2**bits
    lines = 2 ** (bits - 1)
    tokens, width = word.shape
    anywhere = pl.BlockSpec(memory_space=pl.ANY)
    in_vmem = pl.BlockSpec(memory_space=pltpu.VMEM)
    slab_rows = slab.shape[0]
    fourth = width // 4
    shape = jax.ShapeDtypeStruct
    return pl.pallas_call(
        functools.partial(forward_kernel, bits, owns),
        out_shape=[
            shape((tokens, width), F32),
            shape((tokens, width), F32),
            shape((8, width), F32),
            shape((3, 4, width, width), BF16),
            shape((tokens, width), BF16),
            shape((tokens, width), BF16),
            shape((tokens, 1), F32),
            shape((4, 3 * fourth, tokens), BF16),
            shape((4, fourth, tokens), BF16),
            shape((4, 8, tokens), F32),
            shape((tokens, width), BF16),
            shape((tokens, width), BF16),
            shape((tokens, 1), F32),
            shape((4, tokens, width), BF16),
            shape((4, tokens, width), BF16),
        ],
        in_specs=[anywhere] * 4 + [in_vmem] * 6,
        out_specs=[in_vmem] * 3 + [anywhere] + [in_vmem] * 11,
        scratch_shapes=[
            pltpu.VMEM((devices, slab_rows, width), BF16),
            pltpu.VMEM((dps, 4 * slab_rows, tokens), BF16),
            pltpu.VMEM((3, 4, width, width), BF16),
            pltpu.VMEM((4, 8, width), F32),
            pltpu.VMEM((tokens, width), F32),
            pltpu.VMEM((tokens, width), F32),
            pltpu.VMEM((2, tokens // 2 + 128, tokens // 2), F32),
            pltpu.SemaphoreType.DMA((10 * lines + 40 + lines * bits,)),
            pltpu.SemaphoreType.DMA((lines,)),
            pltpu.SemaphoreType.DMA((lines,)),
            pltpu.SemaphoreType.DMA((lines,)),
            pltpu.SemaphoreType.DMA((lines,)),
            pltpu.SemaphoreType.DMA((4 * lines,)),
            pltpu.SemaphoreType.DMA((4, 3 * CHUNKS)),
            pltpu.SemaphoreType.DMA((4, 3 * CHUNKS)),
            pltpu.SemaphoreType.DMA((3,)),
            pltpu.SemaphoreType.DMA((3,)),
            pltpu.SemaphoreType.DMA((3,)),
            pltpu.SemaphoreType.DMA((4,)),
        ],
        name="forward_all",
        compiler_params=pltpu.CompilerParams(
            collective_id=0, has_side_effects=True, vmem_limit_bytes=60 * 2**20
        ),
    )(slab, square, wide, tall, vectors, word, boxes, segments, offsets, cotangent)


def ladder(rows, bits):
    left = [rows]
    for b in range(bits):
        halves = left[-1] % 32 == 0 and b < bits - 1
        left.append(left[-1] // 2 if halves else left[-1])
    return left


SLOTS = 3
PARTS = 3


class Sums:
    def __init__(self, place, outgoing, own, from_core, from_half, from_dp, total, sems, credit):
        self.place = place
        self.outgoing = outgoing
        self.own = own
        self.from_core = from_core
        self.from_half = from_half
        self.from_dp = from_dp
        self.total = total
        self.send_sems, self.recv_sems = sems
        self.credit = credit
        self.rows = own.shape[2]
        self.left = ladder(self.rows, place.bits)
        self.back = [b for b in range(place.bits) if self.left[b + 1] < self.left[b]]

    def copy(self, way, lane, j, src, dst):
        return pltpu.make_async_remote_copy(
            src_ref=src,
            dst_ref=dst,
            send_sem=self.send_sems.at[lane, j],
            recv_sem=self.recv_sems.at[lane, j],
            device_id=self.place.partner(way),
            device_id_type=MESH,
        )

    def start_of(self, level):
        start = 0
        for b in range(level):
            if self.left[b + 1] < self.left[b]:
                start = start + self.place.bit(b) * self.left[b + 1]
        return start

    def span(self, b, near):
        start, rows = self.start_of(b), self.left[b + 1]
        if rows < self.left[b]:
            bit = self.place.bit(b)
            start = start + (bit if near else 1 - bit) * rows
        return pl.ds(pl.multiple_of(start, 16), rows) if b or rows < self.left[0] else pl.ds(0, rows)

    def landing(self, b, j):
        first = sum(self.left[1 : b + 1])
        return self.from_dp.at[j, pl.ds(first, self.left[b + 1])]

    def core(self, j):
        slot = j % SLOTS
        return self.copy("core", 0, j, self.outgoing.at[slot], self.from_core.at[slot])

    def half(self, j):
        return self.copy("half", 1, j, self.own.at[j, 1], self.from_half.at[j])

    def dp(self, b, j):
        return self.copy(
            b, 2 + b, j, self.own.at[j, 0, self.span(b, False)], self.landing(b, j)
        )

    def gather(self, b, j, near=True):
        block = self.total.at[j, self.span(b, near)]
        return self.copy(b, 2 + self.place.bits + b, j, block, block)

    def launch(self, j):
        if j >= SLOTS:
            pl.semaphore_wait(self.credit, 1)
        self.core(j).start()

    def take_core(self, j, count):
        slot = j % SLOTS
        self.core(j).wait_recv()
        for which in (1, 0):
            self.own[j, which] = added(self.own[j, which], self.from_core[slot, which])
        if j + SLOTS < count:
            pl.semaphore_signal(
                self.credit, inc=1, device_id=self.place.partner("core"), device_id_type=MESH
            )

    def take_half(self, j):
        self.half(j).wait_recv()
        span = self.span(0, False)
        self.own[j, 0, span] = added(self.own[j, 0, span], self.from_half[j, span])
        self.dp(0, j).start()
        if self.left[1] < self.left[0]:
            span = self.span(0, True)
            self.own[j, 0, span] = added(self.own[j, 0, span], self.from_half[j, span])

    def take_dp(self, b, j):
        self.dp(b, j).wait_recv()
        span, first = self.span(b, True), sum(self.left[1 : b + 1])
        arrived = self.from_dp[j, pl.ds(first, self.left[b + 1])]
        if b == self.place.bits - 1:
            self.total[j, span] = added(self.own[j, 0, span], arrived)
            if self.back:
                self.gather(self.back[-1], j).start()
            return
        if self.left[b + 1] == self.left[b]:
            self.dp(b, j).wait_send()
        self.own[j, 0, span] = added(self.own[j, 0, span], arrived)
        self.dp(b + 1, j).start()

    def take_back(self, i, j):
        order = self.back[::-1]
        self.gather(order[i], j, False).wait_recv()
        if i + 1 < len(order):
            self.gather(order[i + 1], j).start()

    def stages(self):
        return 1 + self.place.bits + len(self.back)

    def stage(self, s, j):
        if s == 0:
            self.take_half(j)
        elif s <= self.place.bits:
            self.take_dp(s - 1, j)
        else:
            self.take_back(s - 1 - self.place.bits, j)

    def finish(self, count):
        for j in range(max(0, count - SLOTS), count):
            self.core(j).wait_send()

        def one(j, carry):
            self.half(j).wait_send()
            for b in range(self.place.bits):
                if self.left[b + 1] < self.left[b] or b == self.place.bits - 1:
                    self.dp(b, j).wait_send()
            for b in self.back:
                self.gather(b, j).wait_send()
            return carry

        lax.fori_loop(0, count, one, 0)


def table_reduce(place, links, slab_at, width_of, columns, order, halves, lines, half_sems, dp_sems):
    bits = place.bits

    def slab(mask, half):
        return slab_at(place.dp_flip(mask), half).at[:, columns]

    def add(mask, half, landed):
        target = slab(mask, half)
        target[...] = added(target[...], landed[...])

    def lowest(mask):
        return (mask & -mask).bit_length() - 1 if mask else bits

    mine, theirs = place.half, 1 - place.half
    masks = sorted(range(2**bits), key=lambda m: (lowest(m), m))
    slot = 0
    base = {}
    for b in range(bits):
        for h in range(2 if (b == 0 and order == "row") else 1):
            base[b, h] = slot
            slot += 2 ** (bits - 1 - b)

    def index(b, h, mask):
        return base[b, h] + (mask >> (b + 1))

    def send_dp(b, mask, half, h):
        i = index(b, h, mask ^ (1 << b))
        links.send(b, slab(mask, half), lines.at[i], dp_sems.at[i])

    def take_dp(b, mask, half, h):
        i = index(b, h, mask)
        links.arrived(b, lines.at[i], dp_sems.at[i])
        add(mask, half, lines.at[i])

    if order == "half":
        for mask in masks:
            links.send("half", slab(mask, theirs), halves.at[mask], half_sems.at[mask])
        yield
        for mask in masks:
            links.arrived("half", halves.at[mask], half_sems.at[mask])
            add(mask, mine, halves.at[mask])
            if mask & 1:
                send_dp(0, mask, mine, 0)
            yield
    else:
        for h, half in ((1, theirs), (0, mine)):
            for mask in masks:
                if mask & 1:
                    send_dp(0, mask, half, h)
        yield
        kept = [m for m in masks if not m & 1]
        for mask in kept:
            take_dp(0, mask, theirs, 1)
            links.send("half", slab(mask, theirs), halves.at[mask], half_sems.at[mask])
            yield
        for mask in kept:
            take_dp(0, mask, mine, 0)
            yield
        for mask in kept:
            links.arrived("half", halves.at[mask], half_sems.at[mask])
            add(mask, mine, halves.at[mask])
            if bits > 1 and mask & 2:
                send_dp(1, mask, mine, 0)
            yield
    for b in range(0 if order == "half" else 1, bits):
        for mask in masks:
            if mask % (2 << b):
                continue
            take_dp(b, mask, mine, 0)
            if b + 1 < bits and mask & (2 << b):
                send_dp(b + 1, mask, mine, 0)
            yield


def vector_reduce(place, links, vectors, landing, sems):
    for i, way in enumerate(["core", "half"] + list(range(place.bits))):
        links.send(way, vectors.at[i], landing.at[i], sems.at[i])
        yield
        links.arrived(way, landing.at[i], sems.at[i])
        vectors[i + 1] = vectors[i] + landing[i]


def backward_kernel(
    bits,
    owns,
    slab_rows,
    weights_in,
    vectors,
    boxes,
    segments,
    offsets,
    grad_sum,
    ffn_vectors,
    inputs_low,
    centered_in,
    scaled_in,
    projected,
    mixed,
    stats,
    mid_low,
    centered_mid,
    scaled_mid,
    hidden_in,
    slopes_in,
    grad_word,
    weight_sums,
    table_sum,
    vector_sum,
    held,
    hidden,
    slopes,
    outgoing,
    own,
    from_core,
    from_half,
    from_dp,
    halves,
    lines_half,
    lines_row,
    words,
    lookups,
    vector_terms,
    vector_land,
    total,
    low,
    masks,
    grad_heads,
    grad_projected,
    counts,
    send_sems,
    sum_send,
    sum_recv,
    half_sems,
    line_half_sems,
    line_row_sems,
    vector_sems,
    word_sems,
    local_sems,
    credit,
):
    place = Place(bits)
    tokens, width = grad_sum.shape
    dps = 2**bits
    t, core = place.t, place.core
    fourth = width // 4
    part = width // PARTS
    quarter_rows = width
    loads = {}
    for i, (matrix, slot) in enumerate(((2, 0), (1, 1), (0, 0))):
        loads[matrix] = [
            pltpu.make_async_copy(
                weights_in.at[matrix, q],
                held.at[pl.ds((slot * 4 + q) * quarter_rows, quarter_rows)],
                local_sems.at[matrix, q],
            )
            for q in range(4)
        ]
    early = [
        pltpu.make_async_copy(hidden_in, hidden, local_sems.at[3, 0]),
        pltpu.make_async_copy(slopes_in, slopes, local_sems.at[3, 1]),
    ]
    for copy in loads[2] + early + loads[1]:
        copy.start()
    place.greet()
    links = Links(place, send_sems)
    sums = Sums(
        place, outgoing, own, from_core, from_half, from_dp, weight_sums, (sum_send, sum_recv), credit
    )
    chunks = 3 * PARTS

    def quarter(parity, other):
        q = t + other * (2 - 4 * place.half)
        return q + 1 - 2 * core if parity else q

    def held_rows(slot, q, first=0, rows=width):
        start = (slot * 4 + q) * quarter_rows + first
        return held[pl.ds(pl.multiple_of(start, 16), rows)]

    lookup, seg = lookup_rows_of(boxes, segments, offsets, t)
    mask_pages(seg, masks)
    lookups[0] = jnp.concatenate(list(lookup) + [lookup[0]], axis=0)
    links.send("core", lookups.at[0], lookups.at[1], word_sems.at[0])

    def start_rows(rows):
        low[rows] = grad_sum[rows].astype(BF16)

    by_rows(tokens, start_rows)
    vector_terms[0] = jnp.zeros_like(vector_terms[0])
    vector_terms[0, 4:6] = ffn_vectors[0:2]
    vector_terms[0, 7:8] = ffn_vectors[2:3]
    for copy in loads[2] + early:
        copy.wait()

    def chunk(j, term):
        slot = j % SLOTS
        if j >= SLOTS:
            sums.core(j - SLOTS).wait_send()

        def out(i, carry):
            outgoing[slot, i] = term(quarter(1, i)).astype(BF16)
            return carry

        def keep(i, carry):
            own[j, i] = term(quarter(0, i)).astype(BF16)
            return carry

        lax.fori_loop(0, 2, out, 0)
        sums.launch(j)
        lax.fori_loop(0, 2, keep, 0)

    def down_term(part_at, q):
        at = pl.ds(part_at * part, part)
        back = against_rows(low[...], held_rows(0, q, part_at * part, part))
        before = (back * slopes[q, :, at].astype(F32)).astype(BF16)
        slopes[q, :, at] = before
        vector_terms[0, pl.ds(8 + q, 1), at] = jnp.sum(
            before.astype(F32), axis=0, keepdims=True
        )
        return inner_rows(hidden[q, :, at], low[...])

    for p in range(PARTS):
        chunk(p, functools.partial(down_term, p))
        if p:
            sums.take_core(p - 1, chunks)
            sums.half(p - 1).start()
    for copy in loads[0]:
        copy.start()
    sums.take_core(PARTS - 1, chunks)
    for copy in loads[1]:
        copy.wait()
    for p in range(PARTS):
        columns = slice(p * part, (p + 1) * part)
        chunk(PARTS + p, lambda q: inner_rows(mid_low[:, columns], slopes[q]))
        if p:
            sums.take_core(PARTS + p - 1, chunks)
    total[...] = grad_sum[...]

    def mid_term(q, carry):
        total[...] += against_rows(slopes[q], held_rows(1, q))
        return carry

    lax.fori_loop(0, 4, mid_term, 0)
    sums.take_core(2 * PARTS - 1, chunks)

    done = [0]
    stages = sums.stages()

    def tick(limit):
        k = done[0]
        done[0] += 1
        for s in range(stages):
            j = k - s
            if j < 0 or j >= limit:
                continue
            sums.stage(s, j)
            if s == 0 and j + 2 < limit:
                sums.half(j + 2).start()

    def mid_back(rows):
        centered = centered_mid[rows].astype(F32)
        grad = total[rows]
        result = norm_back(grad, centered, scaled_mid[rows], vectors[3:4])
        vector_terms[0, 2:3] += jnp.sum(grad * centered, axis=0, keepdims=True)
        vector_terms[0, 3:4] += jnp.sum(grad, axis=0, keepdims=True)
        vector_terms[0, 6:7] += jnp.sum(result, axis=0, keepdims=True)
        total[rows] = result
        low[rows] = result.astype(BF16)

    by_rows(tokens, mid_back)
    for copy in loads[0]:
        copy.wait()

    def out_back(q, carry):
        grad_heads[q] = against_rows(held_rows(0, q, 3 * fourth, fourth), low[...]).astype(BF16)
        return carry

    lax.fori_loop(0, 4, out_back, 0)
    scale = HEAD ** (-0.5)

    def attend_back(j, carry):
        for h in range(fourth // HEAD):
            rows = slice(h * HEAD, (h + 1) * HEAD)
            key_rows = slice(fourth + h * HEAD, fourth + (h + 1) * HEAD)
            value_rows = slice(2 * fourth + h * HEAD, 2 * fourth + (h + 1) * HEAD)
            grads = []
            for i, (q, nq, k, nk) in enumerate(head_blocks(tokens)):
                queries = projected[j, rows, q : q + nq]
                keys = projected[j, key_rows, k : k + nk]
                values = projected[j, value_rows, k : k + nk]
                grad = grad_heads[j, rows, q : q + nq]
                scores = inner_rows(keys, queries) * scale + masks[i].astype(F32)
                share = jnp.exp(scores - stats[j, h : h + 1, q : q + nq])
                back = inner_rows(values, grad)
                inner = jnp.sum(share * back, axis=0, keepdims=True)
                grad_scores = (share * (back - inner)).astype(BF16)
                grad_projected[j, rows, q : q + nq] = (product(keys, grad_scores) * scale).astype(BF16)
                grads.append(
                    (
                        against_rows(queries, grad_scores) * scale,
                        against_rows(grad, share.astype(BF16)),
                    )
                )
            reach = 128
            for target, (first, second) in zip((key_rows, value_rows), zip(*grads)):
                edge = tokens // 2 - reach
                joined = jnp.concatenate(
                    [
                        first[:, :edge],
                        first[:, edge:] + second[:, : 2 * reach],
                        second[:, 2 * reach :],
                    ],
                    axis=1,
                )
                grad_projected[j, target, :] = joined.astype(BF16)
        ones = jnp.ones((8, tokens), BF16)
        vector_terms[0, pl.ds(12 + j, 1), 0 : 3 * fourth] = against_rows(ones, grad_projected[j])[0:1]
        return carry

    for j in (0, 2):
        lax.fori_loop(j, j + 2, attend_back, 0)
        tick(chunks)

    def square_term(p, q):
        if p < PARTS - 1:
            return product(grad_projected[q, p * part : (p + 1) * part, :], inputs_low[...])
        return jnp.concatenate(
            [
                product(grad_projected[q, p * part :, :], inputs_low[...]),
                product(mixed[q], low[...]),
            ],
            axis=0,
        )

    for p in range(PARTS):
        chunk(2 * PARTS + p, functools.partial(square_term, p))

    def in_term(q, carry):
        total[...] += inner_rows(grad_projected[q], held_rows(0, q, 0, 3 * fourth))
        return carry

    lax.fori_loop(0, 4, in_term, 0)
    for p in range(PARTS):
        sums.take_core(2 * PARTS + p, chunks)

    def in_back(rows):
        centered = centered_in[rows].astype(F32)
        grad = total[rows]
        result = norm_back(grad, centered, scaled_in[rows], vectors[0:1])
        vector_terms[0, 0:1] += jnp.sum(grad * centered, axis=0, keepdims=True)
        vector_terms[0, 1:2] += jnp.sum(grad, axis=0, keepdims=True)
        total[rows] = result
        low[rows] = result.astype(BF16)

    by_rows(tokens, in_back)
    word_copy = pltpu.make_async_copy(total, grad_word, local_sems.at[3, 2])
    word_copy.start()
    links.send("core", low, words, word_sems.at[1])
    links.arrived("core", lookups.at[1], word_sems.at[0])
    tick(chunks)
    links.arrived("core", words, word_sems.at[1])

    def slab_at(dp, half):
        start = (dp * 2 + half) * slab_rows
        return held.at[pl.ds(pl.multiple_of(start, 16), slab_rows)]

    def table_term(dp, carry):
        for i in range(2):
            rows = tuple(lookups[i, w : w + 1, :] for w in range(7))
            for h in range(2):
                counts[i, h * slab_rows : (h + 1) * slab_rows, :] = row_counts(
                    rows, dp * 4 + h * 2 + core, owns, slab_rows, tokens
                )
        start = pl.multiple_of(dp * 2 * slab_rows, 16)
        held[pl.ds(start, 2 * slab_rows)] = (
            product(counts[0], low[...]) + product(counts[1], words[...])
        ).astype(BF16)
        return carry

    lax.fori_loop(0, dps, table_term, 0)
    split = width // 2
    steps = [
        table_reduce(
            place, links, slab_at, width, pl.ds(0, split), "half",
            halves.at[0], lines_half, half_sems.at[0], line_half_sems,
        ),
        table_reduce(
            place, links, slab_at, width, pl.ds(split, split), "row",
            halves.at[1], lines_row, half_sems.at[1], line_row_sems,
        ),
        vector_reduce(place, links, vector_terms, vector_land, vector_sems),
    ]

    def ticks():
        while done[0] < chunks + stages - 1:
            tick(chunks)
            yield
            yield
            yield

    interleave(ticks(), *steps)
    table_sum[...] = slab_at(place.dp, place.half)[...]
    vector_sum[...] = vector_terms[bits + 2]
    word_copy.wait()
    links.finish()
    sums.finish(chunks)


def backward_all(devices, owns, slab_rows, weights, vectors, boxes, segments, offsets, kept):
    bits = (devices // 4).bit_length() - 1
    dps = 2**bits
    tokens, width = kept[0].shape
    anywhere = pl.BlockSpec(memory_space=pl.ANY)
    in_vmem = pl.BlockSpec(memory_space=pltpu.VMEM)
    fourth, part = width // 4, width // PARTS
    chunks = 3 * PARTS
    landing = sum(ladder(part, bits)[1:])
    half_lines = dps - 1
    row_lines = dps - 1 + dps // 2
    held_rows = max(8 * width, 2 * dps * slab_rows)
    shape = jax.ShapeDtypeStruct
    return pl.pallas_call(
        functools.partial(backward_kernel, bits, owns, slab_rows),
        out_shape=[
            shape((tokens, width), F32),
            shape((chunks, part, width), BF16),
            shape((slab_rows, width), BF16),
            shape((16, width), F32),
        ],
        in_specs=[anywhere] + [in_vmem] * (2 + len(kept)) + [anywhere] * 2,
        out_specs=[anywhere] + [in_vmem] * 3,
        scratch_shapes=[
            pltpu.VMEM((held_rows, width), BF16),
            pltpu.VMEM((4, tokens, width), BF16),
            pltpu.VMEM((4, tokens, width), BF16),
            pltpu.VMEM((SLOTS, 2, part, width), BF16),
            pltpu.VMEM((chunks, 2, part, width), BF16),
            pltpu.VMEM((SLOTS, 2, part, width), BF16),
            pltpu.VMEM((chunks, part, width), BF16),
            pltpu.VMEM((chunks, landing, width), BF16),
            pltpu.VMEM((2, dps, slab_rows, width // 2), BF16),
            pltpu.VMEM((half_lines, slab_rows, width // 2), BF16),
            pltpu.VMEM((row_lines, slab_rows, width // 2), BF16),
            pltpu.VMEM((tokens, width), BF16),
            pltpu.VMEM((2, 8, tokens), jnp.int32),
            pltpu.VMEM((bits + 3, 16, width), F32),
            pltpu.VMEM((bits + 2, 16, width), F32),
            pltpu.VMEM((tokens, width), F32),
            pltpu.VMEM((tokens, width), BF16),
            pltpu.VMEM((2, tokens // 2 + 128, tokens // 2), BF16),
            pltpu.VMEM((4, fourth, tokens), BF16),
            pltpu.VMEM((4, 3 * fourth, tokens), BF16),
            pltpu.VMEM((2, 2 * slab_rows, tokens), BF16),
            pltpu.SemaphoreType.DMA((6 * dps + 40,)),
            pltpu.SemaphoreType.DMA((2 + 2 * bits, chunks)),
            pltpu.SemaphoreType.DMA((2 + 2 * bits, chunks)),
            pltpu.SemaphoreType.DMA((2, dps)),
            pltpu.SemaphoreType.DMA((half_lines,)),
            pltpu.SemaphoreType.DMA((row_lines,)),
            pltpu.SemaphoreType.DMA((bits + 2,)),
            pltpu.SemaphoreType.DMA((2,)),
            pltpu.SemaphoreType.DMA((4, 4)),
            pltpu.SemaphoreType.REGULAR,
        ],
        name="backward_all",
        compiler_params=pltpu.CompilerParams(
            collective_id=1, has_side_effects=True, vmem_limit_bytes=60 * 2**20
        ),
    )(weights, vectors, boxes, segments, offsets, *kept)


def body(
    devices,
    word_vectors,
    position_table,
    horizontal_table,
    vertical_table,
    height_table,
    width_table,
    embed_gain,
    embed_shift,
    w_query,
    b_query,
    w_key,
    w_value,
    b_value,
    w_out,
    b_out,
    attn_gain,
    attn_shift,
    w_in,
    b_in,
    w_down,
    b_down,
    ffn_gain,
    ffn_shift,
    boxes,
    segments,
    offsets,
    cotangent,
):
    own_rows, width = word_vectors.shape
    t = lax.axis_index("tensor")
    owned = (position_table, horizontal_table, vertical_table, height_table, width_table)
    slab_rows = sum(table.shape[0] for table in owned)
    slab_padded = -(-slab_rows // 16) * 16
    slab = jnp.concatenate(owned, axis=0)
    slab = jnp.pad(slab, ((0, slab_padded - slab_rows), (0, 0)))
    square = jnp.concatenate((w_query, w_key, w_value, w_out), axis=0)
    fourth = w_query.shape[0]
    bias_rows = jnp.concatenate([b_query, b_value, jnp.zeros((2 * fourth,), F32)])
    vectors = jnp.stack(
        [embed_gain, embed_shift, b_out, attn_gain, attn_shift, b_down, ffn_gain, ffn_shift]
        + [b_in, bias_rows]
        + [jnp.zeros_like(b_in)] * 6
    )
    owns = tuple(table.shape[0] for table in owned)
    layer_out, grad_ffn_sum, ffn_vectors, weights, *kept = forward_all(
        devices,
        owns,
        slab,
        square,
        w_in,
        w_down,
        vectors,
        word_vectors,
        boxes,
        segments,
        offsets,
        cotangent,
    )
    grad_word, weight_sums, table_sum, vector_sum = backward_all(
        devices,
        owns,
        slab_padded,
        weights,
        vectors,
        boxes,
        segments,
        offsets,
        (grad_ffn_sum, ffn_vectors, *kept),
    )
    tall_sum, wide_sum, square_sum = weight_sums.astype(F32).reshape(3, width, width)
    table_sum = table_sum.astype(F32)
    first = [0]
    for own in owns:
        first.append(first[-1] + own)
    bias_in = lax.dynamic_slice_in_dim(vector_sum, 8 + t, 1)[0]
    bias_row = lax.dynamic_slice_in_dim(vector_sum, 12 + t, 1)[0]
    bias_query, bias_value = bias_row[:fourth], bias_row[2 * fourth : 3 * fourth]
    return (
        layer_out,
        grad_word,
        *(table_sum[first[k] : first[k + 1]] for k in range(5)),
        vector_sum[0],
        vector_sum[1],
        square_sum[:fourth],
        bias_query,
        square_sum[fourth : 2 * fourth],
        square_sum[2 * fourth : 3 * fourth],
        bias_value,
        square_sum[3 * fourth :],
        vector_sum[6],
        vector_sum[2],
        vector_sum[3],
        wide_sum,
        bias_in,
        tall_sum,
        vector_sum[7],
        vector_sum[4],
        vector_sum[5],
    )


def solution(mesh):
    devices = mesh.shape["dp"] * mesh.shape["tensor"]
    both = P(("dp", "tensor"), None)
    rows = P("tensor", None)
    return jax.shard_map(
        functools.partial(body, devices),
        mesh=mesh,
        in_specs=(
            *(both,) * 6,
            P(),
            P(),
            rows,
            P("tensor"),
            rows,
            rows,
            P("tensor"),
            rows,
            P(),
            P(),
            P(),
            P(None, "tensor"),
            P("tensor"),
            rows,
            P(),
            P(),
            P(),
            P(None, ("dp", "tensor")),
            P("dp", None),
            P("dp", None),
            both,
        ),
        out_specs=(
            *(both,) * 7,
            P(),
            P(),
            rows,
            P("tensor"),
            rows,
            rows,
            P("tensor"),
            rows,
            P(),
            P(),
            P(),
            P(None, "tensor"),
            P("tensor"),
            rows,
            P(),
            P(),
            P(),
        ),
        check_vma=False,
    )
```

```python
import functools

import jax
import jax.numpy as jnp
from jax import lax
from jax.experimental import pallas as pl
from jax.experimental.pallas import tpu as pltpu
from jax.sharding import PartitionSpec as P

HEAD = 64
MESH = pl.DeviceIdType.MESH
BF16 = jnp.bfloat16
F32 = jnp.float32

epsilon = 1e-06
masked_score = -1e30


class Place:
    def __init__(self, bits):
        self.bits = bits
        self.dp = lax.axis_index("dp")
        self.t = lax.axis_index("tensor")
        self.core = self.t % 2
        self.half = self.t // 2

    def bit(self, i):
        return (self.dp // 2**i) % 2

    def dp_flip(self, mask):
        dp = self.dp
        for i in range(self.bits):
            if mask & (1 << i):
                dp = dp + 2**i - 2 * 2**i * self.bit(i)
        return dp

    def t_flip(self, mask):
        t = self.t
        if mask & 1:
            t = t + 1 - 2 * self.core
        if mask & 2:
            t = t + 2 - 4 * self.half
        return t

    def partner(self, way):
        if way == "core":
            return (self.dp, self.t_flip(1))
        if way == "half":
            return (self.dp, self.t_flip(2))
        return (self.dp_flip(1 << way), self.t)

    def greet(self):
        barrier = pltpu.get_barrier_semaphore()
        ways = ["core", "half"] + list(range(self.bits))
        for way in ways:
            pl.semaphore_signal(
                barrier, inc=1, device_id=self.partner(way), device_id_type=MESH
            )
        pl.semaphore_wait(barrier, len(ways))


class Links:
    def __init__(self, place, send_sems):
        self.place = place
        self.send_sems = send_sems
        self.sent = []
        self.count = 0

    def send(self, way, src, dst, recv_sem):
        copy = pltpu.make_async_remote_copy(
            src_ref=src,
            dst_ref=dst,
            send_sem=self.send_sems.at[self.count],
            recv_sem=recv_sem,
            device_id=self.place.partner(way),
            device_id_type=MESH,
        )
        copy.start()
        self.count += 1
        self.sent.append(copy)
        return copy

    def arrived(self, way, dst, recv_sem):
        pltpu.make_async_remote_copy(
            src_ref=dst,
            dst_ref=dst,
            send_sem=recv_sem,
            recv_sem=recv_sem,
            device_id=self.place.partner(way),
            device_id_type=MESH,
        ).wait_recv()

    def finish(self):
        for copy in self.sent:
            copy.wait_send()


def seldom(steps, times):
    for _ in steps:
        for _ in range(times):
            yield


def interleave(*steps):
    live = list(steps)
    while live:
        for step in list(live):
            try:
                next(step)
            except StopIteration:
                live.remove(step)


def tables_gather(place, links, own, full, sems):
    bits = place.bits
    line_masks = [2 * k for k in range(2 ** (bits - 1))]
    line_sem, half_sem, row_sem, cross_sem, core_sem = sems

    def at(dp_mask, t_mask):
        return full.at[place.dp_flip(dp_mask) * 4 + place.t_flip(t_mask)]

    def to_core(slab, key):
        links.send("core", slab, slab, core_sem.at[key])

    def onward(mask, slab_source, below):
        for b in range(below - 1, 0, -1):
            links.send(b, slab_source, at(mask, 0), line_sem.at[(mask | (1 << b)) // 2])
        links.send("half", slab_source, at(mask, 0), half_sem.at[mask // 2])
        links.send(0, slab_source, at(mask, 0), row_sem.at[mask // 2])
        links.send("core", slab_source, at(mask, 0), core_sem.at[mask * 2])

    onward(0, own, bits)
    yield
    order = []
    held = [0]
    for b in range(bits - 1, 0, -1):
        fresh = [m | (1 << b) for m in held]
        for m in fresh:
            order.append((m, b))
        held = held + fresh
    for mask, b in order:
        links.arrived(b, at(mask, 0), line_sem.at[mask // 2])
        onward(mask, at(mask, 0), b)
        yield
    low = place.bit(1)
    for pair in range(len(line_masks) // 2):
        base = 4 * pair
        for mask in (base, base + 2):
            links.arrived("half", at(mask, 2), half_sem.at[mask // 2])
            to_core(at(mask, 2), mask * 2 + 1)
            links.arrived(0, at(mask + 1, 0), row_sem.at[mask // 2])
            to_core(at(mask + 1, 0), (mask + 1) * 2)
        yield
        dp_other = place.dp_flip(base)
        clear = dp_other - 2 * low
        here_clear = clear * 4 + place.t_flip(2)
        links.send(0, full.at[here_clear], full.at[here_clear], cross_sem.at[2 * pair + low])
        row_dp = place.dp_flip(base + 1)
        raised = row_dp + 2 * (1 - low)
        here_raised = raised * 4 + place.t
        links.send(
            "half", full.at[here_raised], full.at[here_raised], cross_sem.at[2 * pair + 1 - low]
        )
        yield
    def core_arrivals(row):
        for mask in line_masks:
            for t_mask in (0, 2):
                links.arrived(
                    "core",
                    at(mask + row, t_mask + 1),
                    core_sem.at[(mask + row) * 2 + t_mask // 2],
                )

    core_arrivals(0)
    yield "near"
    for pair in range(len(line_masks) // 2):
        base = 4 * pair
        dp_cross = place.dp_flip(base + 1)
        clear = (dp_cross - 2 * low) * 4 + place.t_flip(2)
        links.arrived(0, full.at[clear], cross_sem.at[2 * pair + low])
        links.send("core", full.at[clear], full.at[clear], core_sem.at[(base + 2 * low + 1) * 2 + 1])
        raised = (dp_cross + 2 * (1 - low)) * 4 + place.t_flip(2)
        links.arrived("half", full.at[raised], cross_sem.at[2 * pair + 1 - low])
        links.send(
            "core", full.at[raised], full.at[raised], core_sem.at[(base + 2 * (1 - low) + 1) * 2 + 1]
        )
        yield
    core_arrivals(1)
    yield


def added(left, right):
    return (left.astype(F32) + right.astype(F32)).astype(BF16)


def product(left, right):
    return jnp.dot(left, right, preferred_element_type=F32)


def inner_rows(left, right):
    return lax.dot_general(left, right, (((0,), (0,)), ((), ())), preferred_element_type=F32)


def against_rows(left, right):
    return lax.dot_general(left, right, (((1,), (1,)), ((), ())), preferred_element_type=F32)


CHUNKS = 2


def chunk_rows(place, weights, j, near_row, near_line):
    side = weights.shape[2] // 4
    rows = side // CHUNKS
    row = place.bit(0) if near_row else 1 - place.bit(0)
    line = place.bit(1) if near_line else 1 - place.bit(1)
    start = (2 * row + line) * side + (j % CHUNKS) * rows
    return j // CHUNKS, pl.ds(pl.multiple_of(start, rows), rows)


class Weights:
    def __init__(self, place, weights, send_sems, recv_sems, own_send, own_recv):
        self.place = place
        self.weights = weights
        self.send_sems = send_sems
        self.recv_sems = recv_sems
        self.own_send = own_send
        self.own_recv = own_recv

    def copy(self, way, lane, j, t, near_row=True, near_line=True):
        matrix, rows = chunk_rows(self.place, self.weights, j, near_row, near_line)
        block = self.weights.at[matrix, t, rows]
        return pltpu.make_async_remote_copy(
            src_ref=block,
            dst_ref=block,
            send_sem=self.send_sems.at[lane, j],
            recv_sem=self.recv_sems.at[lane, j],
            device_id=self.place.partner(way),
            device_id_type=MESH,
        )

    def own(self, i):
        block = self.weights.at[i, self.place.t]
        return pltpu.make_async_remote_copy(
            src_ref=block,
            dst_ref=block,
            send_sem=self.own_send.at[i],
            recv_sem=self.own_recv.at[i],
            device_id=self.place.partner("core"),
            device_id_type=MESH,
        )

    def own_arrived(self, i):
        block = self.weights.at[i, self.place.t_flip(1)]
        pltpu.make_async_remote_copy(
            src_ref=block,
            dst_ref=block,
            send_sem=self.own_send.at[i],
            recv_sem=self.own_recv.at[i],
            device_id=self.place.partner("core"),
            device_id_type=MESH,
        ).wait_recv()

    def issue(self, j):
        self.copy("half", 0, j, self.place.t).start()

    def take_half(self, j):
        other = self.place.t_flip(2)
        self.copy("half", 0, j, other).wait_recv()
        self.copy(0, 1, j, other).start()
        self.copy(1, 2, j, other).start()
        self.copy("core", 4, j, other).start()

    def take_row(self, j):
        other = self.place.t_flip(2)
        self.copy(0, 1, j, other, False).wait_recv()
        self.copy(1, 3, j, other, False).start()
        self.copy("core", 5, j, other, False).start()

    def take_line(self, j):
        other = self.place.t_flip(2)
        for lane, near_row in ((2, True), (3, False)):
            self.copy(1, lane, j, other, near_row, False).wait_recv()
            self.copy("core", lane + 4, j, other, near_row, False).start()

    def settle(self, j):
        cross = self.place.t_flip(3)
        for lane, near_row, near_line in self.core_lanes():
            self.copy("core", lane, j, cross, near_row, near_line).wait_recv()

    def core_lanes(self):
        return ((4, True, True), (5, False, True), (6, True, False), (7, False, False))

    def finish(self, count):
        for i in range(3):
            self.own(i).wait_send()

        def one(j, carry):
            other = self.place.t_flip(2)
            self.copy("half", 0, j, self.place.t).wait_send()
            self.copy(0, 1, j, other).wait_send()
            self.copy(1, 2, j, other).wait_send()
            self.copy(1, 3, j, other, False).wait_send()
            for lane, near_row, near_line in self.core_lanes():
                self.copy("core", lane, j, other, near_row, near_line).wait_send()
            return carry

        lax.fori_loop(0, count, one, 0)


def row_counts(lookup_rows, device, owns, slab_rows, tokens):
    by_table = ((0, (0,)), (1, (1, 3)), (2, (2, 4)), (3, (5,)), (4, (6,)))
    if all(own % 16 == 0 for own in owns):
        pieces = []
        for k, which in by_table:
            at = lax.broadcasted_iota(jnp.int32, (owns[k], tokens), 0) + device * owns[k]
            piece = sum(jnp.where(at == lookup_rows[w], 1.0, 0.0) for w in which)
            pieces.append(piece.astype(BF16))
        spare = slab_rows - sum(owns)
        if spare:
            pieces.append(jnp.zeros((spare, tokens), BF16))
        return jnp.concatenate(pieces, axis=0)
    at = lax.broadcasted_iota(jnp.int32, (slab_rows, tokens), 0)
    total = jnp.zeros((slab_rows, tokens), F32)
    first = 0
    for k, which in by_table:
        for w in which:
            local = lookup_rows[w] - device * owns[k]
            inside = (local >= 0) & (local < owns[k])
            total = total + jnp.where(at == jnp.where(inside, local + first, -1), 1.0, 0.0)
        first += owns[k]
    return total.astype(BF16)


def lookup_rows_of(boxes, segments, offsets, t):
    tokens = segments.shape[1]
    pages = offsets.shape[1]
    seg = segments[pl.ds(t, 1), :]
    label = lax.broadcasted_iota(jnp.int32, (pages, tokens), 0)
    place_in = lax.broadcasted_iota(jnp.int32, (pages, tokens), 1).astype(F32)
    member = label == seg
    starts = jnp.min(jnp.where(member, place_in, float(tokens)), axis=1, keepdims=True)
    shift_row = offsets[pl.ds(t, 1), :].astype(F32)
    eye = lax.broadcasted_iota(jnp.int32, (pages, pages), 0) == lax.broadcasted_iota(
        jnp.int32, (pages, pages), 1
    )
    shift = jnp.sum(jnp.where(eye, shift_row, 0.0), axis=1, keepdims=True)
    moved = jnp.sum(jnp.where(member, place_in - starts + shift, 0.0), axis=0, keepdims=True)
    positions = moved.astype(jnp.int32)
    x0, y0, x1, y1 = (boxes[i : i + 1, :] for i in range(4))
    return (positions, x0, y0, x1, y1, jnp.abs(y1 - y0), jnp.abs(x1 - x0)), seg


def norm_parts(values):
    width = values.shape[1]
    row_mean = jnp.sum(values, axis=1, keepdims=True) * (1.0 / width)
    row_var = jnp.sum(values * values, axis=1, keepdims=True) * (1.0 / width) - row_mean * row_mean
    scaled = lax.rsqrt(row_var + epsilon)
    return (values - row_mean) * scaled, scaled


ROWS = 64


def by_rows(count, step):
    def one(i, carry):
        step(pl.ds(pl.multiple_of(i * ROWS, ROWS), ROWS))
        return carry

    lax.fori_loop(0, count // ROWS, one, 0)


def head_blocks(tokens):
    half, reach = tokens // 2, 128
    return ((0, half, 0, half + reach), (half, half, half - reach, half + reach))


def mask_pages(segments_row, masks):
    tokens = segments_row.shape[1]
    rows = jnp.broadcast_to(segments_row.astype(F32), (8, tokens))
    columns = jnp.transpose(rows)
    for i, (q, nq, k, nk) in enumerate(head_blocks(tokens)):
        same = columns[k : k + nk, 0:1] == rows[0:1, q : q + nq]
        masks[i] = jnp.where(same, 0.0, masked_score).astype(masks.dtype)


def forward_kernel(
    bits,
    owns,
    slab_rows,
    pieces,
    *refs,
):
    slabs, refs = refs[:pieces], refs[pieces:]
    forward_body(bits, owns, slab_rows, slabs, *refs)


def forward_body(
    bits,
    owns,
    slab_rows,
    slabs,
    w_query,
    w_key,
    w_value,
    w_out,
    wide,
    tall,
    vectors,
    word,
    boxes,
    segments,
    offsets,
    cotangent,
    layer_out,
    grad_sum,
    grad_vectors,
    weights_out,
    inputs_low_out,
    centered_in_out,
    scaled_in,
    projected_out,
    mixed_out,
    stats,
    mid_low_out,
    centered_mid_out,
    scaled_mid,
    hidden_out,
    slopes_out,
    inputs_low,
    centered_in,
    projected,
    mixed,
    mid_low,
    centered_mid,
    hidden,
    slopes,
    tables,
    counts,
    weights,
    biases,
    normed,
    total,
    masks,
    send_sems,
    line_sem,
    half_sem,
    row_sem,
    cross_sem,
    core_sem,
    weight_send,
    weight_recv,
    own_send,
    own_recv,
    bias_sems,
    local_sems,
    own_sems,
    ship_sems,
):
    place = Place(bits)
    tokens, width = word.shape
    dps = 2**bits
    t = place.t
    me = place.dp * 4 + t
    local = copies_into(tables.at[me], slabs, own_sems.at[3])
    owned = [
        copies_into(weights.at[i, t], sources, own_sems.at[i])
        for i, sources in enumerate(((w_query, w_key, w_value, w_out), (wide,), (tall,)))
    ]
    for copy in local + owned[0] + owned[1] + owned[2]:
        copy.start()
    shipped = []

    def ship(source, target):
        copy = pltpu.make_async_copy(source, target, ship_sems.at[len(shipped)])
        copy.start()
        shipped.append(copy)

    place.greet()
    links = Links(place, send_sems)
    flow = Weights(place, weights, weight_send, weight_recv, own_send, own_recv)
    chunks = 3 * CHUNKS
    for copy in local:
        copy.wait()
    gather = tables_gather(
        place, links, tables.at[me], tables, (line_sem, half_sem, row_sem, cross_sem, core_sem)
    )
    next(gather)
    bias = vectors.at[pl.ds(8, 8)]
    biases[t] = vectors[8:16]
    links.send("core", bias, biases.at[t], bias_sems.at[0])
    links.send("half", bias, biases.at[t], bias_sems.at[1])
    for i, copies in enumerate(owned):
        for copy in copies:
            copy.wait()
        flow.own(i).start()
    flow.issue(0)
    flow.issue(1)

    lookup, seg = lookup_rows_of(boxes, segments, offsets, t)

    def count_dp(dp, carry):
        for j in range(4):
            counts[dp, j * slab_rows : (j + 1) * slab_rows, :] = row_counts(
                lookup, dp * 4 + j, owns, slab_rows, tokens
            )
        return carry

    lax.fori_loop(0, dps, count_dp, 0)
    mask_pages(seg, masks)
    total[...] = word[...].astype(F32)
    def embed(row_bit):
        def one(i, carry):
            dp = 2 * i + row_bit
            rows = tables[pl.ds(dp * 4, 4)].reshape(4 * slab_rows, width)
            total[...] += inner_rows(counts[dp], rows)
            return carry

        lax.fori_loop(0, dps // 2, one, 0)

    for step in gather:
        if step == "near":
            break
    links.arrived("half", biases.at[place.t_flip(2)], bias_sems.at[1])
    links.send("core", biases.at[place.t_flip(2)], biases.at[place.t_flip(2)], bias_sems.at[2])
    flow.take_half(0)
    flow.issue(2)
    embed(place.bit(0))
    flow.take_half(1)
    flow.issue(3)
    flow.take_row(0)
    for step in gather:
        pass
    flow.take_row(1)
    flow.take_line(0)
    embed(1 - place.bit(0))
    flow.take_half(2)
    flow.issue(4)
    flow.take_line(1)

    def norm_in(rows):
        centered, scaled = norm_parts(total[rows])
        centered_in[rows] = centered.astype(BF16)
        scaled_in[rows] = scaled
        result = centered * vectors[0:1] + vectors[1:2]
        normed[rows] = result
        inputs_low[rows] = result.astype(BF16)

    by_rows(tokens, norm_in)
    ship(inputs_low, inputs_low_out)
    ship(centered_in, centered_in_out)
    flow.take_half(3)
    flow.issue(5)
    flow.take_row(2)
    links.arrived("core", biases.at[place.t_flip(1)], bias_sems.at[0])
    links.arrived("core", biases.at[place.t_flip(3)], bias_sems.at[2])
    flow.own_arrived(0)
    flow.settle(0)
    flow.settle(1)
    fourth = width // 4

    def project(j, carry):
        columns = jnp.transpose(biases[j])
        zeros = jnp.zeros((fourth, 1), F32)
        column = jnp.concatenate(
            [columns[0:fourth, 1:2], zeros, columns[fourth : 2 * fourth, 1:2]], axis=0
        )
        projected[j] = (
            against_rows(weights[0, j, : 3 * fourth, :], inputs_low[...]) + column
        ).astype(BF16)
        return carry

    lax.fori_loop(0, 4, project, 0)
    ship(projected, projected_out)
    flow.take_half(4)
    flow.take_row(3)

    def attend(j, carry):
        for h in range(fourth // HEAD):
            rows = slice(h * HEAD, (h + 1) * HEAD)
            key_rows = slice(fourth + h * HEAD, fourth + (h + 1) * HEAD)
            value_rows = slice(2 * fourth + h * HEAD, 2 * fourth + (h + 1) * HEAD)
            for i, (q, nq, k, nk) in enumerate(head_blocks(tokens)):
                scores = (
                    inner_rows(
                        projected[j, key_rows, k : k + nk], projected[j, rows, q : q + nq]
                    )
                    * HEAD ** (-0.5)
                    + masks[i]
                )
                peak = jnp.max(scores, axis=0, keepdims=True)
                exponent = jnp.exp(scores - peak)
                all_of = jnp.sum(exponent, axis=0, keepdims=True)
                stats[j, h : h + 1, q : q + nq] = peak + jnp.log(all_of)
                share = (exponent * (1.0 / all_of)).astype(BF16)
                mixed[j, rows, q : q + nq] = product(
                    projected[j, value_rows, k : k + nk], share
                ).astype(BF16)
        return carry

    def attend_and_pass(j, carry):
        attend(j, carry)

        @pl.when(j < 1)
        def _():
            flow.take_half(5)

        @pl.when(j < 2)
        def _():
            flow.take_row(j + 4)

        @pl.when(j < 3)
        def _():
            flow.take_line(j + 2)

        return carry

    lax.fori_loop(0, 4, attend_and_pass, 0)
    ship(mixed, mixed_out)
    out_rows = weights[0, :, 3 * fourth :, :].reshape(width, width)
    total[...] = inner_rows(mixed[...].reshape(width, tokens), out_rows)
    flow.take_line(5)

    def norm_mid(rows):
        centered, scaled = norm_parts(total[rows] + vectors[2:3] + normed[rows])
        centered_mid[rows] = centered.astype(BF16)
        scaled_mid[rows] = scaled
        result = centered * vectors[3:4] + vectors[4:5]
        normed[rows] = result
        mid_low[rows] = result.astype(BF16)

    by_rows(tokens, norm_mid)
    ship(mid_low, mid_low_out)
    ship(centered_mid, centered_mid_out)
    total[...] = jnp.zeros_like(total)
    columns = 256

    def feed_copies(j):
        return [
            pltpu.make_async_copy(source.at[j], target.at[j], local_sems.at[1 + i, j])
            for i, (source, target) in enumerate(((hidden, hidden_out), (slopes, slopes_out)))
        ]

    def feed(j):
        def one(n, carry):
            at = pl.ds(pl.multiple_of(n * columns, columns), columns)
            before = product(mid_low[...], weights[1, j, :, at]) + biases[j, 0:1, at]
            share = 0.5 * (1.0 + lax.erf(before * 0.5**0.5))
            hidden[j, :, at] = (before * share).astype(BF16)
            density = jnp.exp(before * before * -0.5) * 0.3989422804014327
            slopes[j, :, at] = (share + before * density).astype(BF16)
            return carry

        lax.fori_loop(0, width // columns, one, 0)
        total[...] += product(hidden[j], weights[2, j])
        for copy in feed_copies(j):
            copy.start()

    flow.own_arrived(1)
    flow.own_arrived(2)

    def feed_near(i, carry):
        feed(t + i * (1 - 2 * place.core))
        return carry

    lax.fori_loop(0, 2, feed_near, 0)
    for j in range(CHUNKS, chunks):
        flow.settle(j)
    out_copy = pltpu.make_async_copy(weights, weights_out, local_sems.at[0, 0])
    out_copy.start()

    def feed_far(i, carry):
        feed(place.t_flip(2) + i * (1 - 2 * place.core))
        return carry

    lax.fori_loop(0, 2, feed_far, 0)
    grad_vectors[...] = jnp.zeros_like(grad_vectors)

    def norm_out(rows):
        centered, scaled = norm_parts(total[rows] + vectors[5:6] + normed[rows])
        layer_out[rows] = centered * vectors[6:7] + vectors[7:8]
        grad = cotangent[rows]
        grad_sum[rows] = norm_back(grad, centered, scaled, vectors[6:7])
        grad_vectors[0:1] += jnp.sum(grad * centered, axis=0, keepdims=True)
        grad_vectors[1:2] += jnp.sum(grad, axis=0, keepdims=True)
        grad_vectors[2:3] += jnp.sum(grad_sum[rows], axis=0, keepdims=True)

    by_rows(tokens, norm_out)
    out_copy.wait()
    for copy in shipped:
        copy.wait()
    for j in range(4):
        for copy in feed_copies(j):
            copy.wait()
    links.finish()
    flow.finish(chunks)


def norm_back(grad_out, centered, scaled, norm_gain):
    width = grad_out.shape[1]
    grad_centered = grad_out * norm_gain
    first_mean = jnp.sum(grad_centered, axis=1, keepdims=True) * (1.0 / width)
    second_mean = jnp.sum(grad_centered * centered, axis=1, keepdims=True) * (1.0 / width)
    return scaled * (grad_centered - first_mean - centered * second_mean)


def copies_into(target, sources, sems):
    first, copies = 0, []
    for i, source in enumerate(sources):
        rows = source.shape[0]
        copies.append(
            pltpu.make_async_copy(source, target.at[pl.ds(first, rows)], sems.at[i])
        )
        first += rows
    return copies


def forward_all(
    devices, owns, slab_rows, slabs, matrices, vectors, word, boxes, segments, offsets, cotangent
):
    bits = (devices // 4).bit_length() - 1
    dps = 2**bits
    lines = 2 ** (bits - 1)
    tokens, width = word.shape
    anywhere = pl.BlockSpec(memory_space=pl.ANY)
    in_vmem = pl.BlockSpec(memory_space=pltpu.VMEM)
    fourth = width // 4
    shape = jax.ShapeDtypeStruct
    return pl.pallas_call(
        functools.partial(forward_kernel, bits, owns, slab_rows, len(slabs)),
        out_shape=[
            shape((tokens, width), F32),
            shape((tokens, width), F32),
            shape((8, width), F32),
            shape((3, 4, width, width), BF16),
            shape((tokens, width), BF16),
            shape((tokens, width), BF16),
            shape((tokens, 1), F32),
            shape((4, 3 * fourth, tokens), BF16),
            shape((4, fourth, tokens), BF16),
            shape((4, 8, tokens), F32),
            shape((tokens, width), BF16),
            shape((tokens, width), BF16),
            shape((tokens, 1), F32),
            shape((4, tokens, width), BF16),
            shape((4, tokens, width), BF16),
        ],
        in_specs=[anywhere] * (len(slabs) + len(matrices)) + [in_vmem] * 6,
        out_specs=[in_vmem] * 3
        + [anywhere] * 3
        + [in_vmem]
        + [anywhere] * 2
        + [in_vmem]
        + [anywhere] * 2
        + [in_vmem]
        + [anywhere] * 2,
        scratch_shapes=[
            pltpu.VMEM((tokens, width), BF16),
            pltpu.VMEM((tokens, width), BF16),
            pltpu.VMEM((4, 3 * fourth, tokens), BF16),
            pltpu.VMEM((4, fourth, tokens), BF16),
            pltpu.VMEM((tokens, width), BF16),
            pltpu.VMEM((tokens, width), BF16),
            pltpu.VMEM((4, tokens, width), BF16),
            pltpu.VMEM((4, tokens, width), BF16),
            pltpu.VMEM((devices, slab_rows, width), BF16),
            pltpu.VMEM((dps, 4 * slab_rows, tokens), BF16),
            pltpu.VMEM((3, 4, width, width), BF16),
            pltpu.VMEM((4, 8, width), F32),
            pltpu.VMEM((tokens, width), F32),
            pltpu.VMEM((tokens, width), F32),
            pltpu.VMEM((2, tokens // 2 + 128, tokens // 2), F32),
            pltpu.SemaphoreType.DMA((10 * lines + 40 + lines * bits,)),
            pltpu.SemaphoreType.DMA((lines,)),
            pltpu.SemaphoreType.DMA((lines,)),
            pltpu.SemaphoreType.DMA((lines,)),
            pltpu.SemaphoreType.DMA((lines,)),
            pltpu.SemaphoreType.DMA((4 * lines,)),
            pltpu.SemaphoreType.DMA((8, 3 * CHUNKS)),
            pltpu.SemaphoreType.DMA((8, 3 * CHUNKS)),
            pltpu.SemaphoreType.DMA((3,)),
            pltpu.SemaphoreType.DMA((3,)),
            pltpu.SemaphoreType.DMA((3,)),
            pltpu.SemaphoreType.DMA((3, 4)),
            pltpu.SemaphoreType.DMA((4, max(4, len(slabs)))),
            pltpu.SemaphoreType.DMA((6,)),
        ],
        name="forward_all",
        compiler_params=pltpu.CompilerParams(
            collective_id=0, has_side_effects=True, vmem_limit_bytes=60 * 2**20
        ),
    )(*slabs, *matrices, vectors, word, boxes, segments, offsets, cotangent)


def ladder(rows, bits):
    left = [rows]
    for b in range(bits):
        halves = left[-1] % 32 == 0 and b < bits - 1
        left.append(left[-1] // 2 if halves else left[-1])
    return left


SLOTS = 3
DEPTH = 3
PARTS = 3


class Sums:
    def __init__(self, place, outgoing, own, from_core, from_half, from_dp, total, sems, credit):
        self.place = place
        self.outgoing = outgoing
        self.own = own
        self.from_core = from_core
        self.from_half = from_half
        self.from_dp = from_dp
        self.total = total
        self.send_sems, self.recv_sems = sems
        self.credit = credit
        self.rows = own.shape[2]
        self.left = ladder(self.rows, place.bits)
        self.back = [b for b in range(place.bits) if self.left[b + 1] < self.left[b]]
        self.taken = 0
        self.issued = 0
        self.ticks = 0

    def copy(self, way, lane, j, src, dst):
        return pltpu.make_async_remote_copy(
            src_ref=src,
            dst_ref=dst,
            send_sem=self.send_sems.at[lane, j],
            recv_sem=self.recv_sems.at[lane, j],
            device_id=self.place.partner(way),
            device_id_type=MESH,
        )

    def start_of(self, level):
        start = 0
        for b in range(level):
            if self.left[b + 1] < self.left[b]:
                start = start + self.place.bit(b) * self.left[b + 1]
        return start

    def span(self, b, near):
        start, rows = self.start_of(b), self.left[b + 1]
        if rows < self.left[b]:
            bit = self.place.bit(b)
            start = start + (bit if near else 1 - bit) * rows
        return pl.ds(pl.multiple_of(start, 16), rows) if b or rows < self.left[0] else pl.ds(0, rows)

    def landing(self, b, j):
        first = sum(self.left[1 : b + 1])
        return self.from_dp.at[j, pl.ds(first, self.left[b + 1])]

    def core(self, j):
        slot = j % SLOTS
        return self.copy("core", 0, j, self.outgoing.at[slot], self.from_core.at[slot])

    def half(self, j):
        return self.copy("half", 1, j, self.own.at[j, 1], self.from_half.at[j])

    def dp(self, b, j):
        return self.copy(
            b, 2 + b, j, self.own.at[j, 0, self.span(b, False)], self.landing(b, j)
        )

    def gather(self, b, j, near=True):
        block = self.total.at[j, self.span(b, near)]
        return self.copy(b, 2 + self.place.bits + b, j, block, block)

    def launch(self, j):
        if j >= SLOTS:
            pl.semaphore_wait(self.credit, 1)
        self.core(j).start()

    def take_core(self, j, count):
        slot = j % SLOTS
        self.core(j).wait_recv()
        for which in (1, 0):
            self.own[j, which] = added(self.own[j, which], self.from_core[slot, which])
        if j + SLOTS < count:
            pl.semaphore_signal(
                self.credit, inc=1, device_id=self.place.partner("core"), device_id_type=MESH
            )
        self.taken = j + 1
        self.pump()

    def pump(self):
        while self.issued < min(self.taken, self.ticks + DEPTH):
            self.half(self.issued).start()
            self.issued += 1

    def tick(self, count):
        k = self.ticks
        self.ticks += 1
        for s in range(self.stages()):
            if 0 <= k - s < count:
                self.stage(s, k - s)

    def take_half(self, j):
        self.half(j).wait_recv()
        self.pump()
        span = self.span(0, False)
        self.own[j, 0, span] = added(self.own[j, 0, span], self.from_half[j, span])
        self.dp(0, j).start()
        if self.left[1] < self.left[0]:
            span = self.span(0, True)
            self.own[j, 0, span] = added(self.own[j, 0, span], self.from_half[j, span])

    def take_dp(self, b, j):
        self.dp(b, j).wait_recv()
        span, first = self.span(b, True), sum(self.left[1 : b + 1])
        arrived = self.from_dp[j, pl.ds(first, self.left[b + 1])]
        if b == self.place.bits - 1:
            self.total[j, span] = added(self.own[j, 0, span], arrived)
            if self.back:
                self.gather(self.back[-1], j).start()
            return
        if self.left[b + 1] == self.left[b]:
            self.dp(b, j).wait_send()
        self.own[j, 0, span] = added(self.own[j, 0, span], arrived)
        self.dp(b + 1, j).start()

    def take_back(self, i, j):
        order = self.back[::-1]
        self.gather(order[i], j, False).wait_recv()
        if i + 1 < len(order):
            self.gather(order[i + 1], j).start()

    def stages(self):
        return 1 + self.place.bits + len(self.back)

    def stage(self, s, j):
        if s == 0:
            self.take_half(j)
        elif s <= self.place.bits:
            self.take_dp(s - 1, j)
        else:
            self.take_back(s - 1 - self.place.bits, j)

    def finish(self, count):
        for j in range(max(0, count - SLOTS), count):
            self.core(j).wait_send()

        def one(j, carry):
            self.half(j).wait_send()
            for b in range(self.place.bits):
                if self.left[b + 1] < self.left[b] or b == self.place.bits - 1:
                    self.dp(b, j).wait_send()
            for b in self.back:
                self.gather(b, j).wait_send()
            return carry

        lax.fori_loop(0, count, one, 0)


def table_reduce(place, links, slab_at, columns, order, landing, sems):
    bits = place.bits
    flags = [1 << (bits if way == "half" else way) for way in order]

    def slab(mask):
        half = 1 - place.half if mask >> bits else place.half
        return slab_at(place.dp_flip(mask % (1 << bits)), half).at[:, columns]

    def first(mask):
        for i, flag in enumerate(flags):
            if mask & flag:
                return i
        return len(flags)

    every = sorted(range(2 ** (bits + 1)), key=lambda m: (first(m), m))
    slots = {}
    for i in range(len(flags)):
        for mask in every:
            if first(mask) > i:
                slots[i, mask] = len(slots)

    def send(i, mask):
        slot = slots[i, mask ^ flags[i]]
        links.send(order[i], slab(mask), landing.at[slot], sems.at[slot])

    for mask in sorted(
        (m for m in every if first(m) == 0), key=lambda m: (first(m ^ flags[0]), m)
    ):
        send(0, mask)
    yield
    for i in range(len(flags)):
        for mask in every:
            if first(mask) > i:
                slot = slots[i, mask]
                links.arrived(order[i], landing.at[slot], sems.at[slot])
                target = slab(mask)
                target[...] = added(target[...], landing[slot])
                if first(mask) == i + 1 < len(flags):
                    send(i + 1, mask)
                yield


def vector_reduce(place, links, vectors, landing, sems):
    for i, way in enumerate(["core", "half"] + list(range(place.bits))):
        links.send(way, vectors.at[i], landing.at[i], sems.at[i])
        yield
        links.arrived(way, landing.at[i], sems.at[i])
        vectors[i + 1] = vectors[i] + landing[i]


def backward_kernel(
    bits,
    owns,
    slab_rows,
    weights_in,
    vectors,
    boxes,
    segments,
    offsets,
    grad_sum,
    ffn_vectors,
    inputs_low_in,
    centered_in_in,
    scaled_in,
    projected_in,
    mixed_in,
    stats,
    mid_low_in,
    centered_mid_in,
    scaled_mid,
    hidden_in,
    slopes_in,
    grad_word,
    weight_sums,
    table_sum,
    vector_sum,
    held,
    inputs_low,
    centered_in,
    projected,
    mixed,
    mid_low,
    centered_mid,
    hidden,
    slopes,
    outgoing,
    own,
    from_core,
    from_half,
    from_dp,
    landing,
    words,
    lookups,
    vector_terms,
    vector_land,
    total,
    low,
    masks,
    grad_heads,
    grad_projected,
    counts,
    send_sems,
    sum_send,
    sum_recv,
    landing_sems,
    vector_sems,
    word_sems,
    local_sems,
    later_sems,
    credit,
):
    place = Place(bits)
    tokens, width = grad_sum.shape
    dps = 2**bits
    t, core = place.t, place.core
    fourth = width // 4
    part = width // PARTS
    quarter_rows = width
    loads = {}
    for i, (matrix, slot) in enumerate(((2, 0), (1, 1), (0, 0))):
        loads[matrix] = [
            pltpu.make_async_copy(
                weights_in.at[matrix, q],
                held.at[pl.ds((slot * 4 + q) * quarter_rows, quarter_rows)],
                local_sems.at[matrix, q],
            )
            for q in range(4)
        ]
    early = [
        pltpu.make_async_copy(hidden_in, hidden, local_sems.at[3, 0]),
        pltpu.make_async_copy(slopes_in, slopes, local_sems.at[3, 1]),
    ]
    later = [
        pltpu.make_async_copy(source, target, later_sems.at[i])
        for i, (source, target) in enumerate(
            (
                (mid_low_in, mid_low),
                (centered_mid_in, centered_mid),
                (projected_in, projected),
                (mixed_in, mixed),
                (inputs_low_in, inputs_low),
                (centered_in_in, centered_in),
            )
        )
    ]
    for copy in loads[2] + early + loads[1] + later:
        copy.start()
    place.greet()
    links = Links(place, send_sems)
    sums = Sums(
        place, outgoing, own, from_core, from_half, from_dp, weight_sums, (sum_send, sum_recv), credit
    )
    chunks = 3 * PARTS

    def quarter(parity, other):
        q = t + other * (2 - 4 * place.half)
        return q + 1 - 2 * core if parity else q

    def held_rows(slot, q, first=0, rows=width):
        start = (slot * 4 + q) * quarter_rows + first
        return held[pl.ds(pl.multiple_of(start, 16), rows)]

    lookup, seg = lookup_rows_of(boxes, segments, offsets, t)
    mask_pages(seg, masks)
    lookups[0] = jnp.concatenate(list(lookup) + [lookup[0]], axis=0)
    links.send("core", lookups.at[0], lookups.at[1], word_sems.at[0])

    def start_rows(rows):
        low[rows] = grad_sum[rows].astype(BF16)

    by_rows(tokens, start_rows)
    vector_terms[0] = jnp.zeros_like(vector_terms[0])
    vector_terms[0, 4:6] = ffn_vectors[0:2]
    vector_terms[0, 7:8] = ffn_vectors[2:3]
    for copy in loads[2] + early:
        copy.wait()

    def chunk(j, term):
        slot = j % SLOTS
        if j >= SLOTS:
            sums.core(j - SLOTS).wait_send()

        def out(i, carry):
            outgoing[slot, i] = term(quarter(1, i)).astype(BF16)
            return carry

        def keep(i, carry):
            own[j, i] = term(quarter(0, i)).astype(BF16)
            return carry

        lax.fori_loop(0, 2, out, 0)
        sums.launch(j)
        lax.fori_loop(0, 2, keep, 0)

    def down_term(part_at, q):
        at = pl.ds(part_at * part, part)
        back = against_rows(low[...], held_rows(0, q, part_at * part, part))
        before = (back * slopes[q, :, at].astype(F32)).astype(BF16)
        slopes[q, :, at] = before
        vector_terms[0, pl.ds(8 + q, 1), at] = jnp.sum(
            before.astype(F32), axis=0, keepdims=True
        )
        return inner_rows(hidden[q, :, at], low[...])

    for p in range(PARTS):
        chunk(p, functools.partial(down_term, p))
        if p:
            sums.take_core(p - 1, chunks)
    for copy in loads[0]:
        copy.start()
    sums.take_core(PARTS - 1, chunks)
    for copy in loads[1] + later:
        copy.wait()
    for p in range(PARTS):
        columns = slice(p * part, (p + 1) * part)
        chunk(PARTS + p, lambda q: inner_rows(mid_low[:, columns], slopes[q]))
        if p:
            sums.take_core(PARTS + p - 1, chunks)
        if p == PARTS - 1:
            sums.tick(chunks)
    total[...] = grad_sum[...]

    def mid_term(q, carry):
        total[...] += against_rows(slopes[q], held_rows(1, q))
        return carry

    lax.fori_loop(0, 4, mid_term, 0)
    sums.take_core(2 * PARTS - 1, chunks)

    def mid_back(rows):
        centered = centered_mid[rows].astype(F32)
        grad = total[rows]
        result = norm_back(grad, centered, scaled_mid[rows], vectors[3:4])
        vector_terms[0, 2:3] += jnp.sum(grad * centered, axis=0, keepdims=True)
        vector_terms[0, 3:4] += jnp.sum(grad, axis=0, keepdims=True)
        vector_terms[0, 6:7] += jnp.sum(result, axis=0, keepdims=True)
        total[rows] = result
        low[rows] = result.astype(BF16)

    by_rows(tokens, mid_back)
    for copy in loads[0]:
        copy.wait()

    def out_back(q, carry):
        grad_heads[q] = against_rows(held_rows(0, q, 3 * fourth, fourth), low[...]).astype(BF16)
        return carry

    lax.fori_loop(0, 4, out_back, 0)
    sums.tick(chunks)
    scale = HEAD ** (-0.5)

    def attend_back(j, carry):
        for h in range(fourth // HEAD):
            rows = slice(h * HEAD, (h + 1) * HEAD)
            key_rows = slice(fourth + h * HEAD, fourth + (h + 1) * HEAD)
            value_rows = slice(2 * fourth + h * HEAD, 2 * fourth + (h + 1) * HEAD)
            grads = []
            for i, (q, nq, k, nk) in enumerate(head_blocks(tokens)):
                queries = projected[j, rows, q : q + nq]
                keys = projected[j, key_rows, k : k + nk]
                values = projected[j, value_rows, k : k + nk]
                grad = grad_heads[j, rows, q : q + nq]
                scores = inner_rows(keys, queries) * scale + masks[i].astype(F32)
                share = jnp.exp(scores - stats[j, h : h + 1, q : q + nq])
                back = inner_rows(values, grad)
                inner = jnp.sum(share * back, axis=0, keepdims=True)
                grad_scores = (share * (back - inner)).astype(BF16)
                grad_projected[j, rows, q : q + nq] = (product(keys, grad_scores) * scale).astype(BF16)
                grads.append(
                    (
                        against_rows(queries, grad_scores) * scale,
                        against_rows(grad, share.astype(BF16)),
                    )
                )
            reach = 128
            for target, (first, second) in zip((key_rows, value_rows), zip(*grads)):
                edge = tokens // 2 - reach
                joined = jnp.concatenate(
                    [
                        first[:, :edge],
                        first[:, edge:] + second[:, : 2 * reach],
                        second[:, 2 * reach :],
                    ],
                    axis=1,
                )
                grad_projected[j, target, :] = joined.astype(BF16)
        ones = jnp.ones((8, tokens), BF16)
        vector_terms[0, pl.ds(12 + j, 1), 0 : 3 * fourth] = against_rows(ones, grad_projected[j])[0:1]
        return carry

    for j in (0, 2):
        lax.fori_loop(j, j + 2, attend_back, 0)
        sums.tick(chunks)

    def square_term(p, q):
        if p < PARTS - 1:
            return product(grad_projected[q, p * part : (p + 1) * part, :], inputs_low[...])
        return jnp.concatenate(
            [
                product(grad_projected[q, p * part :, :], inputs_low[...]),
                product(mixed[q], low[...]),
            ],
            axis=0,
        )

    for p in range(PARTS):
        chunk(2 * PARTS + p, functools.partial(square_term, p))

    def in_term(q, carry):
        total[...] += inner_rows(grad_projected[q], held_rows(0, q, 0, 3 * fourth))
        return carry

    lax.fori_loop(0, 4, in_term, 0)
    for p in range(PARTS):
        sums.take_core(2 * PARTS + p, chunks)

    def in_back(rows):
        centered = centered_in[rows].astype(F32)
        grad = total[rows]
        result = norm_back(grad, centered, scaled_in[rows], vectors[0:1])
        vector_terms[0, 0:1] += jnp.sum(grad * centered, axis=0, keepdims=True)
        vector_terms[0, 1:2] += jnp.sum(grad, axis=0, keepdims=True)
        total[rows] = result
        low[rows] = result.astype(BF16)

    by_rows(tokens, in_back)
    word_copy = pltpu.make_async_copy(total, grad_word, local_sems.at[3, 2])
    word_copy.start()
    links.send("core", low, words, word_sems.at[1])
    links.arrived("core", lookups.at[1], word_sems.at[0])
    sums.tick(chunks)
    links.arrived("core", words, word_sems.at[1])

    def slab_at(dp, half):
        start = (dp * 2 + half) * slab_rows
        return held.at[pl.ds(pl.multiple_of(start, 16), slab_rows)]

    def table_term(row_bit):
        def one(n, carry):
            dp = 2 * n + row_bit
            for i in range(2):
                rows = tuple(lookups[i, w : w + 1, :] for w in range(7))
                for h in range(2):
                    counts[i, h * slab_rows : (h + 1) * slab_rows, :] = row_counts(
                        rows, dp * 4 + h * 2 + core, owns, slab_rows, tokens
                    )
            start = pl.multiple_of(dp * 2 * slab_rows, 16)
            held[pl.ds(start, 2 * slab_rows)] = (
                product(counts[0], low[...]) + product(counts[1], words[...])
            ).astype(BF16)
            return carry

        lax.fori_loop(0, dps // 2, one, 0)

    split = width // 2
    lines = list(range(1, bits))
    by_row, by_line = (
        table_reduce(
            place, links, slab_at, pl.ds(i * split, split), order, landing.at[i], landing_sems.at[i]
        )
        for i, order in enumerate(([0, "half"] + lines, lines + ["half", 0]))
    )
    table_term(1 - place.bit(0))
    next(by_row)
    table_term(place.bit(0))
    next(by_line)

    def ticks():
        while sums.ticks < chunks + sums.stages() - 1:
            sums.tick(chunks)
            for _ in range(3):
                yield

    interleave(
        ticks(),
        by_row,
        by_line,
        seldom(vector_reduce(place, links, vector_terms, vector_land, vector_sems), 3),
    )
    table_sum[...] = slab_at(place.dp, place.half)[...]
    vector_sum[...] = vector_terms[bits + 2]
    word_copy.wait()
    links.finish()
    sums.finish(chunks)


def backward_all(devices, owns, slab_rows, weights, vectors, boxes, segments, offsets, kept):
    bits = (devices // 4).bit_length() - 1
    dps = 2**bits
    tokens, width = kept[0].shape
    anywhere = pl.BlockSpec(memory_space=pl.ANY)
    in_vmem = pl.BlockSpec(memory_space=pltpu.VMEM)
    fourth, part = width // 4, width // PARTS
    chunks = 3 * PARTS
    landing = sum(ladder(part, bits)[1:])
    held_rows = max(8 * width, 2 * dps * slab_rows)
    shape = jax.ShapeDtypeStruct
    return pl.pallas_call(
        functools.partial(backward_kernel, bits, owns, slab_rows),
        out_shape=[
            shape((tokens, width), F32),
            shape((chunks, part, width), BF16),
            shape((slab_rows, width), BF16),
            shape((16, width), F32),
        ],
        in_specs=[anywhere]
        + [in_vmem] * 6
        + [anywhere] * 2
        + [in_vmem]
        + [anywhere] * 2
        + [in_vmem]
        + [anywhere] * 2
        + [in_vmem]
        + [anywhere] * 2,
        out_specs=[anywhere] + [in_vmem] * 3,
        scratch_shapes=[
            pltpu.VMEM((held_rows, width), BF16),
            pltpu.VMEM((tokens, width), BF16),
            pltpu.VMEM((tokens, width), BF16),
            pltpu.VMEM((4, 3 * fourth, tokens), BF16),
            pltpu.VMEM((4, fourth, tokens), BF16),
            pltpu.VMEM((tokens, width), BF16),
            pltpu.VMEM((tokens, width), BF16),
            pltpu.VMEM((4, tokens, width), BF16),
            pltpu.VMEM((4, tokens, width), BF16),
            pltpu.VMEM((SLOTS, 2, part, width), BF16),
            pltpu.VMEM((chunks, 2, part, width), BF16),
            pltpu.VMEM((SLOTS, 2, part, width), BF16),
            pltpu.VMEM((chunks, part, width), BF16),
            pltpu.VMEM((chunks, landing, width), BF16),
            pltpu.VMEM((2, 2 * dps - 1, slab_rows, width // 2), BF16),
            pltpu.VMEM((tokens, width), BF16),
            pltpu.VMEM((2, 8, tokens), jnp.int32),
            pltpu.VMEM((bits + 3, 16, width), F32),
            pltpu.VMEM((bits + 2, 16, width), F32),
            pltpu.VMEM((tokens, width), F32),
            pltpu.VMEM((tokens, width), BF16),
            pltpu.VMEM((2, tokens // 2 + 128, tokens // 2), BF16),
            pltpu.VMEM((4, fourth, tokens), BF16),
            pltpu.VMEM((4, 3 * fourth, tokens), BF16),
            pltpu.VMEM((2, 2 * slab_rows, tokens), BF16),
            pltpu.SemaphoreType.DMA((6 * dps + 40,)),
            pltpu.SemaphoreType.DMA((2 + 2 * bits, chunks)),
            pltpu.SemaphoreType.DMA((2 + 2 * bits, chunks)),
            pltpu.SemaphoreType.DMA((2, 2 * dps - 1)),
            pltpu.SemaphoreType.DMA((bits + 2,)),
            pltpu.SemaphoreType.DMA((2,)),
            pltpu.SemaphoreType.DMA((4, 4)),
            pltpu.SemaphoreType.DMA((6,)),
            pltpu.SemaphoreType.REGULAR,
        ],
        name="backward_all",
        compiler_params=pltpu.CompilerParams(
            collective_id=1, has_side_effects=True, vmem_limit_bytes=60 * 2**20
        ),
    )(weights, vectors, boxes, segments, offsets, *kept)


def body(
    devices,
    word_vectors,
    position_table,
    horizontal_table,
    vertical_table,
    height_table,
    width_table,
    embed_gain,
    embed_shift,
    w_query,
    b_query,
    w_key,
    w_value,
    b_value,
    w_out,
    b_out,
    attn_gain,
    attn_shift,
    w_in,
    b_in,
    w_down,
    b_down,
    ffn_gain,
    ffn_shift,
    boxes,
    segments,
    offsets,
    cotangent,
):
    own_rows, width = word_vectors.shape
    t = lax.axis_index("tensor")
    owned = (position_table, horizontal_table, vertical_table, height_table, width_table)
    slab_rows = sum(table.shape[0] for table in owned)
    slab_padded = -(-slab_rows // 16) * 16
    slabs = owned
    if slab_padded > slab_rows or any(table.shape[0] % 16 for table in owned):
        slab = jnp.concatenate(owned, axis=0)
        slabs = (jnp.pad(slab, ((0, slab_padded - slab_rows), (0, 0))),)
    fourth = w_query.shape[0]
    bias_rows = jnp.concatenate([b_query, b_value, jnp.zeros((2 * fourth,), F32)])
    vectors = jnp.stack(
        [embed_gain, embed_shift, b_out, attn_gain, attn_shift, b_down, ffn_gain, ffn_shift]
        + [b_in, bias_rows]
        + [jnp.zeros_like(b_in)] * 6
    )
    owns = tuple(table.shape[0] for table in owned)
    layer_out, grad_ffn_sum, ffn_vectors, weights, *kept = forward_all(
        devices,
        owns,
        slab_padded,
        slabs,
        (w_query, w_key, w_value, w_out, w_in, w_down),
        vectors,
        word_vectors,
        boxes,
        segments,
        offsets,
        cotangent,
    )
    grad_word, weight_sums, table_sum, vector_sum = backward_all(
        devices,
        owns,
        slab_padded,
        weights,
        vectors,
        boxes,
        segments,
        offsets,
        (grad_ffn_sum, ffn_vectors, *kept),
    )
    tall_sum, wide_sum, square_sum = weight_sums.astype(F32).reshape(3, width, width)
    table_sum = table_sum.astype(F32)
    first = [0]
    for own in owns:
        first.append(first[-1] + own)
    bias_in = lax.dynamic_slice_in_dim(vector_sum, 8 + t, 1)[0]
    bias_row = lax.dynamic_slice_in_dim(vector_sum, 12 + t, 1)[0]
    bias_query, bias_value = bias_row[:fourth], bias_row[2 * fourth : 3 * fourth]
    return (
        layer_out,
        grad_word,
        *(table_sum[first[k] : first[k + 1]] for k in range(5)),
        vector_sum[0],
        vector_sum[1],
        square_sum[:fourth],
        bias_query,
        square_sum[fourth : 2 * fourth],
        square_sum[2 * fourth : 3 * fourth],
        bias_value,
        square_sum[3 * fourth :],
        vector_sum[6],
        vector_sum[2],
        vector_sum[3],
        wide_sum,
        bias_in,
        tall_sum,
        vector_sum[7],
        vector_sum[4],
        vector_sum[5],
    )


def solution(mesh):
    devices = mesh.shape["dp"] * mesh.shape["tensor"]
    both = P(("dp", "tensor"), None)
    rows = P("tensor", None)
    return jax.shard_map(
        functools.partial(body, devices),
        mesh=mesh,
        in_specs=(
            *(both,) * 6,
            P(),
            P(),
            rows,
            P("tensor"),
            rows,
            rows,
            P("tensor"),
            rows,
            P(),
            P(),
            P(),
            P(None, "tensor"),
            P("tensor"),
            rows,
            P(),
            P(),
            P(),
            P(None, ("dp", "tensor")),
            P("dp", None),
            P("dp", None),
            both,
        ),
        out_specs=(
            *(both,) * 7,
            P(),
            P(),
            rows,
            P("tensor"),
            rows,
            rows,
            P("tensor"),
            rows,
            P(),
            P(),
            P(),
            P(None, "tensor"),
            P("tensor"),
            rows,
            P(),
            P(),
            P(),
        ),
        check_vma=False,
    )
```

```python
import functools

import jax
import jax.numpy as jnp
from jax import lax
from jax.experimental import pallas as pl
from jax.experimental.pallas import tpu as pltpu
from jax.sharding import PartitionSpec as P

HEAD = 64
MESH = pl.DeviceIdType.MESH
BF16 = jnp.bfloat16
F32 = jnp.float32

epsilon = 1e-06
masked_score = -1e30


class Place:
    def __init__(self, bits):
        self.bits = bits
        self.dp = lax.axis_index("dp")
        self.t = lax.axis_index("tensor")
        self.core = self.t % 2
        self.half = self.t // 2

    def bit(self, i):
        return (self.dp // 2**i) % 2

    def dp_flip(self, mask):
        dp = self.dp
        for i in range(self.bits):
            if mask & (1 << i):
                dp = dp + 2**i - 2 * 2**i * self.bit(i)
        return dp

    def t_flip(self, mask):
        t = self.t
        if mask & 1:
            t = t + 1 - 2 * self.core
        if mask & 2:
            t = t + 2 - 4 * self.half
        return t

    def partner(self, way):
        if way == "core":
            return (self.dp, self.t_flip(1))
        if way == "half":
            return (self.dp, self.t_flip(2))
        return (self.dp_flip(1 << way), self.t)

    def greet(self):
        barrier = pltpu.get_barrier_semaphore()
        ways = ["core", "half"] + list(range(self.bits))
        for way in ways:
            pl.semaphore_signal(
                barrier, inc=1, device_id=self.partner(way), device_id_type=MESH
            )
        pl.semaphore_wait(barrier, len(ways))


class Links:
    def __init__(self, place, send_sems):
        self.place = place
        self.send_sems = send_sems
        self.sent = []
        self.count = 0

    def send(self, way, src, dst, recv_sem):
        copy = pltpu.make_async_remote_copy(
            src_ref=src,
            dst_ref=dst,
            send_sem=self.send_sems.at[self.count],
            recv_sem=recv_sem,
            device_id=self.place.partner(way),
            device_id_type=MESH,
        )
        copy.start()
        self.count += 1
        self.sent.append(copy)
        return copy

    def arrived(self, way, dst, recv_sem):
        pltpu.make_async_remote_copy(
            src_ref=dst,
            dst_ref=dst,
            send_sem=recv_sem,
            recv_sem=recv_sem,
            device_id=self.place.partner(way),
            device_id_type=MESH,
        ).wait_recv()

    def finish(self):
        for copy in self.sent:
            copy.wait_send()


def seldom(steps, times):
    for _ in steps:
        for _ in range(times):
            yield


def interleave(*steps):
    live = list(steps)
    while live:
        for step in list(live):
            try:
                next(step)
            except StopIteration:
                live.remove(step)


def tables_gather(place, links, own, full, sems):
    bits = place.bits
    line_masks = [2 * k for k in range(2 ** (bits - 1))]
    line_sem, half_sem, row_sem, cross_sem, core_sem = sems

    def at(dp_mask, t_mask):
        return full.at[place.dp_flip(dp_mask) * 4 + place.t_flip(t_mask)]

    def to_core(slab, key):
        links.send("core", slab, slab, core_sem.at[key])

    def onward(mask, slab_source, below):
        for b in range(below - 1, 0, -1):
            links.send(b, slab_source, at(mask, 0), line_sem.at[(mask | (1 << b)) // 2])
        links.send("half", slab_source, at(mask, 0), half_sem.at[mask // 2])
        links.send(0, slab_source, at(mask, 0), row_sem.at[mask // 2])
        links.send("core", slab_source, at(mask, 0), core_sem.at[mask * 2])

    onward(0, own, bits)
    yield
    order = []
    held = [0]
    for b in range(bits - 1, 0, -1):
        fresh = [m | (1 << b) for m in held]
        for m in fresh:
            order.append((m, b))
        held = held + fresh
    for mask, b in order:
        links.arrived(b, at(mask, 0), line_sem.at[mask // 2])
        onward(mask, at(mask, 0), b)
        yield
    low = place.bit(1)
    for pair in range(len(line_masks) // 2):
        base = 4 * pair
        for mask in (base, base + 2):
            links.arrived("half", at(mask, 2), half_sem.at[mask // 2])
            to_core(at(mask, 2), mask * 2 + 1)
            links.arrived(0, at(mask + 1, 0), row_sem.at[mask // 2])
            to_core(at(mask + 1, 0), (mask + 1) * 2)
        yield
        dp_other = place.dp_flip(base)
        clear = dp_other - 2 * low
        here_clear = clear * 4 + place.t_flip(2)
        links.send(0, full.at[here_clear], full.at[here_clear], cross_sem.at[2 * pair + low])
        row_dp = place.dp_flip(base + 1)
        raised = row_dp + 2 * (1 - low)
        here_raised = raised * 4 + place.t
        links.send(
            "half", full.at[here_raised], full.at[here_raised], cross_sem.at[2 * pair + 1 - low]
        )
        yield
    def core_arrivals(row):
        for mask in line_masks:
            for t_mask in (0, 2):
                links.arrived(
                    "core",
                    at(mask + row, t_mask + 1),
                    core_sem.at[(mask + row) * 2 + t_mask // 2],
                )

    core_arrivals(0)
    yield "near"
    for pair in range(len(line_masks) // 2):
        base = 4 * pair
        dp_cross = place.dp_flip(base + 1)
        clear = (dp_cross - 2 * low) * 4 + place.t_flip(2)
        links.arrived(0, full.at[clear], cross_sem.at[2 * pair + low])
        links.send("core", full.at[clear], full.at[clear], core_sem.at[(base + 2 * low + 1) * 2 + 1])
        raised = (dp_cross + 2 * (1 - low)) * 4 + place.t_flip(2)
        links.arrived("half", full.at[raised], cross_sem.at[2 * pair + 1 - low])
        links.send(
            "core", full.at[raised], full.at[raised], core_sem.at[(base + 2 * (1 - low) + 1) * 2 + 1]
        )
        yield
    core_arrivals(1)
    yield


def added(left, right):
    return (left.astype(F32) + right.astype(F32)).astype(BF16)


def product(left, right):
    return jnp.dot(left, right, preferred_element_type=F32)


def inner_rows(left, right):
    return lax.dot_general(left, right, (((0,), (0,)), ((), ())), preferred_element_type=F32)


def against_rows(left, right):
    return lax.dot_general(left, right, (((1,), (1,)), ((), ())), preferred_element_type=F32)


CHUNKS = 2


def chunk_rows(place, weights, j, near_row, near_line):
    side = weights.shape[2] // 4
    rows = side // CHUNKS
    row = place.bit(0) if near_row else 1 - place.bit(0)
    line = place.bit(1) if near_line else 1 - place.bit(1)
    start = (2 * row + line) * side + (j % CHUNKS) * rows
    return j // CHUNKS, pl.ds(pl.multiple_of(start, rows), rows)


class Weights:
    def __init__(self, place, weights, send_sems, recv_sems, own_send, own_recv):
        self.place = place
        self.weights = weights
        self.send_sems = send_sems
        self.recv_sems = recv_sems
        self.own_send = own_send
        self.own_recv = own_recv

    def copy(self, way, lane, j, t, near_row=True, near_line=True):
        matrix, rows = chunk_rows(self.place, self.weights, j, near_row, near_line)
        block = self.weights.at[matrix, t, rows]
        return pltpu.make_async_remote_copy(
            src_ref=block,
            dst_ref=block,
            send_sem=self.send_sems.at[lane, j],
            recv_sem=self.recv_sems.at[lane, j],
            device_id=self.place.partner(way),
            device_id_type=MESH,
        )

    def own(self, i):
        block = self.weights.at[i, self.place.t]
        return pltpu.make_async_remote_copy(
            src_ref=block,
            dst_ref=block,
            send_sem=self.own_send.at[i],
            recv_sem=self.own_recv.at[i],
            device_id=self.place.partner("core"),
            device_id_type=MESH,
        )

    def own_arrived(self, i):
        block = self.weights.at[i, self.place.t_flip(1)]
        pltpu.make_async_remote_copy(
            src_ref=block,
            dst_ref=block,
            send_sem=self.own_send.at[i],
            recv_sem=self.own_recv.at[i],
            device_id=self.place.partner("core"),
            device_id_type=MESH,
        ).wait_recv()

    def issue(self, j):
        self.copy("half", 0, j, self.place.t).start()

    def take_half(self, j):
        other = self.place.t_flip(2)
        self.copy("half", 0, j, other).wait_recv()
        self.copy(0, 1, j, other).start()
        self.copy(1, 2, j, other).start()
        self.copy("core", 4, j, other).start()

    def take_row(self, j):
        other = self.place.t_flip(2)
        self.copy(0, 1, j, other, False).wait_recv()
        self.copy(1, 3, j, other, False).start()
        self.copy("core", 5, j, other, False).start()

    def take_line(self, j):
        other = self.place.t_flip(2)
        for lane, near_row in ((2, True), (3, False)):
            self.copy(1, lane, j, other, near_row, False).wait_recv()
            self.copy("core", lane + 4, j, other, near_row, False).start()

    def settle(self, j):
        cross = self.place.t_flip(3)
        for lane, near_row, near_line in self.core_lanes():
            self.copy("core", lane, j, cross, near_row, near_line).wait_recv()

    def core_lanes(self):
        return ((4, True, True), (5, False, True), (6, True, False), (7, False, False))

    def finish(self, count):
        for i in range(3):
            self.own(i).wait_send()

        def one(j, carry):
            other = self.place.t_flip(2)
            self.copy("half", 0, j, self.place.t).wait_send()
            self.copy(0, 1, j, other).wait_send()
            self.copy(1, 2, j, other).wait_send()
            self.copy(1, 3, j, other, False).wait_send()
            for lane, near_row, near_line in self.core_lanes():
                self.copy("core", lane, j, other, near_row, near_line).wait_send()
            return carry

        lax.fori_loop(0, count, one, 0)


def row_counts(lookup_rows, device, owns, slab_rows, tokens):
    by_table = ((0, (0,)), (1, (1, 3)), (2, (2, 4)), (3, (5,)), (4, (6,)))
    if all(own % 16 == 0 for own in owns):
        pieces = []
        for k, which in by_table:
            at = lax.broadcasted_iota(jnp.int32, (owns[k], tokens), 0) + device * owns[k]
            piece = sum(jnp.where(at == lookup_rows[w], 1.0, 0.0) for w in which)
            pieces.append(piece.astype(BF16))
        spare = slab_rows - sum(owns)
        if spare:
            pieces.append(jnp.zeros((spare, tokens), BF16))
        return jnp.concatenate(pieces, axis=0)
    at = lax.broadcasted_iota(jnp.int32, (slab_rows, tokens), 0)
    total = jnp.zeros((slab_rows, tokens), F32)
    first = 0
    for k, which in by_table:
        for w in which:
            local = lookup_rows[w] - device * owns[k]
            inside = (local >= 0) & (local < owns[k])
            total = total + jnp.where(at == jnp.where(inside, local + first, -1), 1.0, 0.0)
        first += owns[k]
    return total.astype(BF16)


def lookup_rows_of(boxes, segments, offsets, t):
    tokens = segments.shape[1]
    pages = offsets.shape[1]
    seg = segments[pl.ds(t, 1), :]
    label = lax.broadcasted_iota(jnp.int32, (pages, tokens), 0)
    place_in = lax.broadcasted_iota(jnp.int32, (pages, tokens), 1).astype(F32)
    member = label == seg
    starts = jnp.min(jnp.where(member, place_in, float(tokens)), axis=1, keepdims=True)
    shift_row = offsets[pl.ds(t, 1), :].astype(F32)
    eye = lax.broadcasted_iota(jnp.int32, (pages, pages), 0) == lax.broadcasted_iota(
        jnp.int32, (pages, pages), 1
    )
    shift = jnp.sum(jnp.where(eye, shift_row, 0.0), axis=1, keepdims=True)
    moved = jnp.sum(jnp.where(member, place_in - starts + shift, 0.0), axis=0, keepdims=True)
    positions = moved.astype(jnp.int32)
    x0, y0, x1, y1 = (boxes[i : i + 1, :] for i in range(4))
    return (positions, x0, y0, x1, y1, jnp.abs(y1 - y0), jnp.abs(x1 - x0)), seg


def norm_parts(values):
    width = values.shape[1]
    row_mean = jnp.sum(values, axis=1, keepdims=True) * (1.0 / width)
    row_var = jnp.sum(values * values, axis=1, keepdims=True) * (1.0 / width) - row_mean * row_mean
    scaled = lax.rsqrt(row_var + epsilon)
    return (values - row_mean) * scaled, scaled


ROWS = 64


def by_rows(count, step):
    def one(i, carry):
        step(pl.ds(pl.multiple_of(i * ROWS, ROWS), ROWS))
        return carry

    lax.fori_loop(0, count // ROWS, one, 0)


def head_blocks(tokens):
    half, reach = tokens // 2, 128
    return ((0, half, 0, half + reach), (half, half, half - reach, half + reach))


def mask_pages(segments_row, masks):
    tokens = segments_row.shape[1]
    rows = jnp.broadcast_to(segments_row.astype(F32), (8, tokens))
    columns = jnp.transpose(rows)
    for i, (q, nq, k, nk) in enumerate(head_blocks(tokens)):
        same = columns[k : k + nk, 0:1] == rows[0:1, q : q + nq]
        masks[i] = jnp.where(same, 0.0, masked_score).astype(masks.dtype)


def forward_kernel(
    bits,
    owns,
    slab_rows,
    pieces,
    *refs,
):
    slabs, refs = refs[:pieces], refs[pieces:]
    forward_body(bits, owns, slab_rows, slabs, *refs)


def forward_body(
    bits,
    owns,
    slab_rows,
    slabs,
    w_query,
    w_key,
    w_value,
    w_out,
    wide,
    tall,
    vectors,
    word,
    boxes,
    segments,
    offsets,
    cotangent,
    layer_out,
    grad_sum,
    grad_vectors,
    weights_out,
    inputs_low_out,
    centered_in_out,
    scaled_in,
    projected_out,
    mixed_out,
    stats,
    mid_low_out,
    centered_mid_out,
    scaled_mid,
    hidden_out,
    slopes_out,
    inputs_low,
    centered_in,
    projected,
    mixed,
    mid_low,
    centered_mid,
    hidden,
    slopes,
    tables,
    counts,
    weights,
    biases,
    normed,
    total,
    masks,
    send_sems,
    line_sem,
    half_sem,
    row_sem,
    cross_sem,
    core_sem,
    weight_send,
    weight_recv,
    own_send,
    own_recv,
    bias_sems,
    local_sems,
    own_sems,
    ship_sems,
):
    place = Place(bits)
    tokens, width = word.shape
    dps = 2**bits
    t = place.t
    me = place.dp * 4 + t
    local = copies_into(tables.at[me], slabs, own_sems.at[3])
    owned = [
        copies_into(weights.at[i, t], sources, own_sems.at[i])
        for i, sources in enumerate(((w_query, w_key, w_value, w_out), (wide,), (tall,)))
    ]
    for copy in local + owned[0] + owned[1] + owned[2]:
        copy.start()
    shipped = []

    def ship(source, target):
        copy = pltpu.make_async_copy(source, target, ship_sems.at[len(shipped)])
        copy.start()
        shipped.append(copy)

    place.greet()
    links = Links(place, send_sems)
    flow = Weights(place, weights, weight_send, weight_recv, own_send, own_recv)
    chunks = 3 * CHUNKS
    for copy in local:
        copy.wait()
    gather = tables_gather(
        place, links, tables.at[me], tables, (line_sem, half_sem, row_sem, cross_sem, core_sem)
    )
    next(gather)
    bias = vectors.at[pl.ds(8, 8)]
    biases[t] = vectors[8:16]
    links.send("core", bias, biases.at[t], bias_sems.at[0])
    links.send("half", bias, biases.at[t], bias_sems.at[1])
    for i, copies in enumerate(owned):
        for copy in copies:
            copy.wait()
        flow.own(i).start()
    flow.issue(0)
    flow.issue(1)

    lookup, seg = lookup_rows_of(boxes, segments, offsets, t)

    def count_dp(dp, carry):
        for j in range(4):
            counts[dp, j * slab_rows : (j + 1) * slab_rows, :] = row_counts(
                lookup, dp * 4 + j, owns, slab_rows, tokens
            )
        return carry

    lax.fori_loop(0, dps, count_dp, 0)
    mask_pages(seg, masks)
    total[...] = word[...].astype(F32)
    def embed(row_bit):
        def one(i, carry):
            dp = 2 * i + row_bit
            rows = tables[pl.ds(dp * 4, 4)].reshape(4 * slab_rows, width)
            total[...] += inner_rows(counts[dp], rows)
            return carry

        lax.fori_loop(0, dps // 2, one, 0)

    for step in gather:
        if step == "near":
            break
    links.arrived("half", biases.at[place.t_flip(2)], bias_sems.at[1])
    links.send("core", biases.at[place.t_flip(2)], biases.at[place.t_flip(2)], bias_sems.at[2])
    flow.take_half(0)
    flow.issue(2)
    embed(place.bit(0))
    flow.take_half(1)
    flow.issue(3)
    flow.take_row(0)
    for step in gather:
        pass
    flow.take_row(1)
    flow.take_line(0)
    embed(1 - place.bit(0))
    flow.take_half(2)
    flow.issue(4)
    flow.take_line(1)

    def norm_in(rows):
        centered, scaled = norm_parts(total[rows])
        centered_in[rows] = centered.astype(BF16)
        scaled_in[rows] = scaled
        result = centered * vectors[0:1] + vectors[1:2]
        normed[rows] = result
        inputs_low[rows] = result.astype(BF16)

    by_rows(tokens, norm_in)
    ship(inputs_low, inputs_low_out)
    ship(centered_in, centered_in_out)
    flow.take_half(3)
    flow.issue(5)
    flow.take_row(2)
    links.arrived("core", biases.at[place.t_flip(1)], bias_sems.at[0])
    links.arrived("core", biases.at[place.t_flip(3)], bias_sems.at[2])
    flow.own_arrived(0)
    flow.settle(0)
    flow.settle(1)
    fourth = width // 4

    def project(j, carry):
        columns = jnp.transpose(biases[j])
        zeros = jnp.zeros((fourth, 1), F32)
        column = jnp.concatenate(
            [columns[0:fourth, 1:2], zeros, columns[fourth : 2 * fourth, 1:2]], axis=0
        )
        projected[j] = (
            against_rows(weights[0, j, : 3 * fourth, :], inputs_low[...]) + column
        ).astype(BF16)
        return carry

    lax.fori_loop(0, 4, project, 0)
    ship(projected, projected_out)
    flow.take_half(4)
    flow.take_row(3)

    def attend(j, carry):
        for h in range(fourth // HEAD):
            rows = slice(h * HEAD, (h + 1) * HEAD)
            key_rows = slice(fourth + h * HEAD, fourth + (h + 1) * HEAD)
            value_rows = slice(2 * fourth + h * HEAD, 2 * fourth + (h + 1) * HEAD)
            for i, (q, nq, k, nk) in enumerate(head_blocks(tokens)):
                scores = (
                    inner_rows(
                        projected[j, key_rows, k : k + nk], projected[j, rows, q : q + nq]
                    )
                    * HEAD ** (-0.5)
                    + masks[i]
                )
                peak = jnp.max(scores, axis=0, keepdims=True)
                exponent = jnp.exp(scores - peak)
                all_of = jnp.sum(exponent, axis=0, keepdims=True)
                stats[j, h : h + 1, q : q + nq] = peak + jnp.log(all_of)
                share = (exponent * (1.0 / all_of)).astype(BF16)
                mixed[j, rows, q : q + nq] = product(
                    projected[j, value_rows, k : k + nk], share
                ).astype(BF16)
        return carry

    def attend_and_pass(j, carry):
        attend(j, carry)

        @pl.when(j < 1)
        def _():
            flow.take_half(5)

        @pl.when(j < 2)
        def _():
            flow.take_row(j + 4)

        @pl.when(j < 3)
        def _():
            flow.take_line(j + 2)

        return carry

    lax.fori_loop(0, 4, attend_and_pass, 0)
    ship(mixed, mixed_out)
    out_rows = weights[0, :, 3 * fourth :, :].reshape(width, width)
    total[...] = inner_rows(mixed[...].reshape(width, tokens), out_rows)
    flow.take_line(5)

    def norm_mid(rows):
        centered, scaled = norm_parts(total[rows] + vectors[2:3] + normed[rows])
        centered_mid[rows] = centered.astype(BF16)
        scaled_mid[rows] = scaled
        result = centered * vectors[3:4] + vectors[4:5]
        normed[rows] = result
        mid_low[rows] = result.astype(BF16)

    by_rows(tokens, norm_mid)
    ship(mid_low, mid_low_out)
    ship(centered_mid, centered_mid_out)
    total[...] = jnp.zeros_like(total)
    columns = 256

    def feed_copies(j):
        return [
            pltpu.make_async_copy(source.at[j], target.at[j], local_sems.at[1 + i, j])
            for i, (source, target) in enumerate(((hidden, hidden_out), (slopes, slopes_out)))
        ]

    def feed(j):
        def one(n, carry):
            at = pl.ds(pl.multiple_of(n * columns, columns), columns)
            before = product(mid_low[...], weights[1, j, :, at]) + biases[j, 0:1, at]
            share = 0.5 * (1.0 + lax.erf(before * 0.5**0.5))
            hidden[j, :, at] = (before * share).astype(BF16)
            density = jnp.exp(before * before * -0.5) * 0.3989422804014327
            slopes[j, :, at] = (share + before * density).astype(BF16)
            return carry

        lax.fori_loop(0, width // columns, one, 0)
        total[...] += product(hidden[j], weights[2, j])
        for copy in feed_copies(j):
            copy.start()

    flow.own_arrived(1)
    flow.own_arrived(2)

    def feed_near(i, carry):
        feed(t + i * (1 - 2 * place.core))
        return carry

    lax.fori_loop(0, 2, feed_near, 0)
    for j in range(CHUNKS, chunks):
        flow.settle(j)
    out_copy = pltpu.make_async_copy(weights, weights_out, local_sems.at[0, 0])
    out_copy.start()

    def feed_far(i, carry):
        feed(place.t_flip(2) + i * (1 - 2 * place.core))
        return carry

    lax.fori_loop(0, 2, feed_far, 0)
    grad_vectors[...] = jnp.zeros_like(grad_vectors)

    def norm_out(rows):
        centered, scaled = norm_parts(total[rows] + vectors[5:6] + normed[rows])
        layer_out[rows] = centered * vectors[6:7] + vectors[7:8]
        grad = cotangent[rows]
        grad_sum[rows] = norm_back(grad, centered, scaled, vectors[6:7])
        grad_vectors[0:1] += jnp.sum(grad * centered, axis=0, keepdims=True)
        grad_vectors[1:2] += jnp.sum(grad, axis=0, keepdims=True)
        grad_vectors[2:3] += jnp.sum(grad_sum[rows], axis=0, keepdims=True)

    by_rows(tokens, norm_out)
    out_copy.wait()
    for copy in shipped:
        copy.wait()
    for j in range(4):
        for copy in feed_copies(j):
            copy.wait()
    links.finish()
    flow.finish(chunks)


def norm_back(grad_out, centered, scaled, norm_gain):
    width = grad_out.shape[1]
    grad_centered = grad_out * norm_gain
    first_mean = jnp.sum(grad_centered, axis=1, keepdims=True) * (1.0 / width)
    second_mean = jnp.sum(grad_centered * centered, axis=1, keepdims=True) * (1.0 / width)
    return scaled * (grad_centered - first_mean - centered * second_mean)


def copies_into(target, sources, sems):
    first, copies = 0, []
    for i, source in enumerate(sources):
        rows = source.shape[0]
        copies.append(
            pltpu.make_async_copy(source, target.at[pl.ds(first, rows)], sems.at[i])
        )
        first += rows
    return copies


def forward_all(
    devices, owns, slab_rows, slabs, matrices, vectors, word, boxes, segments, offsets, cotangent
):
    bits = (devices // 4).bit_length() - 1
    dps = 2**bits
    lines = 2 ** (bits - 1)
    tokens, width = word.shape
    anywhere = pl.BlockSpec(memory_space=pl.ANY)
    in_vmem = pl.BlockSpec(memory_space=pltpu.VMEM)
    fourth = width // 4
    shape = jax.ShapeDtypeStruct
    return pl.pallas_call(
        functools.partial(forward_kernel, bits, owns, slab_rows, len(slabs)),
        out_shape=[
            shape((tokens, width), F32),
            shape((tokens, width), F32),
            shape((8, width), F32),
            shape((3, 4, width, width), BF16),
            shape((tokens, width), BF16),
            shape((tokens, width), BF16),
            shape((tokens, 1), F32),
            shape((4, 3 * fourth, tokens), BF16),
            shape((4, fourth, tokens), BF16),
            shape((4, 8, tokens), F32),
            shape((tokens, width), BF16),
            shape((tokens, width), BF16),
            shape((tokens, 1), F32),
            shape((4, tokens, width), BF16),
            shape((4, tokens, width), BF16),
        ],
        in_specs=[anywhere] * (len(slabs) + len(matrices)) + [in_vmem] * 6,
        out_specs=[in_vmem] * 3
        + [anywhere] * 3
        + [in_vmem]
        + [anywhere] * 2
        + [in_vmem]
        + [anywhere] * 2
        + [in_vmem]
        + [anywhere] * 2,
        scratch_shapes=[
            pltpu.VMEM((tokens, width), BF16),
            pltpu.VMEM((tokens, width), BF16),
            pltpu.VMEM((4, 3 * fourth, tokens), BF16),
            pltpu.VMEM((4, fourth, tokens), BF16),
            pltpu.VMEM((tokens, width), BF16),
            pltpu.VMEM((tokens, width), BF16),
            pltpu.VMEM((4, tokens, width), BF16),
            pltpu.VMEM((4, tokens, width), BF16),
            pltpu.VMEM((devices, slab_rows, width), BF16),
            pltpu.VMEM((dps, 4 * slab_rows, tokens), BF16),
            pltpu.VMEM((3, 4, width, width), BF16),
            pltpu.VMEM((4, 8, width), F32),
            pltpu.VMEM((tokens, width), F32),
            pltpu.VMEM((tokens, width), F32),
            pltpu.VMEM((2, tokens // 2 + 128, tokens // 2), F32),
            pltpu.SemaphoreType.DMA((10 * lines + 40 + lines * bits,)),
            pltpu.SemaphoreType.DMA((lines,)),
            pltpu.SemaphoreType.DMA((lines,)),
            pltpu.SemaphoreType.DMA((lines,)),
            pltpu.SemaphoreType.DMA((lines,)),
            pltpu.SemaphoreType.DMA((4 * lines,)),
            pltpu.SemaphoreType.DMA((8, 3 * CHUNKS)),
            pltpu.SemaphoreType.DMA((8, 3 * CHUNKS)),
            pltpu.SemaphoreType.DMA((3,)),
            pltpu.SemaphoreType.DMA((3,)),
            pltpu.SemaphoreType.DMA((3,)),
            pltpu.SemaphoreType.DMA((3, 4)),
            pltpu.SemaphoreType.DMA((4, max(4, len(slabs)))),
            pltpu.SemaphoreType.DMA((6,)),
        ],
        name="forward_all",
        compiler_params=pltpu.CompilerParams(
            collective_id=0, has_side_effects=True, vmem_limit_bytes=60 * 2**20
        ),
    )(*slabs, *matrices, vectors, word, boxes, segments, offsets, cotangent)


def ladder(rows, bits):
    left = [rows]
    for b in range(bits):
        halves = left[-1] % 32 == 0 and b < bits - 1
        left.append(left[-1] // 2 if halves else left[-1])
    return left


SLOTS = 3
DEPTH = 2
PARTS = 3


class Sums:
    def __init__(self, place, outgoing, own, from_core, from_half, from_dp, total, sems, credit):
        self.place = place
        self.outgoing = outgoing
        self.own = own
        self.from_core = from_core
        self.from_half = from_half
        self.from_dp = from_dp
        self.total = total
        self.send_sems, self.recv_sems = sems
        self.credit = credit
        self.rows = own.shape[2]
        self.left = ladder(self.rows, place.bits)
        self.back = [b for b in range(place.bits) if self.left[b + 1] < self.left[b]]
        self.taken = 0
        self.issued = 0
        self.ticks = 0

    def copy(self, way, lane, j, src, dst):
        return pltpu.make_async_remote_copy(
            src_ref=src,
            dst_ref=dst,
            send_sem=self.send_sems.at[lane, j],
            recv_sem=self.recv_sems.at[lane, j],
            device_id=self.place.partner(way),
            device_id_type=MESH,
        )

    def start_of(self, level):
        start = 0
        for b in range(level):
            if self.left[b + 1] < self.left[b]:
                start = start + self.place.bit(b) * self.left[b + 1]
        return start

    def span(self, b, near):
        start, rows = self.start_of(b), self.left[b + 1]
        if rows < self.left[b]:
            bit = self.place.bit(b)
            start = start + (bit if near else 1 - bit) * rows
        return pl.ds(pl.multiple_of(start, 16), rows) if b or rows < self.left[0] else pl.ds(0, rows)

    def landing(self, b, j):
        first = sum(self.left[1 : b + 1])
        return self.from_dp.at[j, pl.ds(first, self.left[b + 1])]

    def core(self, j):
        slot = j % SLOTS
        return self.copy("core", 0, j, self.outgoing.at[slot], self.from_core.at[slot])

    def half(self, j):
        return self.copy("half", 1, j, self.own.at[j, 1], self.from_half.at[j])

    def dp(self, b, j):
        return self.copy(
            b, 2 + b, j, self.own.at[j, 0, self.span(b, False)], self.landing(b, j)
        )

    def gather(self, b, j, near=True):
        block = self.total.at[j, self.span(b, near)]
        return self.copy(b, 2 + self.place.bits + b, j, block, block)

    def launch(self, j):
        if j >= SLOTS:
            pl.semaphore_wait(self.credit, 1)
        self.core(j).start()

    def take_core(self, j, count):
        slot = j % SLOTS
        self.core(j).wait_recv()
        for which in (1, 0):
            self.own[j, which] = added(self.own[j, which], self.from_core[slot, which])
        if j + SLOTS < count:
            pl.semaphore_signal(
                self.credit, inc=1, device_id=self.place.partner("core"), device_id_type=MESH
            )
        self.taken = j + 1
        self.pump()

    def pump(self):
        while self.issued < min(self.taken, self.ticks + DEPTH):
            self.half(self.issued).start()
            self.issued += 1

    def tick(self, count):
        k = self.ticks
        self.ticks += 1
        for s in range(self.stages()):
            if 0 <= k - s < count:
                self.stage(s, k - s)

    def take_half(self, j):
        self.half(j).wait_recv()
        self.pump()
        span = self.span(0, False)
        self.own[j, 0, span] = added(self.own[j, 0, span], self.from_half[j, span])
        self.dp(0, j).start()
        if self.left[1] < self.left[0]:
            span = self.span(0, True)
            self.own[j, 0, span] = added(self.own[j, 0, span], self.from_half[j, span])

    def take_dp(self, b, j):
        self.dp(b, j).wait_recv()
        span, first = self.span(b, True), sum(self.left[1 : b + 1])
        arrived = self.from_dp[j, pl.ds(first, self.left[b + 1])]
        if b == self.place.bits - 1:
            self.total[j, span] = added(self.own[j, 0, span], arrived)
            if self.back:
                self.gather(self.back[-1], j).start()
            return
        if self.left[b + 1] == self.left[b]:
            self.dp(b, j).wait_send()
        self.own[j, 0, span] = added(self.own[j, 0, span], arrived)
        self.dp(b + 1, j).start()

    def take_back(self, i, j):
        order = self.back[::-1]
        self.gather(order[i], j, False).wait_recv()
        if i + 1 < len(order):
            self.gather(order[i + 1], j).start()

    def stages(self):
        return 1 + self.place.bits + len(self.back)

    def stage(self, s, j):
        if s == 0:
            self.take_half(j)
        elif s <= self.place.bits:
            self.take_dp(s - 1, j)
        else:
            self.take_back(s - 1 - self.place.bits, j)

    def finish(self, count):
        for j in range(max(0, count - SLOTS), count):
            self.core(j).wait_send()

        def one(j, carry):
            self.half(j).wait_send()
            for b in range(self.place.bits):
                if self.left[b + 1] < self.left[b] or b == self.place.bits - 1:
                    self.dp(b, j).wait_send()
            for b in self.back:
                self.gather(b, j).wait_send()
            return carry

        lax.fori_loop(0, count, one, 0)


def table_reduce(place, links, slab_at, columns, order, landing, sems):
    bits = place.bits
    flags = [1 << (bits if way == "half" else way) for way in order]

    def slab(mask):
        half = 1 - place.half if mask >> bits else place.half
        return slab_at(place.dp_flip(mask % (1 << bits)), half).at[:, columns]

    def first(mask):
        for i, flag in enumerate(flags):
            if mask & flag:
                return i
        return len(flags)

    every = sorted(range(2 ** (bits + 1)), key=lambda m: (first(m), m))
    slots = {}
    for i in range(len(flags)):
        for mask in every:
            if first(mask) > i:
                slots[i, mask] = len(slots)

    def send(i, mask):
        slot = slots[i, mask ^ flags[i]]
        links.send(order[i], slab(mask), landing.at[slot], sems.at[slot])

    for mask in sorted(
        (m for m in every if first(m) == 0), key=lambda m: (first(m ^ flags[0]), m)
    ):
        send(0, mask)
    yield
    for i in range(len(flags)):
        for mask in every:
            if first(mask) > i:
                slot = slots[i, mask]
                links.arrived(order[i], landing.at[slot], sems.at[slot])
                target = slab(mask)
                target[...] = added(target[...], landing[slot])
                if first(mask) == i + 1 < len(flags):
                    send(i + 1, mask)
                yield


def vector_reduce(place, links, vectors, landing, sems):
    for i, way in enumerate(["core", "half"] + list(range(place.bits))):
        links.send(way, vectors.at[i], landing.at[i], sems.at[i])
        yield
        links.arrived(way, landing.at[i], sems.at[i])
        vectors[i + 1] = vectors[i] + landing[i]


def backward_kernel(
    bits,
    owns,
    slab_rows,
    weights_in,
    vectors,
    boxes,
    segments,
    offsets,
    grad_sum,
    ffn_vectors,
    inputs_low_in,
    centered_in_in,
    scaled_in,
    projected_in,
    mixed_in,
    stats,
    mid_low_in,
    centered_mid_in,
    scaled_mid,
    hidden_in,
    slopes_in,
    grad_word,
    weight_sums,
    table_sum,
    vector_sum,
    held,
    inputs_low,
    centered_in,
    projected,
    mixed,
    mid_low,
    centered_mid,
    hidden,
    slopes,
    outgoing,
    own,
    from_core,
    from_half,
    from_dp,
    landing,
    words,
    lookups,
    vector_terms,
    vector_land,
    total,
    low,
    masks,
    grad_heads,
    grad_projected,
    counts,
    send_sems,
    sum_send,
    sum_recv,
    landing_sems,
    vector_sems,
    word_sems,
    local_sems,
    later_sems,
    credit,
):
    place = Place(bits)
    tokens, width = grad_sum.shape
    dps = 2**bits
    t, core = place.t, place.core
    fourth = width // 4
    part = width // PARTS
    quarter_rows = width
    loads = {}
    for i, (matrix, slot) in enumerate(((2, 0), (1, 1), (0, 0))):
        loads[matrix] = [
            pltpu.make_async_copy(
                weights_in.at[matrix, q],
                held.at[pl.ds((slot * 4 + q) * quarter_rows, quarter_rows)],
                local_sems.at[matrix, q],
            )
            for q in range(4)
        ]
    early = [
        pltpu.make_async_copy(hidden_in, hidden, local_sems.at[3, 0]),
        pltpu.make_async_copy(slopes_in, slopes, local_sems.at[3, 1]),
    ]
    later = [
        pltpu.make_async_copy(source, target, later_sems.at[i])
        for i, (source, target) in enumerate(
            (
                (mid_low_in, mid_low),
                (centered_mid_in, centered_mid),
                (projected_in, projected),
                (mixed_in, mixed),
                (inputs_low_in, inputs_low),
                (centered_in_in, centered_in),
            )
        )
    ]
    for copy in loads[2] + early + loads[1] + later:
        copy.start()
    place.greet()
    links = Links(place, send_sems)
    sums = Sums(
        place, outgoing, own, from_core, from_half, from_dp, weight_sums, (sum_send, sum_recv), credit
    )
    chunks = 3 * PARTS

    def quarter(parity, other):
        q = t + other * (2 - 4 * place.half)
        return q + 1 - 2 * core if parity else q

    def held_rows(slot, q, first=0, rows=width):
        start = (slot * 4 + q) * quarter_rows + first
        return held[pl.ds(pl.multiple_of(start, 16), rows)]

    lookup, seg = lookup_rows_of(boxes, segments, offsets, t)
    mask_pages(seg, masks)
    lookups[0] = jnp.concatenate(list(lookup) + [lookup[0]], axis=0)
    links.send("core", lookups.at[0], lookups.at[1], word_sems.at[0])

    def start_rows(rows):
        low[rows] = grad_sum[rows].astype(BF16)

    by_rows(tokens, start_rows)
    vector_terms[0] = jnp.zeros_like(vector_terms[0])
    vector_terms[0, 4:6] = ffn_vectors[0:2]
    vector_terms[0, 7:8] = ffn_vectors[2:3]
    for copy in loads[2] + early:
        copy.wait()

    def chunk(j, term):
        slot = j % SLOTS
        if j >= SLOTS:
            sums.core(j - SLOTS).wait_send()

        def out(i, carry):
            outgoing[slot, i] = term(quarter(1, i)).astype(BF16)
            return carry

        def keep(i, carry):
            own[j, i] = term(quarter(0, i)).astype(BF16)
            return carry

        lax.fori_loop(0, 2, out, 0)
        sums.launch(j)
        lax.fori_loop(0, 2, keep, 0)

    def down_term(part_at, q):
        at = pl.ds(part_at * part, part)
        back = against_rows(low[...], held_rows(0, q, part_at * part, part))
        before = (back * slopes[q, :, at].astype(F32)).astype(BF16)
        slopes[q, :, at] = before
        vector_terms[0, pl.ds(8 + q, 1), at] = jnp.sum(
            before.astype(F32), axis=0, keepdims=True
        )
        return inner_rows(hidden[q, :, at], low[...])

    for p in range(PARTS):
        chunk(p, functools.partial(down_term, p))
        if p:
            sums.take_core(p - 1, chunks)
    for copy in loads[0]:
        copy.start()
    sums.take_core(PARTS - 1, chunks)
    for copy in loads[1] + later:
        copy.wait()
    for p in range(PARTS):
        columns = slice(p * part, (p + 1) * part)
        chunk(PARTS + p, lambda q: inner_rows(mid_low[:, columns], slopes[q]))
        if p:
            sums.take_core(PARTS + p - 1, chunks)
        if p == PARTS - 1:
            sums.tick(chunks)
    total[...] = grad_sum[...]

    def mid_term(q, carry):
        total[...] += against_rows(slopes[q], held_rows(1, q))
        return carry

    lax.fori_loop(0, 4, mid_term, 0)
    sums.take_core(2 * PARTS - 1, chunks)

    def mid_back(rows):
        centered = centered_mid[rows].astype(F32)
        grad = total[rows]
        result = norm_back(grad, centered, scaled_mid[rows], vectors[3:4])
        vector_terms[0, 2:3] += jnp.sum(grad * centered, axis=0, keepdims=True)
        vector_terms[0, 3:4] += jnp.sum(grad, axis=0, keepdims=True)
        vector_terms[0, 6:7] += jnp.sum(result, axis=0, keepdims=True)
        total[rows] = result
        low[rows] = result.astype(BF16)

    by_rows(tokens, mid_back)
    for copy in loads[0]:
        copy.wait()

    def out_back(q, carry):
        grad_heads[q] = against_rows(held_rows(0, q, 3 * fourth, fourth), low[...]).astype(BF16)
        return carry

    lax.fori_loop(0, 4, out_back, 0)
    sums.tick(chunks)
    scale = HEAD ** (-0.5)

    def attend_back(j, carry):
        for h in range(fourth // HEAD):
            rows = slice(h * HEAD, (h + 1) * HEAD)
            key_rows = slice(fourth + h * HEAD, fourth + (h + 1) * HEAD)
            value_rows = slice(2 * fourth + h * HEAD, 2 * fourth + (h + 1) * HEAD)
            grads = []
            for i, (q, nq, k, nk) in enumerate(head_blocks(tokens)):
                queries = projected[j, rows, q : q + nq]
                keys = projected[j, key_rows, k : k + nk]
                values = projected[j, value_rows, k : k + nk]
                grad = grad_heads[j, rows, q : q + nq]
                scores = inner_rows(keys, queries) * scale + masks[i].astype(F32)
                share = jnp.exp(scores - stats[j, h : h + 1, q : q + nq])
                back = inner_rows(values, grad)
                inner = jnp.sum(share * back, axis=0, keepdims=True)
                grad_scores = (share * (back - inner)).astype(BF16)
                grad_projected[j, rows, q : q + nq] = (product(keys, grad_scores) * scale).astype(BF16)
                grads.append(
                    (
                        against_rows(queries, grad_scores) * scale,
                        against_rows(grad, share.astype(BF16)),
                    )
                )
            reach = 128
            for target, (first, second) in zip((key_rows, value_rows), zip(*grads)):
                edge = tokens // 2 - reach
                joined = jnp.concatenate(
                    [
                        first[:, :edge],
                        first[:, edge:] + second[:, : 2 * reach],
                        second[:, 2 * reach :],
                    ],
                    axis=1,
                )
                grad_projected[j, target, :] = joined.astype(BF16)
        ones = jnp.ones((8, tokens), BF16)
        vector_terms[0, pl.ds(12 + j, 1), 0 : 3 * fourth] = against_rows(ones, grad_projected[j])[0:1]
        return carry

    for j in (0, 2):
        lax.fori_loop(j, j + 2, attend_back, 0)
        sums.tick(chunks)

    def square_term(p, q):
        if p < PARTS - 1:
            return product(grad_projected[q, p * part : (p + 1) * part, :], inputs_low[...])
        return jnp.concatenate(
            [
                product(grad_projected[q, p * part :, :], inputs_low[...]),
                product(mixed[q], low[...]),
            ],
            axis=0,
        )

    for p in range(PARTS):
        chunk(2 * PARTS + p, functools.partial(square_term, p))

    def in_term(q, carry):
        total[...] += inner_rows(grad_projected[q], held_rows(0, q, 0, 3 * fourth))
        return carry

    lax.fori_loop(0, 4, in_term, 0)
    for p in range(PARTS):
        sums.take_core(2 * PARTS + p, chunks)

    def in_back(rows):
        centered = centered_in[rows].astype(F32)
        grad = total[rows]
        result = norm_back(grad, centered, scaled_in[rows], vectors[0:1])
        vector_terms[0, 0:1] += jnp.sum(grad * centered, axis=0, keepdims=True)
        vector_terms[0, 1:2] += jnp.sum(grad, axis=0, keepdims=True)
        total[rows] = result
        low[rows] = result.astype(BF16)

    by_rows(tokens, in_back)
    word_copy = pltpu.make_async_copy(total, grad_word, local_sems.at[3, 2])
    word_copy.start()
    links.send("core", low, words, word_sems.at[1])
    links.arrived("core", lookups.at[1], word_sems.at[0])
    sums.tick(chunks)
    links.arrived("core", words, word_sems.at[1])

    def slab_at(dp, half):
        start = (dp * 2 + half) * slab_rows
        return held.at[pl.ds(pl.multiple_of(start, 16), slab_rows)]

    def table_term(row_bit):
        def one(n, carry):
            dp = 2 * n + row_bit
            for i in range(2):
                rows = tuple(lookups[i, w : w + 1, :] for w in range(7))
                for h in range(2):
                    counts[i, h * slab_rows : (h + 1) * slab_rows, :] = row_counts(
                        rows, dp * 4 + h * 2 + core, owns, slab_rows, tokens
                    )
            start = pl.multiple_of(dp * 2 * slab_rows, 16)
            held[pl.ds(start, 2 * slab_rows)] = (
                product(counts[0], low[...]) + product(counts[1], words[...])
            ).astype(BF16)
            return carry

        lax.fori_loop(0, dps // 2, one, 0)

    split = width // 3
    lines = list(range(1, bits))
    by_row, by_line, by_half = (
        table_reduce(
            place, links, slab_at, pl.ds(i * split, split), order, landing.at[i], landing_sems.at[i]
        )
        for i, order in enumerate(([0, "half"] + lines, lines + ["half", 0], ["half", 0] + lines))
    )
    table_term(1 - place.bit(0))
    next(by_row)
    table_term(place.bit(0))
    next(by_line)
    next(by_half)

    def ticks():
        while sums.ticks < chunks + sums.stages() - 1:
            sums.tick(chunks)
            for _ in range(2):
                yield

    interleave(
        ticks(),
        by_row,
        by_line,
        by_half,
        seldom(vector_reduce(place, links, vector_terms, vector_land, vector_sems), 3),
    )
    table_sum[...] = slab_at(place.dp, place.half)[...]
    vector_sum[...] = vector_terms[bits + 2]
    word_copy.wait()
    links.finish()
    sums.finish(chunks)


def backward_all(devices, owns, slab_rows, weights, vectors, boxes, segments, offsets, kept):
    bits = (devices // 4).bit_length() - 1
    dps = 2**bits
    tokens, width = kept[0].shape
    anywhere = pl.BlockSpec(memory_space=pl.ANY)
    in_vmem = pl.BlockSpec(memory_space=pltpu.VMEM)
    fourth, part = width // 4, width // PARTS
    chunks = 3 * PARTS
    landing = sum(ladder(part, bits)[1:])
    held_rows = max(8 * width, 2 * dps * slab_rows)
    shape = jax.ShapeDtypeStruct
    return pl.pallas_call(
        functools.partial(backward_kernel, bits, owns, slab_rows),
        out_shape=[
            shape((tokens, width), F32),
            shape((chunks, part, width), BF16),
            shape((slab_rows, width), BF16),
            shape((16, width), F32),
        ],
        in_specs=[anywhere]
        + [in_vmem] * 6
        + [anywhere] * 2
        + [in_vmem]
        + [anywhere] * 2
        + [in_vmem]
        + [anywhere] * 2
        + [in_vmem]
        + [anywhere] * 2,
        out_specs=[anywhere] + [in_vmem] * 3,
        scratch_shapes=[
            pltpu.VMEM((held_rows, width), BF16),
            pltpu.VMEM((tokens, width), BF16),
            pltpu.VMEM((tokens, width), BF16),
            pltpu.VMEM((4, 3 * fourth, tokens), BF16),
            pltpu.VMEM((4, fourth, tokens), BF16),
            pltpu.VMEM((tokens, width), BF16),
            pltpu.VMEM((tokens, width), BF16),
            pltpu.VMEM((4, tokens, width), BF16),
            pltpu.VMEM((4, tokens, width), BF16),
            pltpu.VMEM((SLOTS, 2, part, width), BF16),
            pltpu.VMEM((chunks, 2, part, width), BF16),
            pltpu.VMEM((SLOTS, 2, part, width), BF16),
            pltpu.VMEM((chunks, part, width), BF16),
            pltpu.VMEM((chunks, landing, width), BF16),
            pltpu.VMEM((3, 2 * dps - 1, slab_rows, width // 3), BF16),
            pltpu.VMEM((tokens, width), BF16),
            pltpu.VMEM((2, 8, tokens), jnp.int32),
            pltpu.VMEM((bits + 3, 16, width), F32),
            pltpu.VMEM((bits + 2, 16, width), F32),
            pltpu.VMEM((tokens, width), F32),
            pltpu.VMEM((tokens, width), BF16),
            pltpu.VMEM((2, tokens // 2 + 128, tokens // 2), BF16),
            pltpu.VMEM((4, fourth, tokens), BF16),
            pltpu.VMEM((4, 3 * fourth, tokens), BF16),
            pltpu.VMEM((2, 2 * slab_rows, tokens), BF16),
            pltpu.SemaphoreType.DMA((6 * dps + 40,)),
            pltpu.SemaphoreType.DMA((2 + 2 * bits, chunks)),
            pltpu.SemaphoreType.DMA((2 + 2 * bits, chunks)),
            pltpu.SemaphoreType.DMA((3, 2 * dps - 1)),
            pltpu.SemaphoreType.DMA((bits + 2,)),
            pltpu.SemaphoreType.DMA((2,)),
            pltpu.SemaphoreType.DMA((4, 4)),
            pltpu.SemaphoreType.DMA((6,)),
            pltpu.SemaphoreType.REGULAR,
        ],
        name="backward_all",
        compiler_params=pltpu.CompilerParams(
            collective_id=1, has_side_effects=True, vmem_limit_bytes=60 * 2**20
        ),
    )(weights, vectors, boxes, segments, offsets, *kept)


def body(
    devices,
    word_vectors,
    position_table,
    horizontal_table,
    vertical_table,
    height_table,
    width_table,
    embed_gain,
    embed_shift,
    w_query,
    b_query,
    w_key,
    w_value,
    b_value,
    w_out,
    b_out,
    attn_gain,
    attn_shift,
    w_in,
    b_in,
    w_down,
    b_down,
    ffn_gain,
    ffn_shift,
    boxes,
    segments,
    offsets,
    cotangent,
):
    own_rows, width = word_vectors.shape
    t = lax.axis_index("tensor")
    owned = (position_table, horizontal_table, vertical_table, height_table, width_table)
    slab_rows = sum(table.shape[0] for table in owned)
    slab_padded = -(-slab_rows // 16) * 16
    slabs = owned
    if slab_padded > slab_rows or any(table.shape[0] % 16 for table in owned):
        slab = jnp.concatenate(owned, axis=0)
        slabs = (jnp.pad(slab, ((0, slab_padded - slab_rows), (0, 0))),)
    fourth = w_query.shape[0]
    bias_rows = jnp.concatenate([b_query, b_value, jnp.zeros((2 * fourth,), F32)])
    vectors = jnp.concatenate(
        [embed_gain, embed_shift, b_out, attn_gain, attn_shift, b_down, ffn_gain, ffn_shift]
        + [b_in, bias_rows, jnp.zeros((6 * width,), F32)]
    ).reshape(16, width)
    owns = tuple(table.shape[0] for table in owned)
    layer_out, grad_ffn_sum, ffn_vectors, weights, *kept = forward_all(
        devices,
        owns,
        slab_padded,
        slabs,
        (w_query, w_key, w_value, w_out, w_in, w_down),
        vectors,
        word_vectors,
        boxes,
        segments,
        offsets,
        cotangent,
    )
    grad_word, weight_sums, table_sum, vector_sum = backward_all(
        devices,
        owns,
        slab_padded,
        weights,
        vectors,
        boxes,
        segments,
        offsets,
        (grad_ffn_sum, ffn_vectors, *kept),
    )
    tall_sum, wide_sum, square_sum = weight_sums.astype(F32).reshape(3, width, width)
    table_sum = table_sum.astype(F32)
    first = [0]
    for own in owns:
        first.append(first[-1] + own)
    bias_in = lax.dynamic_slice_in_dim(vector_sum, 8 + t, 1)[0]
    bias_row = lax.dynamic_slice_in_dim(vector_sum, 12 + t, 1)[0]
    bias_query, bias_value = bias_row[:fourth], bias_row[2 * fourth : 3 * fourth]
    return (
        layer_out,
        grad_word,
        *(table_sum[first[k] : first[k + 1]] for k in range(5)),
        vector_sum[0],
        vector_sum[1],
        square_sum[:fourth],
        bias_query,
        square_sum[fourth : 2 * fourth],
        square_sum[2 * fourth : 3 * fourth],
        bias_value,
        square_sum[3 * fourth :],
        vector_sum[6],
        vector_sum[2],
        vector_sum[3],
        wide_sum,
        bias_in,
        tall_sum,
        vector_sum[7],
        vector_sum[4],
        vector_sum[5],
    )


def solution(mesh):
    devices = mesh.shape["dp"] * mesh.shape["tensor"]
    both = P(("dp", "tensor"), None)
    rows = P("tensor", None)
    return jax.shard_map(
        functools.partial(body, devices),
        mesh=mesh,
        in_specs=(
            *(both,) * 6,
            P(),
            P(),
            rows,
            P("tensor"),
            rows,
            rows,
            P("tensor"),
            rows,
            P(),
            P(),
            P(),
            P(None, "tensor"),
            P("tensor"),
            rows,
            P(),
            P(),
            P(),
            P(None, ("dp", "tensor")),
            P("dp", None),
            P("dp", None),
            both,
        ),
        out_specs=(
            *(both,) * 7,
            P(),
            P(),
            rows,
            P("tensor"),
            rows,
            rows,
            P("tensor"),
            rows,
            P(),
            P(),
            P(),
            P(None, "tensor"),
            P("tensor"),
            rows,
            P(),
            P(),
            P(),
        ),
        check_vma=False,
    )
```

```python
import functools

import jax
import jax.numpy as jnp
from jax import lax
from jax.experimental import pallas as pl
from jax.experimental.pallas import tpu as pltpu
from jax.sharding import PartitionSpec as P

HEAD = 64
MESH = pl.DeviceIdType.MESH
BF16 = jnp.bfloat16
F32 = jnp.float32

epsilon = 1e-06
masked_score = -1e30


class Place:
    def __init__(self, bits):
        self.bits = bits
        self.dp = lax.axis_index("dp")
        self.t = lax.axis_index("tensor")
        self.core = self.t % 2
        self.half = self.t // 2

    def bit(self, i):
        return (self.dp // 2**i) % 2

    def dp_flip(self, mask):
        dp = self.dp
        for i in range(self.bits):
            if mask & (1 << i):
                dp = dp + 2**i - 2 * 2**i * self.bit(i)
        return dp

    def t_flip(self, mask):
        t = self.t
        if mask & 1:
            t = t + 1 - 2 * self.core
        if mask & 2:
            t = t + 2 - 4 * self.half
        return t

    def partner(self, way):
        if way == "core":
            return (self.dp, self.t_flip(1))
        if way == "half":
            return (self.dp, self.t_flip(2))
        return (self.dp_flip(1 << way), self.t)

    def greet(self):
        barrier = pltpu.get_barrier_semaphore()
        ways = ["core", "half"] + list(range(self.bits))
        for way in ways:
            pl.semaphore_signal(
                barrier, inc=1, device_id=self.partner(way), device_id_type=MESH
            )
        pl.semaphore_wait(barrier, len(ways))


class Links:
    def __init__(self, place, send_sems):
        self.place = place
        self.send_sems = send_sems
        self.sent = []
        self.count = 0

    def send(self, way, src, dst, recv_sem):
        copy = pltpu.make_async_remote_copy(
            src_ref=src,
            dst_ref=dst,
            send_sem=self.send_sems.at[self.count],
            recv_sem=recv_sem,
            device_id=self.place.partner(way),
            device_id_type=MESH,
        )
        copy.start()
        self.count += 1
        self.sent.append(copy)
        return copy

    def arrived(self, way, dst, recv_sem):
        pltpu.make_async_remote_copy(
            src_ref=dst,
            dst_ref=dst,
            send_sem=recv_sem,
            recv_sem=recv_sem,
            device_id=self.place.partner(way),
            device_id_type=MESH,
        ).wait_recv()

    def finish(self):
        for copy in self.sent:
            copy.wait_send()


def seldom(steps, times):
    for _ in steps:
        for _ in range(times):
            yield


def interleave(*steps):
    live = list(steps)
    while live:
        for step in list(live):
            try:
                next(step)
            except StopIteration:
                live.remove(step)


def tables_gather(place, links, own, full, sems):
    bits = place.bits
    line_masks = [2 * k for k in range(2 ** (bits - 1))]
    line_sem, half_sem, row_sem, cross_sem, core_sem = sems

    def at(dp_mask, t_mask):
        return full.at[place.dp_flip(dp_mask) * 4 + place.t_flip(t_mask)]

    def to_core(slab, key):
        links.send("core", slab, slab, core_sem.at[key])

    def onward(mask, slab_source, below):
        for b in range(below - 1, 0, -1):
            links.send(b, slab_source, at(mask, 0), line_sem.at[(mask | (1 << b)) // 2])
        links.send("half", slab_source, at(mask, 0), half_sem.at[mask // 2])
        links.send(0, slab_source, at(mask, 0), row_sem.at[mask // 2])
        links.send("core", slab_source, at(mask, 0), core_sem.at[mask * 2])

    onward(0, own, bits)
    yield
    order = []
    held = [0]
    for b in range(bits - 1, 0, -1):
        fresh = [m | (1 << b) for m in held]
        for m in fresh:
            order.append((m, b))
        held = held + fresh
    for mask, b in order:
        links.arrived(b, at(mask, 0), line_sem.at[mask // 2])
        onward(mask, at(mask, 0), b)
        yield
    low = place.bit(1)
    for pair in range(len(line_masks) // 2):
        base = 4 * pair
        for mask in (base, base + 2):
            links.arrived("half", at(mask, 2), half_sem.at[mask // 2])
            to_core(at(mask, 2), mask * 2 + 1)
            links.arrived(0, at(mask + 1, 0), row_sem.at[mask // 2])
            to_core(at(mask + 1, 0), (mask + 1) * 2)
        yield
        dp_other = place.dp_flip(base)
        clear = dp_other - 2 * low
        here_clear = clear * 4 + place.t_flip(2)
        links.send(0, full.at[here_clear], full.at[here_clear], cross_sem.at[2 * pair + low])
        row_dp = place.dp_flip(base + 1)
        raised = row_dp + 2 * (1 - low)
        here_raised = raised * 4 + place.t
        links.send(
            "half", full.at[here_raised], full.at[here_raised], cross_sem.at[2 * pair + 1 - low]
        )
        yield
    def core_arrivals(row):
        for mask in line_masks:
            for t_mask in (0, 2):
                links.arrived(
                    "core",
                    at(mask + row, t_mask + 1),
                    core_sem.at[(mask + row) * 2 + t_mask // 2],
                )

    core_arrivals(0)
    yield "near"
    for pair in range(len(line_masks) // 2):
        base = 4 * pair
        dp_cross = place.dp_flip(base + 1)
        clear = (dp_cross - 2 * low) * 4 + place.t_flip(2)
        links.arrived(0, full.at[clear], cross_sem.at[2 * pair + low])
        links.send("core", full.at[clear], full.at[clear], core_sem.at[(base + 2 * low + 1) * 2 + 1])
        raised = (dp_cross + 2 * (1 - low)) * 4 + place.t_flip(2)
        links.arrived("half", full.at[raised], cross_sem.at[2 * pair + 1 - low])
        links.send(
            "core", full.at[raised], full.at[raised], core_sem.at[(base + 2 * (1 - low) + 1) * 2 + 1]
        )
        yield
    core_arrivals(1)
    yield


def added(left, right):
    return (left.astype(F32) + right.astype(F32)).astype(BF16)


def product(left, right):
    return jnp.dot(left, right, preferred_element_type=F32)


def inner_rows(left, right):
    return lax.dot_general(left, right, (((0,), (0,)), ((), ())), preferred_element_type=F32)


def against_rows(left, right):
    return lax.dot_general(left, right, (((1,), (1,)), ((), ())), preferred_element_type=F32)


CHUNKS = 2


def chunk_rows(place, weights, j, near_row, near_line):
    side = weights.shape[2] // 4
    rows = side // CHUNKS
    row = place.bit(0) if near_row else 1 - place.bit(0)
    line = place.bit(1) if near_line else 1 - place.bit(1)
    start = (2 * row + line) * side + (j % CHUNKS) * rows
    return j // CHUNKS, pl.ds(pl.multiple_of(start, rows), rows)


class Weights:
    def __init__(self, place, weights, send_sems, recv_sems, own_send, own_recv):
        self.place = place
        self.weights = weights
        self.send_sems = send_sems
        self.recv_sems = recv_sems
        self.own_send = own_send
        self.own_recv = own_recv

    def copy(self, way, lane, j, t, near_row=True, near_line=True):
        matrix, rows = chunk_rows(self.place, self.weights, j, near_row, near_line)
        block = self.weights.at[matrix, t, rows]
        return pltpu.make_async_remote_copy(
            src_ref=block,
            dst_ref=block,
            send_sem=self.send_sems.at[lane, j],
            recv_sem=self.recv_sems.at[lane, j],
            device_id=self.place.partner(way),
            device_id_type=MESH,
        )

    def own(self, i):
        block = self.weights.at[i, self.place.t]
        return pltpu.make_async_remote_copy(
            src_ref=block,
            dst_ref=block,
            send_sem=self.own_send.at[i],
            recv_sem=self.own_recv.at[i],
            device_id=self.place.partner("core"),
            device_id_type=MESH,
        )

    def own_arrived(self, i):
        block = self.weights.at[i, self.place.t_flip(1)]
        pltpu.make_async_remote_copy(
            src_ref=block,
            dst_ref=block,
            send_sem=self.own_send.at[i],
            recv_sem=self.own_recv.at[i],
            device_id=self.place.partner("core"),
            device_id_type=MESH,
        ).wait_recv()

    def issue(self, j):
        self.copy("half", 0, j, self.place.t).start()

    def take_half(self, j):
        other = self.place.t_flip(2)
        self.copy("half", 0, j, other).wait_recv()
        self.copy(0, 1, j, other).start()
        self.copy(1, 2, j, other).start()
        self.copy("core", 4, j, other).start()

    def take_row(self, j):
        other = self.place.t_flip(2)
        self.copy(0, 1, j, other, False).wait_recv()
        self.copy(1, 3, j, other, False).start()
        self.copy("core", 5, j, other, False).start()

    def take_line(self, j):
        other = self.place.t_flip(2)
        for lane, near_row in ((2, True), (3, False)):
            self.copy(1, lane, j, other, near_row, False).wait_recv()
            self.copy("core", lane + 4, j, other, near_row, False).start()

    def settle(self, j):
        cross = self.place.t_flip(3)
        for lane, near_row, near_line in self.core_lanes():
            self.copy("core", lane, j, cross, near_row, near_line).wait_recv()

    def core_lanes(self):
        return ((4, True, True), (5, False, True), (6, True, False), (7, False, False))

    def finish(self, count):
        for i in range(3):
            self.own(i).wait_send()

        def one(j, carry):
            other = self.place.t_flip(2)
            self.copy("half", 0, j, self.place.t).wait_send()
            self.copy(0, 1, j, other).wait_send()
            self.copy(1, 2, j, other).wait_send()
            self.copy(1, 3, j, other, False).wait_send()
            for lane, near_row, near_line in self.core_lanes():
                self.copy("core", lane, j, other, near_row, near_line).wait_send()
            return carry

        lax.fori_loop(0, count, one, 0)


def row_counts(lookup_rows, device, owns, slab_rows, tokens):
    by_table = ((0, (0,)), (1, (1, 3)), (2, (2, 4)), (3, (5,)), (4, (6,)))
    if all(own % 16 == 0 for own in owns):
        pieces = []
        for k, which in by_table:
            at = lax.broadcasted_iota(jnp.int32, (owns[k], tokens), 0) + device * owns[k]
            piece = sum(jnp.where(at == lookup_rows[w], 1.0, 0.0) for w in which)
            pieces.append(piece.astype(BF16))
        spare = slab_rows - sum(owns)
        if spare:
            pieces.append(jnp.zeros((spare, tokens), BF16))
        return jnp.concatenate(pieces, axis=0)
    at = lax.broadcasted_iota(jnp.int32, (slab_rows, tokens), 0)
    total = jnp.zeros((slab_rows, tokens), F32)
    first = 0
    for k, which in by_table:
        for w in which:
            local = lookup_rows[w] - device * owns[k]
            inside = (local >= 0) & (local < owns[k])
            total = total + jnp.where(at == jnp.where(inside, local + first, -1), 1.0, 0.0)
        first += owns[k]
    return total.astype(BF16)


def lookup_rows_of(boxes, segments, offsets, t):
    tokens = segments.shape[1]
    pages = offsets.shape[1]
    seg = segments[pl.ds(t, 1), :]
    label = lax.broadcasted_iota(jnp.int32, (pages, tokens), 0)
    place_in = lax.broadcasted_iota(jnp.int32, (pages, tokens), 1).astype(F32)
    member = label == seg
    starts = jnp.min(jnp.where(member, place_in, float(tokens)), axis=1, keepdims=True)
    shift_row = offsets[pl.ds(t, 1), :].astype(F32)
    eye = lax.broadcasted_iota(jnp.int32, (pages, pages), 0) == lax.broadcasted_iota(
        jnp.int32, (pages, pages), 1
    )
    shift = jnp.sum(jnp.where(eye, shift_row, 0.0), axis=1, keepdims=True)
    moved = jnp.sum(jnp.where(member, place_in - starts + shift, 0.0), axis=0, keepdims=True)
    positions = moved.astype(jnp.int32)
    x0, y0, x1, y1 = (boxes[i : i + 1, :] for i in range(4))
    return (positions, x0, y0, x1, y1, jnp.abs(y1 - y0), jnp.abs(x1 - x0)), seg


def norm_parts(values):
    width = values.shape[1]
    row_mean = jnp.sum(values, axis=1, keepdims=True) * (1.0 / width)
    row_var = jnp.sum(values * values, axis=1, keepdims=True) * (1.0 / width) - row_mean * row_mean
    scaled = lax.rsqrt(row_var + epsilon)
    return (values - row_mean) * scaled, scaled


ROWS = 64


def by_rows(count, step):
    def one(i, carry):
        step(pl.ds(pl.multiple_of(i * ROWS, ROWS), ROWS))
        return carry

    lax.fori_loop(0, count // ROWS, one, 0)


def head_blocks(tokens):
    half, reach = tokens // 2, 128
    return ((0, half, 0, half + reach), (half, half, half - reach, half + reach))


def mask_pages(segments_row, masks):
    tokens = segments_row.shape[1]
    rows = jnp.broadcast_to(segments_row.astype(F32), (8, tokens))
    columns = jnp.transpose(rows)
    for i, (q, nq, k, nk) in enumerate(head_blocks(tokens)):
        same = columns[k : k + nk, 0:1] == rows[0:1, q : q + nq]
        masks[i] = jnp.where(same, 0.0, masked_score).astype(masks.dtype)


def forward_kernel(
    bits,
    owns,
    slab_rows,
    pieces,
    *refs,
):
    slabs, refs = refs[:pieces], refs[pieces:]
    forward_body(bits, owns, slab_rows, slabs, *refs)


def forward_body(
    bits,
    owns,
    slab_rows,
    slabs,
    w_query,
    w_key,
    w_value,
    w_out,
    wide,
    tall,
    vectors,
    word,
    boxes,
    segments,
    offsets,
    cotangent,
    layer_out,
    grad_sum,
    grad_vectors,
    weights_out,
    inputs_low_out,
    centered_in_out,
    scaled_in,
    projected_out,
    mixed_out,
    stats,
    mid_low_out,
    centered_mid_out,
    scaled_mid,
    hidden_out,
    slopes_out,
    inputs_low,
    centered_in,
    projected,
    mixed,
    mid_low,
    centered_mid,
    hidden,
    slopes,
    tables,
    counts,
    weights,
    biases,
    normed,
    total,
    masks,
    send_sems,
    line_sem,
    half_sem,
    row_sem,
    cross_sem,
    core_sem,
    weight_send,
    weight_recv,
    own_send,
    own_recv,
    bias_sems,
    local_sems,
    own_sems,
    ship_sems,
):
    place = Place(bits)
    tokens, width = word.shape
    dps = 2**bits
    t = place.t
    me = place.dp * 4 + t
    local = copies_into(tables.at[me], slabs, own_sems.at[3])
    owned = [
        copies_into(weights.at[i, t], sources, own_sems.at[i])
        for i, sources in enumerate(((w_query, w_key, w_value, w_out), (wide,), (tall,)))
    ]
    for copy in local + owned[0] + owned[1] + owned[2]:
        copy.start()
    shipped = []

    def ship(source, target):
        copy = pltpu.make_async_copy(source, target, ship_sems.at[len(shipped)])
        copy.start()
        shipped.append(copy)

    place.greet()
    links = Links(place, send_sems)
    flow = Weights(place, weights, weight_send, weight_recv, own_send, own_recv)
    chunks = 3 * CHUNKS
    for copy in local:
        copy.wait()
    gather = tables_gather(
        place, links, tables.at[me], tables, (line_sem, half_sem, row_sem, cross_sem, core_sem)
    )
    next(gather)
    bias = vectors.at[pl.ds(8, 8)]
    biases[t] = vectors[8:16]
    links.send("core", bias, biases.at[t], bias_sems.at[0])
    links.send("half", bias, biases.at[t], bias_sems.at[1])
    for i, copies in enumerate(owned):
        for copy in copies:
            copy.wait()
        flow.own(i).start()
    flow.issue(0)
    flow.issue(1)

    lookup, seg = lookup_rows_of(boxes, segments, offsets, t)

    def count_dp(dp, carry):
        for j in range(4):
            counts[dp, j * slab_rows : (j + 1) * slab_rows, :] = row_counts(
                lookup, dp * 4 + j, owns, slab_rows, tokens
            )
        return carry

    lax.fori_loop(0, dps, count_dp, 0)
    mask_pages(seg, masks)
    total[...] = word[...].astype(F32)
    def embed(row_bit):
        def one(i, carry):
            dp = 2 * i + row_bit
            rows = tables[pl.ds(dp * 4, 4)].reshape(4 * slab_rows, width)
            total[...] += inner_rows(counts[dp], rows)
            return carry

        lax.fori_loop(0, dps // 2, one, 0)

    for step in gather:
        if step == "near":
            break
    links.arrived("half", biases.at[place.t_flip(2)], bias_sems.at[1])
    links.send("core", biases.at[place.t_flip(2)], biases.at[place.t_flip(2)], bias_sems.at[2])
    flow.take_half(0)
    flow.issue(2)
    embed(place.bit(0))
    flow.take_half(1)
    flow.issue(3)
    flow.take_row(0)
    for step in gather:
        pass
    flow.take_row(1)
    flow.take_line(0)
    embed(1 - place.bit(0))
    flow.take_half(2)
    flow.issue(4)
    flow.take_line(1)

    def norm_in(rows):
        centered, scaled = norm_parts(total[rows])
        centered_in[rows] = centered.astype(BF16)
        scaled_in[rows] = scaled
        result = centered * vectors[0:1] + vectors[1:2]
        normed[rows] = result
        inputs_low[rows] = result.astype(BF16)

    by_rows(tokens, norm_in)
    ship(inputs_low, inputs_low_out)
    ship(centered_in, centered_in_out)
    flow.take_half(3)
    flow.issue(5)
    flow.take_row(2)
    links.arrived("core", biases.at[place.t_flip(1)], bias_sems.at[0])
    links.arrived("core", biases.at[place.t_flip(3)], bias_sems.at[2])
    flow.own_arrived(0)
    flow.settle(0)
    flow.settle(1)
    fourth = width // 4

    def project(j, carry):
        columns = jnp.transpose(biases[j])
        zeros = jnp.zeros((fourth, 1), F32)
        column = jnp.concatenate(
            [columns[0:fourth, 1:2], zeros, columns[fourth : 2 * fourth, 1:2]], axis=0
        )
        projected[j] = (
            against_rows(weights[0, j, : 3 * fourth, :], inputs_low[...]) + column
        ).astype(BF16)
        return carry

    lax.fori_loop(0, 4, project, 0)
    ship(projected, projected_out)
    flow.take_half(4)
    flow.take_row(3)

    def attend(j, carry):
        for h in range(fourth // HEAD):
            rows = slice(h * HEAD, (h + 1) * HEAD)
            key_rows = slice(fourth + h * HEAD, fourth + (h + 1) * HEAD)
            value_rows = slice(2 * fourth + h * HEAD, 2 * fourth + (h + 1) * HEAD)
            for i, (q, nq, k, nk) in enumerate(head_blocks(tokens)):
                scores = (
                    inner_rows(
                        projected[j, key_rows, k : k + nk], projected[j, rows, q : q + nq]
                    )
                    * HEAD ** (-0.5)
                    + masks[i]
                )
                peak = jnp.max(scores, axis=0, keepdims=True)
                exponent = jnp.exp(scores - peak)
                all_of = jnp.sum(exponent, axis=0, keepdims=True)
                stats[j, h : h + 1, q : q + nq] = peak + jnp.log(all_of)
                share = (exponent * (1.0 / all_of)).astype(BF16)
                mixed[j, rows, q : q + nq] = product(
                    projected[j, value_rows, k : k + nk], share
                ).astype(BF16)
        return carry

    def attend_and_pass(j, carry):
        attend(j, carry)

        @pl.when(j < 1)
        def _():
            flow.take_half(5)

        @pl.when(j < 2)
        def _():
            flow.take_row(j + 4)

        @pl.when(j >= 1)
        def _():
            flow.take_line(j + 1)

        return carry

    lax.fori_loop(0, 4, attend_and_pass, 0)
    ship(mixed, mixed_out)
    out_rows = weights[0, :, 3 * fourth :, :].reshape(width, width)
    total[...] = inner_rows(mixed[...].reshape(width, tokens), out_rows)

    def norm_mid(rows):
        centered, scaled = norm_parts(total[rows] + vectors[2:3] + normed[rows])
        centered_mid[rows] = centered.astype(BF16)
        scaled_mid[rows] = scaled
        result = centered * vectors[3:4] + vectors[4:5]
        normed[rows] = result
        mid_low[rows] = result.astype(BF16)

    by_rows(tokens, norm_mid)
    ship(mid_low, mid_low_out)
    ship(centered_mid, centered_mid_out)
    total[...] = jnp.zeros_like(total)
    columns = 256

    def feed_copies(j):
        return [
            pltpu.make_async_copy(source.at[j], target.at[j], local_sems.at[1 + i, j])
            for i, (source, target) in enumerate(((hidden, hidden_out), (slopes, slopes_out)))
        ]

    def feed(j):
        def one(n, carry):
            at = pl.ds(pl.multiple_of(n * columns, columns), columns)
            before = product(mid_low[...], weights[1, j, :, at]) + biases[j, 0:1, at]
            share = 0.5 * (1.0 + lax.erf(before * 0.5**0.5))
            hidden[j, :, at] = (before * share).astype(BF16)
            density = jnp.exp(before * before * -0.5) * 0.3989422804014327
            slopes[j, :, at] = (share + before * density).astype(BF16)
            return carry

        lax.fori_loop(0, width // columns, one, 0)
        total[...] += product(hidden[j], weights[2, j])
        for copy in feed_copies(j):
            copy.start()

    flow.own_arrived(1)
    flow.own_arrived(2)

    def feed_near(i, carry):
        feed(t + i * (1 - 2 * place.core))
        return carry

    lax.fori_loop(0, 2, feed_near, 0)
    flow.take_line(5)
    for j in range(CHUNKS, chunks):
        flow.settle(j)
    out_copy = pltpu.make_async_copy(weights, weights_out, local_sems.at[0, 0])
    out_copy.start()

    def feed_far(i, carry):
        feed(place.t_flip(2) + i * (1 - 2 * place.core))
        return carry

    lax.fori_loop(0, 2, feed_far, 0)
    grad_vectors[...] = jnp.zeros_like(grad_vectors)

    def norm_out(rows):
        centered, scaled = norm_parts(total[rows] + vectors[5:6] + normed[rows])
        layer_out[rows] = centered * vectors[6:7] + vectors[7:8]
        grad = cotangent[rows]
        grad_sum[rows] = norm_back(grad, centered, scaled, vectors[6:7])
        grad_vectors[0:1] += jnp.sum(grad * centered, axis=0, keepdims=True)
        grad_vectors[1:2] += jnp.sum(grad, axis=0, keepdims=True)
        grad_vectors[2:3] += jnp.sum(grad_sum[rows], axis=0, keepdims=True)

    by_rows(tokens, norm_out)
    out_copy.wait()
    for copy in shipped:
        copy.wait()
    for j in range(4):
        for copy in feed_copies(j):
            copy.wait()
    links.finish()
    flow.finish(chunks)


def norm_back(grad_out, centered, scaled, norm_gain):
    width = grad_out.shape[1]
    grad_centered = grad_out * norm_gain
    first_mean = jnp.sum(grad_centered, axis=1, keepdims=True) * (1.0 / width)
    second_mean = jnp.sum(grad_centered * centered, axis=1, keepdims=True) * (1.0 / width)
    return scaled * (grad_centered - first_mean - centered * second_mean)


def copies_into(target, sources, sems):
    first, copies = 0, []
    for i, source in enumerate(sources):
        rows = source.shape[0]
        copies.append(
            pltpu.make_async_copy(source, target.at[pl.ds(first, rows)], sems.at[i])
        )
        first += rows
    return copies


def forward_all(
    devices, owns, slab_rows, slabs, matrices, vectors, word, boxes, segments, offsets, cotangent
):
    bits = (devices // 4).bit_length() - 1
    dps = 2**bits
    lines = 2 ** (bits - 1)
    tokens, width = word.shape
    anywhere = pl.BlockSpec(memory_space=pl.ANY)
    in_vmem = pl.BlockSpec(memory_space=pltpu.VMEM)
    fourth = width // 4
    shape = jax.ShapeDtypeStruct
    return pl.pallas_call(
        functools.partial(forward_kernel, bits, owns, slab_rows, len(slabs)),
        out_shape=[
            shape((tokens, width), F32),
            shape((tokens, width), F32),
            shape((8, width), F32),
            shape((3, 4, width, width), BF16),
            shape((tokens, width), BF16),
            shape((tokens, width), BF16),
            shape((tokens, 1), F32),
            shape((4, 3 * fourth, tokens), BF16),
            shape((4, fourth, tokens), BF16),
            shape((4, 8, tokens), F32),
            shape((tokens, width), BF16),
            shape((tokens, width), BF16),
            shape((tokens, 1), F32),
            shape((4, tokens, width), BF16),
            shape((4, tokens, width), BF16),
        ],
        in_specs=[anywhere] * (len(slabs) + len(matrices)) + [in_vmem] * 6,
        out_specs=[in_vmem] * 3
        + [anywhere] * 3
        + [in_vmem]
        + [anywhere] * 2
        + [in_vmem]
        + [anywhere] * 2
        + [in_vmem]
        + [anywhere] * 2,
        scratch_shapes=[
            pltpu.VMEM((tokens, width), BF16),
            pltpu.VMEM((tokens, width), BF16),
            pltpu.VMEM((4, 3 * fourth, tokens), BF16),
            pltpu.VMEM((4, fourth, tokens), BF16),
            pltpu.VMEM((tokens, width), BF16),
            pltpu.VMEM((tokens, width), BF16),
            pltpu.VMEM((4, tokens, width), BF16),
            pltpu.VMEM((4, tokens, width), BF16),
            pltpu.VMEM((devices, slab_rows, width), BF16),
            pltpu.VMEM((dps, 4 * slab_rows, tokens), BF16),
            pltpu.VMEM((3, 4, width, width), BF16),
            pltpu.VMEM((4, 8, width), F32),
            pltpu.VMEM((tokens, width), F32),
            pltpu.VMEM((tokens, width), F32),
            pltpu.VMEM((2, tokens // 2 + 128, tokens // 2), F32),
            pltpu.SemaphoreType.DMA((10 * lines + 40 + lines * bits,)),
            pltpu.SemaphoreType.DMA((lines,)),
            pltpu.SemaphoreType.DMA((lines,)),
            pltpu.SemaphoreType.DMA((lines,)),
            pltpu.SemaphoreType.DMA((lines,)),
            pltpu.SemaphoreType.DMA((4 * lines,)),
            pltpu.SemaphoreType.DMA((8, 3 * CHUNKS)),
            pltpu.SemaphoreType.DMA((8, 3 * CHUNKS)),
            pltpu.SemaphoreType.DMA((3,)),
            pltpu.SemaphoreType.DMA((3,)),
            pltpu.SemaphoreType.DMA((3,)),
            pltpu.SemaphoreType.DMA((3, 4)),
            pltpu.SemaphoreType.DMA((4, max(4, len(slabs)))),
            pltpu.SemaphoreType.DMA((6,)),
        ],
        name="forward_all",
        compiler_params=pltpu.CompilerParams(
            collective_id=0, has_side_effects=True, vmem_limit_bytes=60 * 2**20
        ),
    )(*slabs, *matrices, vectors, word, boxes, segments, offsets, cotangent)


def ladder(rows, bits):
    left = [rows]
    for b in range(bits):
        halves = left[-1] % 32 == 0 and b < bits - 1
        left.append(left[-1] // 2 if halves else left[-1])
    return left


SLOTS = 3
DEPTH = 2
PARTS = 3


class Sums:
    def __init__(self, place, outgoing, own, from_core, from_half, from_dp, total, sems, credit):
        self.place = place
        self.outgoing = outgoing
        self.own = own
        self.from_core = from_core
        self.from_half = from_half
        self.from_dp = from_dp
        self.total = total
        self.send_sems, self.recv_sems = sems
        self.credit = credit
        self.rows = own.shape[2]
        self.left = ladder(self.rows, place.bits)
        self.back = [b for b in range(place.bits) if self.left[b + 1] < self.left[b]]
        self.taken = 0
        self.issued = 0
        self.ticks = 0

    def copy(self, way, lane, j, src, dst):
        return pltpu.make_async_remote_copy(
            src_ref=src,
            dst_ref=dst,
            send_sem=self.send_sems.at[lane, j],
            recv_sem=self.recv_sems.at[lane, j],
            device_id=self.place.partner(way),
            device_id_type=MESH,
        )

    def start_of(self, level):
        start = 0
        for b in range(level):
            if self.left[b + 1] < self.left[b]:
                start = start + self.place.bit(b) * self.left[b + 1]
        return start

    def span(self, b, near):
        start, rows = self.start_of(b), self.left[b + 1]
        if rows < self.left[b]:
            bit = self.place.bit(b)
            start = start + (bit if near else 1 - bit) * rows
        return pl.ds(pl.multiple_of(start, 16), rows) if b or rows < self.left[0] else pl.ds(0, rows)

    def landing(self, b, j):
        first = sum(self.left[1 : b + 1])
        return self.from_dp.at[j, pl.ds(first, self.left[b + 1])]

    def core(self, j):
        slot = j % SLOTS
        return self.copy("core", 0, j, self.outgoing.at[slot], self.from_core.at[slot])

    def half(self, j):
        return self.copy("half", 1, j, self.own.at[j, 1], self.from_half.at[j])

    def dp(self, b, j):
        return self.copy(
            b, 2 + b, j, self.own.at[j, 0, self.span(b, False)], self.landing(b, j)
        )

    def gather(self, b, j, near=True):
        block = self.total.at[j, self.span(b, near)]
        return self.copy(b, 2 + self.place.bits + b, j, block, block)

    def launch(self, j):
        if j >= SLOTS:
            pl.semaphore_wait(self.credit, 1)
        self.core(j).start()

    def take_core(self, j, count):
        slot = j % SLOTS
        self.core(j).wait_recv()
        for which in (1, 0):
            self.own[j, which] = added(self.own[j, which], self.from_core[slot, which])
        if j + SLOTS < count:
            pl.semaphore_signal(
                self.credit, inc=1, device_id=self.place.partner("core"), device_id_type=MESH
            )
        self.taken = j + 1
        self.pump()

    def pump(self):
        while self.issued < min(self.taken, self.ticks + DEPTH):
            self.half(self.issued).start()
            self.issued += 1

    def tick(self, count):
        k = self.ticks
        self.ticks += 1
        for s in range(self.stages()):
            if 0 <= k - s < count:
                self.stage(s, k - s)

    def take_half(self, j):
        self.half(j).wait_recv()
        self.pump()
        span = self.span(0, False)
        self.own[j, 0, span] = added(self.own[j, 0, span], self.from_half[j, span])
        self.dp(0, j).start()
        if self.left[1] < self.left[0]:
            span = self.span(0, True)
            self.own[j, 0, span] = added(self.own[j, 0, span], self.from_half[j, span])

    def take_dp(self, b, j):
        self.dp(b, j).wait_recv()
        span, first = self.span(b, True), sum(self.left[1 : b + 1])
        arrived = self.from_dp[j, pl.ds(first, self.left[b + 1])]
        if b == self.place.bits - 1:
            self.total[j, span] = added(self.own[j, 0, span], arrived)
            if self.back:
                self.gather(self.back[-1], j).start()
            return
        if self.left[b + 1] == self.left[b]:
            self.dp(b, j).wait_send()
        self.own[j, 0, span] = added(self.own[j, 0, span], arrived)
        self.dp(b + 1, j).start()

    def take_back(self, i, j):
        order = self.back[::-1]
        self.gather(order[i], j, False).wait_recv()
        if i + 1 < len(order):
            self.gather(order[i + 1], j).start()

    def stages(self):
        return 1 + self.place.bits + len(self.back)

    def stage(self, s, j):
        if s == 0:
            self.take_half(j)
        elif s <= self.place.bits:
            self.take_dp(s - 1, j)
        else:
            self.take_back(s - 1 - self.place.bits, j)

    def finish(self, count):
        for j in range(max(0, count - SLOTS), count):
            self.core(j).wait_send()

        def one(j, carry):
            self.half(j).wait_send()
            for b in range(self.place.bits):
                if self.left[b + 1] < self.left[b] or b == self.place.bits - 1:
                    self.dp(b, j).wait_send()
            for b in self.back:
                self.gather(b, j).wait_send()
            return carry

        lax.fori_loop(0, count, one, 0)


def table_reduce(place, links, slab_at, columns, order, landing, sems):
    bits = place.bits
    flags = [1 << (bits if way == "half" else way) for way in order]

    def slab(mask):
        half = 1 - place.half if mask >> bits else place.half
        return slab_at(place.dp_flip(mask % (1 << bits)), half).at[:, columns]

    def first(mask):
        for i, flag in enumerate(flags):
            if mask & flag:
                return i
        return len(flags)

    every = sorted(range(2 ** (bits + 1)), key=lambda m: (first(m), m))
    slots = {}
    for i in range(len(flags)):
        for mask in every:
            if first(mask) > i:
                slots[i, mask] = len(slots)

    def send(i, mask):
        slot = slots[i, mask ^ flags[i]]
        links.send(order[i], slab(mask), landing.at[slot], sems.at[slot])

    for mask in sorted(
        (m for m in every if first(m) == 0), key=lambda m: (first(m ^ flags[0]), m)
    ):
        send(0, mask)
    yield
    for i in range(len(flags)):
        for mask in every:
            if first(mask) > i:
                slot = slots[i, mask]
                links.arrived(order[i], landing.at[slot], sems.at[slot])
                target = slab(mask)
                target[...] = added(target[...], landing[slot])
                if first(mask) == i + 1 < len(flags):
                    send(i + 1, mask)
                yield


def vector_reduce(place, links, vectors, landing, sems):
    for i, way in enumerate(["core", "half"] + list(range(place.bits))):
        links.send(way, vectors.at[i], landing.at[i], sems.at[i])
        yield
        links.arrived(way, landing.at[i], sems.at[i])
        vectors[i + 1] = vectors[i] + landing[i]


def backward_kernel(
    bits,
    owns,
    slab_rows,
    weights_in,
    vectors,
    boxes,
    segments,
    offsets,
    grad_sum,
    ffn_vectors,
    inputs_low_in,
    centered_in_in,
    scaled_in,
    projected_in,
    mixed_in,
    stats,
    mid_low_in,
    centered_mid_in,
    scaled_mid,
    hidden_in,
    slopes_in,
    grad_word,
    weight_sums,
    table_sum,
    vector_sum,
    held,
    inputs_low,
    centered_in,
    projected,
    mixed,
    mid_low,
    centered_mid,
    hidden,
    slopes,
    outgoing,
    own,
    from_core,
    from_half,
    from_dp,
    landing,
    words,
    lookups,
    vector_terms,
    vector_land,
    total,
    low,
    masks,
    grad_heads,
    grad_projected,
    counts,
    send_sems,
    sum_send,
    sum_recv,
    landing_sems,
    vector_sems,
    word_sems,
    local_sems,
    later_sems,
    credit,
):
    place = Place(bits)
    tokens, width = grad_sum.shape
    dps = 2**bits
    t, core = place.t, place.core
    fourth = width // 4
    part = width // PARTS
    quarter_rows = width
    loads = {}
    for i, (matrix, slot) in enumerate(((2, 0), (1, 1), (0, 0))):
        loads[matrix] = [
            pltpu.make_async_copy(
                weights_in.at[matrix, q],
                held.at[pl.ds((slot * 4 + q) * quarter_rows, quarter_rows)],
                local_sems.at[matrix, q],
            )
            for q in range(4)
        ]
    early = [
        pltpu.make_async_copy(hidden_in, hidden, local_sems.at[3, 0]),
        pltpu.make_async_copy(slopes_in, slopes, local_sems.at[3, 1]),
    ]
    later = [
        pltpu.make_async_copy(source, target, later_sems.at[i])
        for i, (source, target) in enumerate(
            (
                (mid_low_in, mid_low),
                (centered_mid_in, centered_mid),
                (projected_in, projected),
                (mixed_in, mixed),
                (inputs_low_in, inputs_low),
                (centered_in_in, centered_in),
            )
        )
    ]
    for copy in loads[2] + early + loads[1] + later:
        copy.start()
    place.greet()
    links = Links(place, send_sems)
    sums = Sums(
        place, outgoing, own, from_core, from_half, from_dp, weight_sums, (sum_send, sum_recv), credit
    )
    chunks = 3 * PARTS

    def quarter(parity, other):
        q = t + other * (2 - 4 * place.half)
        return q + 1 - 2 * core if parity else q

    def held_rows(slot, q, first=0, rows=width):
        start = (slot * 4 + q) * quarter_rows + first
        return held[pl.ds(pl.multiple_of(start, 16), rows)]

    lookup, seg = lookup_rows_of(boxes, segments, offsets, t)
    mask_pages(seg, masks)
    lookups[0] = jnp.concatenate(list(lookup) + [lookup[0]], axis=0)
    links.send("core", lookups.at[0], lookups.at[1], word_sems.at[0])

    def start_rows(rows):
        low[rows] = grad_sum[rows].astype(BF16)

    by_rows(tokens, start_rows)
    vector_terms[0] = jnp.zeros_like(vector_terms[0])
    vector_terms[0, 4:6] = ffn_vectors[0:2]
    vector_terms[0, 7:8] = ffn_vectors[2:3]
    for copy in loads[2] + early:
        copy.wait()

    def chunk(j, term):
        slot = j % SLOTS
        if j >= SLOTS:
            sums.core(j - SLOTS).wait_send()

        def out(i, carry):
            outgoing[slot, i] = term(quarter(1, i)).astype(BF16)
            return carry

        def keep(i, carry):
            own[j, i] = term(quarter(0, i)).astype(BF16)
            return carry

        lax.fori_loop(0, 2, out, 0)
        sums.launch(j)
        lax.fori_loop(0, 2, keep, 0)

    def down_term(part_at, q):
        at = pl.ds(part_at * part, part)
        back = against_rows(low[...], held_rows(0, q, part_at * part, part))
        before = (back * slopes[q, :, at].astype(F32)).astype(BF16)
        slopes[q, :, at] = before
        vector_terms[0, pl.ds(8 + q, 1), at] = jnp.sum(
            before.astype(F32), axis=0, keepdims=True
        )
        return inner_rows(hidden[q, :, at], low[...])

    for p in range(PARTS):
        chunk(p, functools.partial(down_term, p))
        if p:
            sums.take_core(p - 1, chunks)
    for copy in loads[0]:
        copy.start()
    sums.take_core(PARTS - 1, chunks)
    for copy in loads[1] + later:
        copy.wait()
    for p in range(PARTS):
        columns = slice(p * part, (p + 1) * part)
        chunk(PARTS + p, lambda q: inner_rows(mid_low[:, columns], slopes[q]))
        if p:
            sums.take_core(PARTS + p - 1, chunks)
        if p == PARTS - 1:
            sums.tick(chunks)
    total[...] = grad_sum[...]

    def mid_term(q, carry):
        total[...] += against_rows(slopes[q], held_rows(1, q))
        return carry

    lax.fori_loop(0, 4, mid_term, 0)
    sums.take_core(2 * PARTS - 1, chunks)

    def mid_back(rows):
        centered = centered_mid[rows].astype(F32)
        grad = total[rows]
        result = norm_back(grad, centered, scaled_mid[rows], vectors[3:4])
        vector_terms[0, 2:3] += jnp.sum(grad * centered, axis=0, keepdims=True)
        vector_terms[0, 3:4] += jnp.sum(grad, axis=0, keepdims=True)
        vector_terms[0, 6:7] += jnp.sum(result, axis=0, keepdims=True)
        total[rows] = result
        low[rows] = result.astype(BF16)

    by_rows(tokens, mid_back)
    for copy in loads[0]:
        copy.wait()

    def out_back(q, carry):
        grad_heads[q] = against_rows(held_rows(0, q, 3 * fourth, fourth), low[...]).astype(BF16)
        return carry

    lax.fori_loop(0, 4, out_back, 0)
    sums.tick(chunks)
    scale = HEAD ** (-0.5)

    def attend_back(j, carry):
        for h in range(fourth // HEAD):
            rows = slice(h * HEAD, (h + 1) * HEAD)
            key_rows = slice(fourth + h * HEAD, fourth + (h + 1) * HEAD)
            value_rows = slice(2 * fourth + h * HEAD, 2 * fourth + (h + 1) * HEAD)
            grads = []
            for i, (q, nq, k, nk) in enumerate(head_blocks(tokens)):
                queries = projected[j, rows, q : q + nq]
                keys = projected[j, key_rows, k : k + nk]
                values = projected[j, value_rows, k : k + nk]
                grad = grad_heads[j, rows, q : q + nq]
                scores = inner_rows(keys, queries) * scale + masks[i].astype(F32)
                share = jnp.exp(scores - stats[j, h : h + 1, q : q + nq])
                back = inner_rows(values, grad)
                inner = jnp.sum(share * back, axis=0, keepdims=True)
                grad_scores = (share * (back - inner)).astype(BF16)
                grad_projected[j, rows, q : q + nq] = (product(keys, grad_scores) * scale).astype(BF16)
                grads.append(
                    (
                        against_rows(queries, grad_scores) * scale,
                        against_rows(grad, share.astype(BF16)),
                    )
                )
            reach = 128
            for target, (first, second) in zip((key_rows, value_rows), zip(*grads)):
                edge = tokens // 2 - reach
                joined = jnp.concatenate(
                    [
                        first[:, :edge],
                        first[:, edge:] + second[:, : 2 * reach],
                        second[:, 2 * reach :],
                    ],
                    axis=1,
                )
                grad_projected[j, target, :] = joined.astype(BF16)
        ones = jnp.ones((8, tokens), BF16)
        vector_terms[0, pl.ds(12 + j, 1), 0 : 3 * fourth] = against_rows(ones, grad_projected[j])[0:1]
        return carry

    for j in (0, 2):
        lax.fori_loop(j, j + 2, attend_back, 0)
        sums.tick(chunks)

    def square_term(p, q):
        if p < PARTS - 1:
            return product(grad_projected[q, p * part : (p + 1) * part, :], inputs_low[...])
        return jnp.concatenate(
            [
                product(grad_projected[q, p * part :, :], inputs_low[...]),
                product(mixed[q], low[...]),
            ],
            axis=0,
        )

    for p in range(PARTS):
        chunk(2 * PARTS + p, functools.partial(square_term, p))

    def in_term(q, carry):
        total[...] += inner_rows(grad_projected[q], held_rows(0, q, 0, 3 * fourth))
        return carry

    lax.fori_loop(0, 4, in_term, 0)
    for p in range(PARTS):
        sums.take_core(2 * PARTS + p, chunks)

    def in_back(rows):
        centered = centered_in[rows].astype(F32)
        grad = total[rows]
        result = norm_back(grad, centered, scaled_in[rows], vectors[0:1])
        vector_terms[0, 0:1] += jnp.sum(grad * centered, axis=0, keepdims=True)
        vector_terms[0, 1:2] += jnp.sum(grad, axis=0, keepdims=True)
        total[rows] = result
        low[rows] = result.astype(BF16)

    by_rows(tokens, in_back)
    word_copy = pltpu.make_async_copy(total, grad_word, local_sems.at[3, 2])
    word_copy.start()
    links.send("core", low, words, word_sems.at[1])
    links.arrived("core", lookups.at[1], word_sems.at[0])
    sums.tick(chunks)
    links.arrived("core", words, word_sems.at[1])

    def slab_at(dp, half):
        start = (dp * 2 + half) * slab_rows
        return held.at[pl.ds(pl.multiple_of(start, 16), slab_rows)]

    def table_term(row_bit):
        def one(n, carry):
            dp = 2 * n + row_bit
            for i in range(2):
                rows = tuple(lookups[i, w : w + 1, :] for w in range(7))
                for h in range(2):
                    counts[i, h * slab_rows : (h + 1) * slab_rows, :] = row_counts(
                        rows, dp * 4 + h * 2 + core, owns, slab_rows, tokens
                    )
            start = pl.multiple_of(dp * 2 * slab_rows, 16)
            held[pl.ds(start, 2 * slab_rows)] = (
                product(counts[0], low[...]) + product(counts[1], words[...])
            ).astype(BF16)
            return carry

        lax.fori_loop(0, dps // 2, one, 0)

    split = width // 3
    lines = list(range(1, bits))
    by_row, by_line, by_half = (
        table_reduce(
            place, links, slab_at, pl.ds(i * split, split), order, landing.at[i], landing_sems.at[i]
        )
        for i, order in enumerate(([0, "half"] + lines, lines + ["half", 0], ["half", 0] + lines))
    )
    table_term(1 - place.bit(0))
    next(by_row)
    table_term(place.bit(0))
    next(by_line)
    next(by_half)

    def ticks():
        while sums.ticks < chunks + sums.stages() - 1:
            sums.tick(chunks)
            for _ in range(2):
                yield

    interleave(
        ticks(),
        by_row,
        by_line,
        by_half,
        seldom(vector_reduce(place, links, vector_terms, vector_land, vector_sems), 3),
    )
    table_sum[...] = slab_at(place.dp, place.half)[...]
    vector_sum[...] = vector_terms[bits + 2]
    word_copy.wait()
    links.finish()
    sums.finish(chunks)


def backward_all(devices, owns, slab_rows, weights, vectors, boxes, segments, offsets, kept):
    bits = (devices // 4).bit_length() - 1
    dps = 2**bits
    tokens, width = kept[0].shape
    anywhere = pl.BlockSpec(memory_space=pl.ANY)
    in_vmem = pl.BlockSpec(memory_space=pltpu.VMEM)
    fourth, part = width // 4, width // PARTS
    chunks = 3 * PARTS
    landing = sum(ladder(part, bits)[1:])
    held_rows = max(8 * width, 2 * dps * slab_rows)
    shape = jax.ShapeDtypeStruct
    return pl.pallas_call(
        functools.partial(backward_kernel, bits, owns, slab_rows),
        out_shape=[
            shape((tokens, width), F32),
            shape((chunks, part, width), BF16),
            shape((slab_rows, width), BF16),
            shape((16, width), F32),
        ],
        in_specs=[anywhere]
        + [in_vmem] * 6
        + [anywhere] * 2
        + [in_vmem]
        + [anywhere] * 2
        + [in_vmem]
        + [anywhere] * 2
        + [in_vmem]
        + [anywhere] * 2,
        out_specs=[anywhere] + [in_vmem] * 3,
        scratch_shapes=[
            pltpu.VMEM((held_rows, width), BF16),
            pltpu.VMEM((tokens, width), BF16),
            pltpu.VMEM((tokens, width), BF16),
            pltpu.VMEM((4, 3 * fourth, tokens), BF16),
            pltpu.VMEM((4, fourth, tokens), BF16),
            pltpu.VMEM((tokens, width), BF16),
            pltpu.VMEM((tokens, width), BF16),
            pltpu.VMEM((4, tokens, width), BF16),
            pltpu.VMEM((4, tokens, width), BF16),
            pltpu.VMEM((SLOTS, 2, part, width), BF16),
            pltpu.VMEM((chunks, 2, part, width), BF16),
            pltpu.VMEM((SLOTS, 2, part, width), BF16),
            pltpu.VMEM((chunks, part, width), BF16),
            pltpu.VMEM((chunks, landing, width), BF16),
            pltpu.VMEM((3, 2 * dps - 1, slab_rows, width // 3), BF16),
            pltpu.VMEM((tokens, width), BF16),
            pltpu.VMEM((2, 8, tokens), jnp.int32),
            pltpu.VMEM((bits + 3, 16, width), F32),
            pltpu.VMEM((bits + 2, 16, width), F32),
            pltpu.VMEM((tokens, width), F32),
            pltpu.VMEM((tokens, width), BF16),
            pltpu.VMEM((2, tokens // 2 + 128, tokens // 2), BF16),
            pltpu.VMEM((4, fourth, tokens), BF16),
            pltpu.VMEM((4, 3 * fourth, tokens), BF16),
            pltpu.VMEM((2, 2 * slab_rows, tokens), BF16),
            pltpu.SemaphoreType.DMA((6 * dps + 40,)),
            pltpu.SemaphoreType.DMA((2 + 2 * bits, chunks)),
            pltpu.SemaphoreType.DMA((2 + 2 * bits, chunks)),
            pltpu.SemaphoreType.DMA((3, 2 * dps - 1)),
            pltpu.SemaphoreType.DMA((bits + 2,)),
            pltpu.SemaphoreType.DMA((2,)),
            pltpu.SemaphoreType.DMA((4, 4)),
            pltpu.SemaphoreType.DMA((6,)),
            pltpu.SemaphoreType.REGULAR,
        ],
        name="backward_all",
        compiler_params=pltpu.CompilerParams(
            collective_id=1, has_side_effects=True, vmem_limit_bytes=60 * 2**20
        ),
    )(weights, vectors, boxes, segments, offsets, *kept)


def body(
    devices,
    word_vectors,
    position_table,
    horizontal_table,
    vertical_table,
    height_table,
    width_table,
    embed_gain,
    embed_shift,
    w_query,
    b_query,
    w_key,
    w_value,
    b_value,
    w_out,
    b_out,
    attn_gain,
    attn_shift,
    w_in,
    b_in,
    w_down,
    b_down,
    ffn_gain,
    ffn_shift,
    boxes,
    segments,
    offsets,
    cotangent,
):
    own_rows, width = word_vectors.shape
    t = lax.axis_index("tensor")
    owned = (position_table, horizontal_table, vertical_table, height_table, width_table)
    slab_rows = sum(table.shape[0] for table in owned)
    slab_padded = -(-slab_rows // 16) * 16
    slabs = owned
    if slab_padded > slab_rows or any(table.shape[0] % 16 for table in owned):
        slab = jnp.concatenate(owned, axis=0)
        slabs = (jnp.pad(slab, ((0, slab_padded - slab_rows), (0, 0))),)
    fourth = w_query.shape[0]
    bias_rows = jnp.concatenate([b_query, b_value, jnp.zeros((2 * fourth,), F32)])
    vectors = jnp.concatenate(
        [embed_gain, embed_shift, b_out, attn_gain, attn_shift, b_down, ffn_gain, ffn_shift]
        + [b_in, bias_rows, jnp.zeros((6 * width,), F32)]
    ).reshape(16, width)
    owns = tuple(table.shape[0] for table in owned)
    layer_out, grad_ffn_sum, ffn_vectors, weights, *kept = forward_all(
        devices,
        owns,
        slab_padded,
        slabs,
        (w_query, w_key, w_value, w_out, w_in, w_down),
        vectors,
        word_vectors,
        boxes,
        segments,
        offsets,
        cotangent,
    )
    grad_word, weight_sums, table_sum, vector_sum = backward_all(
        devices,
        owns,
        slab_padded,
        weights,
        vectors,
        boxes,
        segments,
        offsets,
        (grad_ffn_sum, ffn_vectors, *kept),
    )
    tall_sum, wide_sum, square_sum = weight_sums.astype(F32).reshape(3, width, width)
    table_sum = table_sum.astype(F32)
    first = [0]
    for own in owns:
        first.append(first[-1] + own)
    bias_in = lax.dynamic_slice_in_dim(vector_sum, 8 + t, 1)[0]
    bias_row = lax.dynamic_slice_in_dim(vector_sum, 12 + t, 1)[0]
    bias_query, bias_value = bias_row[:fourth], bias_row[2 * fourth : 3 * fourth]
    return (
        layer_out,
        grad_word,
        *(table_sum[first[k] : first[k + 1]] for k in range(5)),
        vector_sum[0],
        vector_sum[1],
        square_sum[:fourth],
        bias_query,
        square_sum[fourth : 2 * fourth],
        square_sum[2 * fourth : 3 * fourth],
        bias_value,
        square_sum[3 * fourth :],
        vector_sum[6],
        vector_sum[2],
        vector_sum[3],
        wide_sum,
        bias_in,
        tall_sum,
        vector_sum[7],
        vector_sum[4],
        vector_sum[5],
    )


def solution(mesh):
    devices = mesh.shape["dp"] * mesh.shape["tensor"]
    both = P(("dp", "tensor"), None)
    rows = P("tensor", None)
    return jax.shard_map(
        functools.partial(body, devices),
        mesh=mesh,
        in_specs=(
            *(both,) * 6,
            P(),
            P(),
            rows,
            P("tensor"),
            rows,
            rows,
            P("tensor"),
            rows,
            P(),
            P(),
            P(),
            P(None, "tensor"),
            P("tensor"),
            rows,
            P(),
            P(),
            P(),
            P(None, ("dp", "tensor")),
            P("dp", None),
            P("dp", None),
            both,
        ),
        out_specs=(
            *(both,) * 7,
            P(),
            P(),
            rows,
            P("tensor"),
            rows,
            rows,
            P("tensor"),
            rows,
            P(),
            P(),
            P(),
            P(None, "tensor"),
            P("tensor"),
            rows,
            P(),
            P(),
            P(),
        ),
        check_vma=False,
    )
```

```python
import functools

import jax
import jax.numpy as jnp
from jax import lax
from jax.experimental import pallas as pl
from jax.experimental.pallas import tpu as pltpu
from jax.sharding import PartitionSpec as P

HEAD = 64
MESH = pl.DeviceIdType.MESH
BF16 = jnp.bfloat16
F32 = jnp.float32

epsilon = 1e-06
masked_score = -1e30


class Place:
    def __init__(self, bits):
        self.bits = bits
        self.dp = lax.axis_index("dp")
        self.t = lax.axis_index("tensor")
        self.core = self.t % 2
        self.half = self.t // 2

    def bit(self, i):
        return (self.dp // 2**i) % 2

    def dp_flip(self, mask):
        dp = self.dp
        for i in range(self.bits):
            if mask & (1 << i):
                dp = dp + 2**i - 2 * 2**i * self.bit(i)
        return dp

    def t_flip(self, mask):
        t = self.t
        if mask & 1:
            t = t + 1 - 2 * self.core
        if mask & 2:
            t = t + 2 - 4 * self.half
        return t

    def partner(self, way):
        if way == "core":
            return (self.dp, self.t_flip(1))
        if way == "half":
            return (self.dp, self.t_flip(2))
        return (self.dp_flip(1 << way), self.t)

    def greet(self):
        barrier = pltpu.get_barrier_semaphore()
        ways = ["core", "half"] + list(range(self.bits))
        for way in ways:
            pl.semaphore_signal(
                barrier, inc=1, device_id=self.partner(way), device_id_type=MESH
            )
        pl.semaphore_wait(barrier, len(ways))


class Links:
    def __init__(self, place, send_sems):
        self.place = place
        self.send_sems = send_sems
        self.sent = []
        self.count = 0

    def send(self, way, src, dst, recv_sem):
        copy = pltpu.make_async_remote_copy(
            src_ref=src,
            dst_ref=dst,
            send_sem=self.send_sems.at[self.count],
            recv_sem=recv_sem,
            device_id=self.place.partner(way),
            device_id_type=MESH,
        )
        copy.start()
        self.count += 1
        self.sent.append(copy)
        return copy

    def arrived(self, way, dst, recv_sem):
        pltpu.make_async_remote_copy(
            src_ref=dst,
            dst_ref=dst,
            send_sem=recv_sem,
            recv_sem=recv_sem,
            device_id=self.place.partner(way),
            device_id_type=MESH,
        ).wait_recv()

    def finish(self):
        for copy in self.sent:
            copy.wait_send()


def seldom(steps, times):
    for _ in steps:
        for _ in range(times):
            yield


def interleave(*steps):
    live = list(steps)
    while live:
        for step in list(live):
            try:
                next(step)
            except StopIteration:
                live.remove(step)


def tables_gather(place, links, own, full, sems):
    bits = place.bits
    line_masks = [2 * k for k in range(2 ** (bits - 1))]
    line_sem, half_sem, row_sem, cross_sem, core_sem = sems

    def at(dp_mask, t_mask):
        return full.at[place.dp_flip(dp_mask) * 4 + place.t_flip(t_mask)]

    def to_core(slab, key):
        links.send("core", slab, slab, core_sem.at[key])

    def onward(mask, slab_source, below):
        for b in range(below - 1, 0, -1):
            links.send(b, slab_source, at(mask, 0), line_sem.at[(mask | (1 << b)) // 2])
        links.send("half", slab_source, at(mask, 0), half_sem.at[mask // 2])
        links.send(0, slab_source, at(mask, 0), row_sem.at[mask // 2])
        links.send("core", slab_source, at(mask, 0), core_sem.at[mask * 2])

    onward(0, own, bits)
    yield
    order = []
    held = [0]
    for b in range(bits - 1, 0, -1):
        fresh = [m | (1 << b) for m in held]
        for m in fresh:
            order.append((m, b))
        held = held + fresh
    for mask, b in order:
        links.arrived(b, at(mask, 0), line_sem.at[mask // 2])
        onward(mask, at(mask, 0), b)
        yield
    low = place.bit(1)
    for pair in range(len(line_masks) // 2):
        base = 4 * pair
        for mask in (base, base + 2):
            links.arrived("half", at(mask, 2), half_sem.at[mask // 2])
            to_core(at(mask, 2), mask * 2 + 1)
            links.arrived(0, at(mask + 1, 0), row_sem.at[mask // 2])
            to_core(at(mask + 1, 0), (mask + 1) * 2)
        yield
        dp_other = place.dp_flip(base)
        clear = dp_other - 2 * low
        here_clear = clear * 4 + place.t_flip(2)
        links.send(0, full.at[here_clear], full.at[here_clear], cross_sem.at[2 * pair + low])
        row_dp = place.dp_flip(base + 1)
        raised = row_dp + 2 * (1 - low)
        here_raised = raised * 4 + place.t
        links.send(
            "half", full.at[here_raised], full.at[here_raised], cross_sem.at[2 * pair + 1 - low]
        )
        yield
    def core_arrivals(row):
        for mask in line_masks:
            for t_mask in (0, 2):
                links.arrived(
                    "core",
                    at(mask + row, t_mask + 1),
                    core_sem.at[(mask + row) * 2 + t_mask // 2],
                )

    core_arrivals(0)
    yield "near"
    for pair in range(len(line_masks) // 2):
        base = 4 * pair
        dp_cross = place.dp_flip(base + 1)
        clear = (dp_cross - 2 * low) * 4 + place.t_flip(2)
        links.arrived(0, full.at[clear], cross_sem.at[2 * pair + low])
        links.send("core", full.at[clear], full.at[clear], core_sem.at[(base + 2 * low + 1) * 2 + 1])
        raised = (dp_cross + 2 * (1 - low)) * 4 + place.t_flip(2)
        links.arrived("half", full.at[raised], cross_sem.at[2 * pair + 1 - low])
        links.send(
            "core", full.at[raised], full.at[raised], core_sem.at[(base + 2 * (1 - low) + 1) * 2 + 1]
        )
        yield
    core_arrivals(1)
    yield


def added(left, right):
    return (left.astype(F32) + right.astype(F32)).astype(BF16)


def product(left, right):
    return jnp.dot(left, right, preferred_element_type=F32)


def inner_rows(left, right):
    return lax.dot_general(left, right, (((0,), (0,)), ((), ())), preferred_element_type=F32)


def against_rows(left, right):
    return lax.dot_general(left, right, (((1,), (1,)), ((), ())), preferred_element_type=F32)


CHUNKS = 2


def chunk_rows(place, weights, j, near_row, near_line):
    side = weights.shape[2] // 4
    rows = side // CHUNKS
    row = place.bit(0) if near_row else 1 - place.bit(0)
    line = place.bit(1) if near_line else 1 - place.bit(1)
    start = (2 * row + line) * side + (j % CHUNKS) * rows
    return j // CHUNKS, pl.ds(pl.multiple_of(start, rows), rows)


class Weights:
    def __init__(self, place, weights, send_sems, recv_sems, own_send, own_recv):
        self.place = place
        self.weights = weights
        self.send_sems = send_sems
        self.recv_sems = recv_sems
        self.own_send = own_send
        self.own_recv = own_recv

    def copy(self, way, lane, j, t, near_row=True, near_line=True):
        matrix, rows = chunk_rows(self.place, self.weights, j, near_row, near_line)
        block = self.weights.at[matrix, t, rows]
        return pltpu.make_async_remote_copy(
            src_ref=block,
            dst_ref=block,
            send_sem=self.send_sems.at[lane, j],
            recv_sem=self.recv_sems.at[lane, j],
            device_id=self.place.partner(way),
            device_id_type=MESH,
        )

    def own(self, i):
        block = self.weights.at[i, self.place.t]
        return pltpu.make_async_remote_copy(
            src_ref=block,
            dst_ref=block,
            send_sem=self.own_send.at[i],
            recv_sem=self.own_recv.at[i],
            device_id=self.place.partner("core"),
            device_id_type=MESH,
        )

    def own_arrived(self, i):
        block = self.weights.at[i, self.place.t_flip(1)]
        pltpu.make_async_remote_copy(
            src_ref=block,
            dst_ref=block,
            send_sem=self.own_send.at[i],
            recv_sem=self.own_recv.at[i],
            device_id=self.place.partner("core"),
            device_id_type=MESH,
        ).wait_recv()

    def issue(self, j):
        self.copy("half", 0, j, self.place.t).start()

    def take_half(self, j):
        other = self.place.t_flip(2)
        self.copy("half", 0, j, other).wait_recv()
        self.copy(0, 1, j, other).start()
        self.copy(1, 2, j, other).start()
        self.copy("core", 4, j, other).start()

    def take_row(self, j):
        other = self.place.t_flip(2)
        self.copy(0, 1, j, other, False).wait_recv()
        self.copy(1, 3, j, other, False).start()
        self.copy("core", 5, j, other, False).start()

    def take_line(self, j):
        other = self.place.t_flip(2)
        for lane, near_row in ((2, True), (3, False)):
            self.copy(1, lane, j, other, near_row, False).wait_recv()
            self.copy("core", lane + 4, j, other, near_row, False).start()

    def settle(self, j):
        cross = self.place.t_flip(3)
        for lane, near_row, near_line in self.core_lanes():
            self.copy("core", lane, j, cross, near_row, near_line).wait_recv()

    def core_lanes(self):
        return ((4, True, True), (5, False, True), (6, True, False), (7, False, False))

    def finish(self, count):
        for i in range(3):
            self.own(i).wait_send()

        def one(j, carry):
            other = self.place.t_flip(2)
            self.copy("half", 0, j, self.place.t).wait_send()
            self.copy(0, 1, j, other).wait_send()
            self.copy(1, 2, j, other).wait_send()
            self.copy(1, 3, j, other, False).wait_send()
            for lane, near_row, near_line in self.core_lanes():
                self.copy("core", lane, j, other, near_row, near_line).wait_send()
            return carry

        lax.fori_loop(0, count, one, 0)


def row_counts(lookup_rows, device, owns, slab_rows, tokens):
    by_table = ((0, (0,)), (1, (1, 3)), (2, (2, 4)), (3, (5,)), (4, (6,)))
    if all(own % 16 == 0 for own in owns):
        pieces = []
        for k, which in by_table:
            at = lax.broadcasted_iota(jnp.int32, (owns[k], tokens), 0) + device * owns[k]
            piece = sum(jnp.where(at == lookup_rows[w], 1.0, 0.0) for w in which)
            pieces.append(piece.astype(BF16))
        spare = slab_rows - sum(owns)
        if spare:
            pieces.append(jnp.zeros((spare, tokens), BF16))
        return jnp.concatenate(pieces, axis=0)
    at = lax.broadcasted_iota(jnp.int32, (slab_rows, tokens), 0)
    total = jnp.zeros((slab_rows, tokens), F32)
    first = 0
    for k, which in by_table:
        for w in which:
            local = lookup_rows[w] - device * owns[k]
            inside = (local >= 0) & (local < owns[k])
            total = total + jnp.where(at == jnp.where(inside, local + first, -1), 1.0, 0.0)
        first += owns[k]
    return total.astype(BF16)


def lookup_rows_of(boxes, segments, offsets, t):
    tokens = segments.shape[1]
    pages = offsets.shape[1]
    seg = segments[pl.ds(t, 1), :]
    label = lax.broadcasted_iota(jnp.int32, (pages, tokens), 0)
    place_in = lax.broadcasted_iota(jnp.int32, (pages, tokens), 1).astype(F32)
    member = label == seg
    starts = jnp.min(jnp.where(member, place_in, float(tokens)), axis=1, keepdims=True)
    shift_row = offsets[pl.ds(t, 1), :].astype(F32)
    eye = lax.broadcasted_iota(jnp.int32, (pages, pages), 0) == lax.broadcasted_iota(
        jnp.int32, (pages, pages), 1
    )
    shift = jnp.sum(jnp.where(eye, shift_row, 0.0), axis=1, keepdims=True)
    moved = jnp.sum(jnp.where(member, place_in - starts + shift, 0.0), axis=0, keepdims=True)
    positions = moved.astype(jnp.int32)
    x0, y0, x1, y1 = (boxes[i : i + 1, :] for i in range(4))
    return (positions, x0, y0, x1, y1, jnp.abs(y1 - y0), jnp.abs(x1 - x0)), seg


def norm_parts(values):
    width = values.shape[1]
    row_mean = jnp.sum(values, axis=1, keepdims=True) * (1.0 / width)
    row_var = jnp.sum(values * values, axis=1, keepdims=True) * (1.0 / width) - row_mean * row_mean
    scaled = lax.rsqrt(row_var + epsilon)
    return (values - row_mean) * scaled, scaled


ROWS = 64


def by_rows(count, step):
    def one(i, carry):
        step(pl.ds(pl.multiple_of(i * ROWS, ROWS), ROWS))
        return carry

    lax.fori_loop(0, count // ROWS, one, 0)


def head_blocks(tokens):
    half, reach = tokens // 2, 128
    return ((0, half, 0, half + reach), (half, half, half - reach, half + reach))


def mask_pages(segments_row, masks):
    tokens = segments_row.shape[1]
    rows = jnp.broadcast_to(segments_row.astype(F32), (8, tokens))
    columns = jnp.transpose(rows)
    for i, (q, nq, k, nk) in enumerate(head_blocks(tokens)):
        same = columns[k : k + nk, 0:1] == rows[0:1, q : q + nq]
        masks[i] = jnp.where(same, 0.0, masked_score).astype(masks.dtype)


def forward_kernel(
    bits,
    owns,
    slab_rows,
    pieces,
    *refs,
):
    slabs, refs = refs[:pieces], refs[pieces:]
    forward_body(bits, owns, slab_rows, slabs, *refs)


def forward_body(
    bits,
    owns,
    slab_rows,
    slabs,
    w_query,
    w_key,
    w_value,
    w_out,
    wide,
    tall,
    vectors,
    word,
    boxes,
    segments,
    offsets,
    cotangent,
    layer_out,
    grad_sum,
    grad_vectors,
    weights_out,
    inputs_low_out,
    centered_in_out,
    scaled_in,
    projected_out,
    mixed_out,
    stats,
    mid_low_out,
    centered_mid_out,
    scaled_mid,
    hidden_out,
    slopes_out,
    inputs_low,
    centered_in,
    projected,
    mixed,
    mid_low,
    centered_mid,
    hidden,
    slopes,
    tables,
    counts,
    weights,
    biases,
    normed,
    total,
    masks,
    send_sems,
    line_sem,
    half_sem,
    row_sem,
    cross_sem,
    core_sem,
    weight_send,
    weight_recv,
    own_send,
    own_recv,
    bias_sems,
    local_sems,
    own_sems,
    ship_sems,
):
    place = Place(bits)
    tokens, width = word.shape
    dps = 2**bits
    t = place.t
    me = place.dp * 4 + t
    local = copies_into(tables.at[me], slabs, own_sems.at[3])
    owned = [
        copies_into(weights.at[i, t], sources, own_sems.at[i])
        for i, sources in enumerate(((w_query, w_key, w_value, w_out), (wide,), (tall,)))
    ]
    for copy in local + owned[0] + owned[1] + owned[2]:
        copy.start()
    shipped = []

    def ship(source, target):
        copy = pltpu.make_async_copy(source, target, ship_sems.at[len(shipped)])
        copy.start()
        shipped.append(copy)

    place.greet()
    links = Links(place, send_sems)
    flow = Weights(place, weights, weight_send, weight_recv, own_send, own_recv)
    chunks = 3 * CHUNKS
    for copy in local:
        copy.wait()
    gather = tables_gather(
        place, links, tables.at[me], tables, (line_sem, half_sem, row_sem, cross_sem, core_sem)
    )
    next(gather)
    bias = vectors.at[pl.ds(8, 8)]
    biases[t] = vectors[8:16]
    links.send("core", bias, biases.at[t], bias_sems.at[0])
    links.send("half", bias, biases.at[t], bias_sems.at[1])
    for i, copies in enumerate(owned):
        for copy in copies:
            copy.wait()
        flow.own(i).start()
    flow.issue(0)
    flow.issue(1)

    lookup, seg = lookup_rows_of(boxes, segments, offsets, t)

    def count_dp(dp, carry):
        for j in range(4):
            counts[dp, j * slab_rows : (j + 1) * slab_rows, :] = row_counts(
                lookup, dp * 4 + j, owns, slab_rows, tokens
            )
        return carry

    lax.fori_loop(0, dps, count_dp, 0)
    mask_pages(seg, masks)
    total[...] = word[...].astype(F32)
    def embed(row_bit):
        def one(i, carry):
            dp = 2 * i + row_bit
            rows = tables[pl.ds(dp * 4, 4)].reshape(4 * slab_rows, width)
            total[...] += inner_rows(counts[dp], rows)
            return carry

        lax.fori_loop(0, dps // 2, one, 0)

    for step in gather:
        if step == "near":
            break
    links.arrived("half", biases.at[place.t_flip(2)], bias_sems.at[1])
    links.send("core", biases.at[place.t_flip(2)], biases.at[place.t_flip(2)], bias_sems.at[2])
    flow.take_half(0)
    flow.issue(2)
    embed(place.bit(0))
    flow.take_half(1)
    flow.issue(3)
    flow.take_row(0)
    for step in gather:
        pass
    flow.take_row(1)
    flow.take_line(0)
    embed(1 - place.bit(0))
    flow.take_half(2)
    flow.issue(4)
    flow.take_line(1)

    def norm_in(rows):
        centered, scaled = norm_parts(total[rows])
        centered_in[rows] = centered.astype(BF16)
        scaled_in[rows] = scaled
        result = centered * vectors[0:1] + vectors[1:2]
        normed[rows] = result
        inputs_low[rows] = result.astype(BF16)

    by_rows(tokens, norm_in)
    ship(inputs_low, inputs_low_out)
    ship(centered_in, centered_in_out)
    flow.take_half(3)
    flow.issue(5)
    flow.take_row(2)
    links.arrived("core", biases.at[place.t_flip(1)], bias_sems.at[0])
    links.arrived("core", biases.at[place.t_flip(3)], bias_sems.at[2])
    flow.own_arrived(0)
    flow.settle(0)
    flow.settle(1)
    fourth = width // 4

    def project(j, carry):
        columns = jnp.transpose(biases[j])
        zeros = jnp.zeros((fourth, 1), F32)
        column = jnp.concatenate(
            [columns[0:fourth, 1:2], zeros, columns[fourth : 2 * fourth, 1:2]], axis=0
        )
        projected[j] = (
            against_rows(weights[0, j, : 3 * fourth, :], inputs_low[...]) + column
        ).astype(BF16)
        return carry

    lax.fori_loop(0, 4, project, 0)
    ship(projected, projected_out)
    flow.take_half(4)
    flow.take_row(3)

    def attend(j, carry):
        for h in range(fourth // HEAD):
            rows = slice(h * HEAD, (h + 1) * HEAD)
            key_rows = slice(fourth + h * HEAD, fourth + (h + 1) * HEAD)
            value_rows = slice(2 * fourth + h * HEAD, 2 * fourth + (h + 1) * HEAD)
            for i, (q, nq, k, nk) in enumerate(head_blocks(tokens)):
                scores = (
                    inner_rows(
                        projected[j, key_rows, k : k + nk], projected[j, rows, q : q + nq]
                    )
                    * HEAD ** (-0.5)
                    + masks[i]
                )
                peak = jnp.max(scores, axis=0, keepdims=True)
                exponent = jnp.exp(scores - peak)
                all_of = jnp.sum(exponent, axis=0, keepdims=True)
                stats[j, h : h + 1, q : q + nq] = peak + jnp.log(all_of)
                share = (exponent * (1.0 / all_of)).astype(BF16)
                mixed[j, rows, q : q + nq] = product(
                    projected[j, value_rows, k : k + nk], share
                ).astype(BF16)
        return carry

    def attend_and_pass(j, carry):
        attend(j, carry)

        @pl.when(j < 1)
        def _():
            flow.take_half(5)

        @pl.when(j < 2)
        def _():
            flow.take_row(j + 4)

        @pl.when(j < 3)
        def _():
            flow.take_line(j + 2)

        return carry

    lax.fori_loop(0, 4, attend_and_pass, 0)
    ship(mixed, mixed_out)
    out_rows = weights[0, :, 3 * fourth :, :].reshape(width, width)
    total[...] = inner_rows(mixed[...].reshape(width, tokens), out_rows)
    flow.take_line(5)

    def norm_mid(rows):
        centered, scaled = norm_parts(total[rows] + vectors[2:3] + normed[rows])
        centered_mid[rows] = centered.astype(BF16)
        scaled_mid[rows] = scaled
        result = centered * vectors[3:4] + vectors[4:5]
        normed[rows] = result
        mid_low[rows] = result.astype(BF16)

    by_rows(tokens, norm_mid)
    ship(mid_low, mid_low_out)
    ship(centered_mid, centered_mid_out)
    total[...] = jnp.zeros_like(total)
    columns = 256

    def feed_copies(j):
        return [
            pltpu.make_async_copy(source.at[j], target.at[j], local_sems.at[1 + i, j])
            for i, (source, target) in enumerate(((hidden, hidden_out), (slopes, slopes_out)))
        ]

    def feed(j):
        def one(n, carry):
            at = pl.ds(pl.multiple_of(n * columns, columns), columns)
            before = product(mid_low[...], weights[1, j, :, at]) + biases[j, 0:1, at]
            share = 0.5 * (1.0 + lax.erf(before * 0.5**0.5))
            hidden[j, :, at] = (before * share).astype(BF16)
            density = jnp.exp(before * before * -0.5) * 0.3989422804014327
            slopes[j, :, at] = (share + before * density).astype(BF16)
            return carry

        lax.fori_loop(0, width // columns, one, 0)
        total[...] += product(hidden[j], weights[2, j])
        for copy in feed_copies(j):
            copy.start()

    flow.own_arrived(1)
    flow.own_arrived(2)

    def feed_near(i, carry):
        feed(t + i * (1 - 2 * place.core))
        return carry

    lax.fori_loop(0, 2, feed_near, 0)
    for j in range(CHUNKS, chunks):
        flow.settle(j)
    out_copy = pltpu.make_async_copy(weights, weights_out, local_sems.at[0, 0])
    out_copy.start()

    def feed_far(i, carry):
        feed(place.t_flip(2) + i * (1 - 2 * place.core))
        return carry

    lax.fori_loop(0, 2, feed_far, 0)
    grad_vectors[...] = jnp.zeros_like(grad_vectors)

    def norm_out(rows):
        centered, scaled = norm_parts(total[rows] + vectors[5:6] + normed[rows])
        layer_out[rows] = centered * vectors[6:7] + vectors[7:8]
        grad = cotangent[rows]
        grad_sum[rows] = norm_back(grad, centered, scaled, vectors[6:7])
        grad_vectors[0:1] += jnp.sum(grad * centered, axis=0, keepdims=True)
        grad_vectors[1:2] += jnp.sum(grad, axis=0, keepdims=True)
        grad_vectors[2:3] += jnp.sum(grad_sum[rows], axis=0, keepdims=True)

    by_rows(tokens, norm_out)
    out_copy.wait()
    for copy in shipped:
        copy.wait()
    for j in range(4):
        for copy in feed_copies(j):
            copy.wait()
    links.finish()
    flow.finish(chunks)


def norm_back(grad_out, centered, scaled, norm_gain):
    width = grad_out.shape[1]
    grad_centered = grad_out * norm_gain
    first_mean = jnp.sum(grad_centered, axis=1, keepdims=True) * (1.0 / width)
    second_mean = jnp.sum(grad_centered * centered, axis=1, keepdims=True) * (1.0 / width)
    return scaled * (grad_centered - first_mean - centered * second_mean)


def copies_into(target, sources, sems):
    first, copies = 0, []
    for i, source in enumerate(sources):
        rows = source.shape[0]
        copies.append(
            pltpu.make_async_copy(source, target.at[pl.ds(first, rows)], sems.at[i])
        )
        first += rows
    return copies


def forward_all(
    devices, owns, slab_rows, slabs, matrices, vectors, word, boxes, segments, offsets, cotangent
):
    bits = (devices // 4).bit_length() - 1
    dps = 2**bits
    lines = 2 ** (bits - 1)
    tokens, width = word.shape
    anywhere = pl.BlockSpec(memory_space=pl.ANY)
    in_vmem = pl.BlockSpec(memory_space=pltpu.VMEM)
    fourth = width // 4
    shape = jax.ShapeDtypeStruct
    return pl.pallas_call(
        functools.partial(forward_kernel, bits, owns, slab_rows, len(slabs)),
        out_shape=[
            shape((tokens, width), F32),
            shape((tokens, width), F32),
            shape((8, width), F32),
            shape((3, 4, width, width), BF16),
            shape((tokens, width), BF16),
            shape((tokens, width), BF16),
            shape((tokens, 1), F32),
            shape((4, 3 * fourth, tokens), BF16),
            shape((4, fourth, tokens), BF16),
            shape((4, 8, tokens), F32),
            shape((tokens, width), BF16),
            shape((tokens, width), BF16),
            shape((tokens, 1), F32),
            shape((4, tokens, width), BF16),
            shape((4, tokens, width), BF16),
        ],
        in_specs=[anywhere] * (len(slabs) + len(matrices)) + [in_vmem] * 6,
        out_specs=[in_vmem] * 3
        + [anywhere] * 3
        + [in_vmem]
        + [anywhere] * 2
        + [in_vmem]
        + [anywhere] * 2
        + [in_vmem]
        + [anywhere] * 2,
        scratch_shapes=[
            pltpu.VMEM((tokens, width), BF16),
            pltpu.VMEM((tokens, width), BF16),
            pltpu.VMEM((4, 3 * fourth, tokens), BF16),
            pltpu.VMEM((4, fourth, tokens), BF16),
            pltpu.VMEM((tokens, width), BF16),
            pltpu.VMEM((tokens, width), BF16),
            pltpu.VMEM((4, tokens, width), BF16),
            pltpu.VMEM((4, tokens, width), BF16),
            pltpu.VMEM((devices, slab_rows, width), BF16),
            pltpu.VMEM((dps, 4 * slab_rows, tokens), BF16),
            pltpu.VMEM((3, 4, width, width), BF16),
            pltpu.VMEM((4, 8, width), F32),
            pltpu.VMEM((tokens, width), F32),
            pltpu.VMEM((tokens, width), F32),
            pltpu.VMEM((2, tokens // 2 + 128, tokens // 2), F32),
            pltpu.SemaphoreType.DMA((10 * lines + 40 + lines * bits,)),
            pltpu.SemaphoreType.DMA((lines,)),
            pltpu.SemaphoreType.DMA((lines,)),
            pltpu.SemaphoreType.DMA((lines,)),
            pltpu.SemaphoreType.DMA((lines,)),
            pltpu.SemaphoreType.DMA((4 * lines,)),
            pltpu.SemaphoreType.DMA((8, 3 * CHUNKS)),
            pltpu.SemaphoreType.DMA((8, 3 * CHUNKS)),
            pltpu.SemaphoreType.DMA((3,)),
            pltpu.SemaphoreType.DMA((3,)),
            pltpu.SemaphoreType.DMA((3,)),
            pltpu.SemaphoreType.DMA((3, 4)),
            pltpu.SemaphoreType.DMA((4, max(4, len(slabs)))),
            pltpu.SemaphoreType.DMA((6,)),
        ],
        name="forward_all",
        compiler_params=pltpu.CompilerParams(
            collective_id=0, has_side_effects=True, vmem_limit_bytes=60 * 2**20
        ),
    )(*slabs, *matrices, vectors, word, boxes, segments, offsets, cotangent)


def ladder(rows, bits):
    left = [rows]
    for b in range(bits):
        halves = left[-1] % 32 == 0 and b < bits - 1
        left.append(left[-1] // 2 if halves else left[-1])
    return left


SLOTS = 3
DEPTH = 2
PARTS = 3


class Sums:
    def __init__(self, place, outgoing, own, from_core, from_half, from_dp, total, sems, credit):
        self.place = place
        self.outgoing = outgoing
        self.own = own
        self.from_core = from_core
        self.from_half = from_half
        self.from_dp = from_dp
        self.total = total
        self.send_sems, self.recv_sems = sems
        self.credit = credit
        self.rows = own.shape[2]
        self.left = ladder(self.rows, place.bits)
        self.back = [b for b in range(place.bits) if self.left[b + 1] < self.left[b]]
        self.taken = 0
        self.issued = 0
        self.ticks = 0

    def copy(self, way, lane, j, src, dst):
        return pltpu.make_async_remote_copy(
            src_ref=src,
            dst_ref=dst,
            send_sem=self.send_sems.at[lane, j],
            recv_sem=self.recv_sems.at[lane, j],
            device_id=self.place.partner(way),
            device_id_type=MESH,
        )

    def start_of(self, level):
        start = 0
        for b in range(level):
            if self.left[b + 1] < self.left[b]:
                start = start + self.place.bit(b) * self.left[b + 1]
        return start

    def span(self, b, near):
        start, rows = self.start_of(b), self.left[b + 1]
        if rows < self.left[b]:
            bit = self.place.bit(b)
            start = start + (bit if near else 1 - bit) * rows
        return pl.ds(pl.multiple_of(start, 16), rows) if b or rows < self.left[0] else pl.ds(0, rows)

    def landing(self, b, j):
        first = sum(self.left[1 : b + 1])
        return self.from_dp.at[j, pl.ds(first, self.left[b + 1])]

    def core(self, j):
        slot = j % SLOTS
        return self.copy("core", 0, j, self.outgoing.at[slot], self.from_core.at[slot])

    def half(self, j):
        return self.copy("half", 1, j, self.own.at[j, 1], self.from_half.at[j])

    def dp(self, b, j):
        return self.copy(
            b, 2 + b, j, self.own.at[j, 0, self.span(b, False)], self.landing(b, j)
        )

    def gather(self, b, j, near=True):
        block = self.total.at[j, self.span(b, near)]
        return self.copy(b, 2 + self.place.bits + b, j, block, block)

    def launch(self, j):
        if j >= SLOTS:
            pl.semaphore_wait(self.credit, 1)
        self.core(j).start()

    def take_core(self, j, count):
        slot = j % SLOTS
        self.core(j).wait_recv()
        for which in (1, 0):
            self.own[j, which] = added(self.own[j, which], self.from_core[slot, which])
        if j + SLOTS < count:
            pl.semaphore_signal(
                self.credit, inc=1, device_id=self.place.partner("core"), device_id_type=MESH
            )
        self.taken = j + 1
        self.pump()

    def pump(self):
        while self.issued < min(self.taken, self.ticks + DEPTH):
            self.half(self.issued).start()
            self.issued += 1

    def tick(self, count):
        k = self.ticks
        self.ticks += 1
        for s in range(self.stages()):
            if 0 <= k - s < count:
                self.stage(s, k - s)

    def take_half(self, j):
        self.half(j).wait_recv()
        self.pump()
        span = self.span(0, False)
        self.own[j, 0, span] = added(self.own[j, 0, span], self.from_half[j, span])
        self.dp(0, j).start()
        if self.left[1] < self.left[0]:
            span = self.span(0, True)
            self.own[j, 0, span] = added(self.own[j, 0, span], self.from_half[j, span])

    def take_dp(self, b, j):
        self.dp(b, j).wait_recv()
        span, first = self.span(b, True), sum(self.left[1 : b + 1])
        arrived = self.from_dp[j, pl.ds(first, self.left[b + 1])]
        if b == self.place.bits - 1:
            self.total[j, span] = added(self.own[j, 0, span], arrived)
            if self.back:
                self.gather(self.back[-1], j).start()
            return
        if self.left[b + 1] == self.left[b]:
            self.dp(b, j).wait_send()
        self.own[j, 0, span] = added(self.own[j, 0, span], arrived)
        self.dp(b + 1, j).start()

    def take_back(self, i, j):
        order = self.back[::-1]
        self.gather(order[i], j, False).wait_recv()
        if i + 1 < len(order):
            self.gather(order[i + 1], j).start()

    def stages(self):
        return 1 + self.place.bits + len(self.back)

    def stage(self, s, j):
        if s == 0:
            self.take_half(j)
        elif s <= self.place.bits:
            self.take_dp(s - 1, j)
        else:
            self.take_back(s - 1 - self.place.bits, j)

    def finish(self, count):
        for j in range(max(0, count - SLOTS), count):
            self.core(j).wait_send()

        def one(j, carry):
            self.half(j).wait_send()
            for b in range(self.place.bits):
                if self.left[b + 1] < self.left[b] or b == self.place.bits - 1:
                    self.dp(b, j).wait_send()
            for b in self.back:
                self.gather(b, j).wait_send()
            return carry

        lax.fori_loop(0, count, one, 0)


def table_reduce(place, links, slab_at, columns, order, landing, sems):
    bits = place.bits
    flags = [1 << (bits if way == "half" else way) for way in order]

    def slab(mask):
        half = 1 - place.half if mask >> bits else place.half
        return slab_at(place.dp_flip(mask % (1 << bits)), half).at[:, columns]

    def first(mask):
        for i, flag in enumerate(flags):
            if mask & flag:
                return i
        return len(flags)

    every = sorted(range(2 ** (bits + 1)), key=lambda m: (first(m), m))
    slots = {}
    for i in range(len(flags)):
        for mask in every:
            if first(mask) > i:
                slots[i, mask] = len(slots)

    def send(i, mask):
        slot = slots[i, mask ^ flags[i]]
        links.send(order[i], slab(mask), landing.at[slot], sems.at[slot])

    for mask in sorted(
        (m for m in every if first(m) == 0), key=lambda m: (first(m ^ flags[0]), m)
    ):
        send(0, mask)
    yield
    for i in range(len(flags)):
        for mask in every:
            if first(mask) > i:
                slot = slots[i, mask]
                links.arrived(order[i], landing.at[slot], sems.at[slot])
                target = slab(mask)
                target[...] = added(target[...], landing[slot])
                if first(mask) == i + 1 < len(flags):
                    send(i + 1, mask)
                yield


def vector_reduce(place, links, vectors, landing, sems):
    for i, way in enumerate(["core", "half"] + list(range(place.bits))):
        links.send(way, vectors.at[i], landing.at[i], sems.at[i])
        yield
        links.arrived(way, landing.at[i], sems.at[i])
        vectors[i + 1] = vectors[i] + landing[i]


def backward_kernel(
    bits,
    owns,
    slab_rows,
    weights_in,
    vectors,
    boxes,
    segments,
    offsets,
    grad_sum,
    ffn_vectors,
    inputs_low_in,
    centered_in_in,
    scaled_in,
    projected_in,
    mixed_in,
    stats,
    mid_low_in,
    centered_mid_in,
    scaled_mid,
    hidden_in,
    slopes_in,
    grad_word,
    weight_sums,
    table_sum,
    vector_sum,
    held,
    inputs_low,
    centered_in,
    projected,
    mixed,
    mid_low,
    centered_mid,
    hidden,
    slopes,
    outgoing,
    own,
    from_core,
    from_half,
    from_dp,
    landing,
    words,
    lookups,
    vector_terms,
    vector_land,
    total,
    low,
    masks,
    grad_heads,
    grad_projected,
    counts,
    send_sems,
    sum_send,
    sum_recv,
    landing_sems,
    vector_sems,
    word_sems,
    local_sems,
    later_sems,
    credit,
):
    place = Place(bits)
    tokens, width = grad_sum.shape
    dps = 2**bits
    t, core = place.t, place.core
    fourth = width // 4
    part = width // PARTS
    quarter_rows = width
    loads = {}
    for i, (matrix, slot) in enumerate(((2, 0), (1, 1), (0, 0))):
        loads[matrix] = [
            pltpu.make_async_copy(
                weights_in.at[matrix, q],
                held.at[pl.ds((slot * 4 + q) * quarter_rows, quarter_rows)],
                local_sems.at[matrix, q],
            )
            for q in range(4)
        ]
    early = [
        pltpu.make_async_copy(hidden_in, hidden, local_sems.at[3, 0]),
        pltpu.make_async_copy(slopes_in, slopes, local_sems.at[3, 1]),
    ]
    later = [
        pltpu.make_async_copy(source, target, later_sems.at[i])
        for i, (source, target) in enumerate(
            (
                (mid_low_in, mid_low),
                (centered_mid_in, centered_mid),
                (projected_in, projected),
                (mixed_in, mixed),
                (inputs_low_in, inputs_low),
                (centered_in_in, centered_in),
            )
        )
    ]
    for copy in loads[2] + early + loads[1] + later:
        copy.start()
    place.greet()
    links = Links(place, send_sems)
    sums = Sums(
        place, outgoing, own, from_core, from_half, from_dp, weight_sums, (sum_send, sum_recv), credit
    )
    chunks = 3 * PARTS

    def quarter(parity, other):
        q = t + other * (2 - 4 * place.half)
        return q + 1 - 2 * core if parity else q

    def held_rows(slot, q, first=0, rows=width):
        start = (slot * 4 + q) * quarter_rows + first
        return held[pl.ds(pl.multiple_of(start, 16), rows)]

    lookup, seg = lookup_rows_of(boxes, segments, offsets, t)
    mask_pages(seg, masks)
    lookups[0] = jnp.concatenate(list(lookup) + [lookup[0]], axis=0)
    links.send("core", lookups.at[0], lookups.at[1], word_sems.at[0])

    def start_rows(rows):
        low[rows] = grad_sum[rows].astype(BF16)

    by_rows(tokens, start_rows)
    vector_terms[0] = jnp.zeros_like(vector_terms[0])
    vector_terms[0, 4:6] = ffn_vectors[0:2]
    vector_terms[0, 7:8] = ffn_vectors[2:3]
    for copy in loads[2] + early:
        copy.wait()

    def chunk(j, term):
        slot = j % SLOTS
        if j >= SLOTS:
            sums.core(j - SLOTS).wait_send()

        def out(i, carry):
            outgoing[slot, i] = term(quarter(1, i)).astype(BF16)
            return carry

        def keep(i, carry):
            own[j, i] = term(quarter(0, i)).astype(BF16)
            return carry

        lax.fori_loop(0, 2, out, 0)
        sums.launch(j)
        lax.fori_loop(0, 2, keep, 0)

    def down_term(part_at, q):
        at = pl.ds(part_at * part, part)
        back = against_rows(low[...], held_rows(0, q, part_at * part, part))
        before = (back * slopes[q, :, at].astype(F32)).astype(BF16)
        slopes[q, :, at] = before
        vector_terms[0, pl.ds(8 + q, 1), at] = jnp.sum(
            before.astype(F32), axis=0, keepdims=True
        )
        return inner_rows(hidden[q, :, at], low[...])

    for p in range(PARTS):
        chunk(p, functools.partial(down_term, p))
        if p:
            sums.take_core(p - 1, chunks)
    for copy in loads[0]:
        copy.start()
    sums.take_core(PARTS - 1, chunks)
    for copy in loads[1] + later:
        copy.wait()
    for p in range(PARTS):
        columns = slice(p * part, (p + 1) * part)
        chunk(PARTS + p, lambda q: inner_rows(mid_low[:, columns], slopes[q]))
        if p:
            sums.take_core(PARTS + p - 1, chunks)
        if p == PARTS - 1:
            sums.tick(chunks)
    total[...] = grad_sum[...]

    def mid_term(q, carry):
        total[...] += against_rows(slopes[q], held_rows(1, q))
        return carry

    lax.fori_loop(0, 4, mid_term, 0)
    sums.take_core(2 * PARTS - 1, chunks)

    def mid_back(rows):
        centered = centered_mid[rows].astype(F32)
        grad = total[rows]
        result = norm_back(grad, centered, scaled_mid[rows], vectors[3:4])
        vector_terms[0, 2:3] += jnp.sum(grad * centered, axis=0, keepdims=True)
        vector_terms[0, 3:4] += jnp.sum(grad, axis=0, keepdims=True)
        vector_terms[0, 6:7] += jnp.sum(result, axis=0, keepdims=True)
        total[rows] = result
        low[rows] = result.astype(BF16)

    by_rows(tokens, mid_back)
    for copy in loads[0]:
        copy.wait()

    def out_back(q, carry):
        grad_heads[q] = against_rows(held_rows(0, q, 3 * fourth, fourth), low[...]).astype(BF16)
        return carry

    lax.fori_loop(0, 4, out_back, 0)
    sums.tick(chunks)
    scale = HEAD ** (-0.5)

    def attend_back(j, carry):
        for h in range(fourth // HEAD):
            rows = slice(h * HEAD, (h + 1) * HEAD)
            key_rows = slice(fourth + h * HEAD, fourth + (h + 1) * HEAD)
            value_rows = slice(2 * fourth + h * HEAD, 2 * fourth + (h + 1) * HEAD)
            grads = []
            for i, (q, nq, k, nk) in enumerate(head_blocks(tokens)):
                queries = projected[j, rows, q : q + nq]
                keys = projected[j, key_rows, k : k + nk]
                values = projected[j, value_rows, k : k + nk]
                grad = grad_heads[j, rows, q : q + nq]
                scores = inner_rows(keys, queries) * scale + masks[i].astype(F32)
                share = jnp.exp(scores - stats[j, h : h + 1, q : q + nq])
                back = inner_rows(values, grad)
                inner = jnp.sum(share * back, axis=0, keepdims=True)
                grad_scores = (share * (back - inner)).astype(BF16)
                grad_projected[j, rows, q : q + nq] = (product(keys, grad_scores) * scale).astype(BF16)
                grads.append(
                    (
                        against_rows(queries, grad_scores) * scale,
                        against_rows(grad, share.astype(BF16)),
                    )
                )
            reach = 128
            for target, (first, second) in zip((key_rows, value_rows), zip(*grads)):
                edge = tokens // 2 - reach
                joined = jnp.concatenate(
                    [
                        first[:, :edge],
                        first[:, edge:] + second[:, : 2 * reach],
                        second[:, 2 * reach :],
                    ],
                    axis=1,
                )
                grad_projected[j, target, :] = joined.astype(BF16)
        ones = jnp.ones((8, tokens), BF16)
        vector_terms[0, pl.ds(12 + j, 1), 0 : 3 * fourth] = against_rows(ones, grad_projected[j])[0:1]
        return carry

    for j in (0, 2):
        lax.fori_loop(j, j + 2, attend_back, 0)
        sums.tick(chunks)

    def square_term(p, q):
        if p < PARTS - 1:
            return product(grad_projected[q, p * part : (p + 1) * part, :], inputs_low[...])
        return jnp.concatenate(
            [
                product(grad_projected[q, p * part :, :], inputs_low[...]),
                product(mixed[q], low[...]),
            ],
            axis=0,
        )

    for p in range(PARTS):
        chunk(2 * PARTS + p, functools.partial(square_term, p))

    def in_term(q, carry):
        total[...] += inner_rows(grad_projected[q], held_rows(0, q, 0, 3 * fourth))
        return carry

    lax.fori_loop(0, 4, in_term, 0)
    for p in range(PARTS):
        sums.take_core(2 * PARTS + p, chunks)

    def in_back(rows):
        centered = centered_in[rows].astype(F32)
        grad = total[rows]
        result = norm_back(grad, centered, scaled_in[rows], vectors[0:1])
        vector_terms[0, 0:1] += jnp.sum(grad * centered, axis=0, keepdims=True)
        vector_terms[0, 1:2] += jnp.sum(grad, axis=0, keepdims=True)
        total[rows] = result
        low[rows] = result.astype(BF16)

    by_rows(tokens, in_back)
    word_copy = pltpu.make_async_copy(total, grad_word, local_sems.at[3, 2])
    word_copy.start()
    links.send("core", low, words, word_sems.at[1])
    links.arrived("core", lookups.at[1], word_sems.at[0])
    sums.tick(chunks)
    links.arrived("core", words, word_sems.at[1])

    def slab_at(dp, half):
        start = (dp * 2 + half) * slab_rows
        return held.at[pl.ds(pl.multiple_of(start, 16), slab_rows)]

    def table_term(row_bit):
        def one(n, carry):
            dp = 2 * n + row_bit
            for i in range(2):
                rows = tuple(lookups[i, w : w + 1, :] for w in range(7))
                for h in range(2):
                    counts[i, h * slab_rows : (h + 1) * slab_rows, :] = row_counts(
                        rows, dp * 4 + h * 2 + core, owns, slab_rows, tokens
                    )
            start = pl.multiple_of(dp * 2 * slab_rows, 16)
            held[pl.ds(start, 2 * slab_rows)] = (
                product(counts[0], low[...]) + product(counts[1], words[...])
            ).astype(BF16)
            return carry

        lax.fori_loop(0, dps // 2, one, 0)

    split = width // 3
    lines = list(range(1, bits))
    by_row, by_line, by_half = (
        table_reduce(
            place, links, slab_at, pl.ds(i * split, split), order, landing.at[i], landing_sems.at[i]
        )
        for i, order in enumerate(([0, "half"] + lines, lines + ["half", 0], ["half", 0] + lines))
    )
    table_term(1 - place.bit(0))
    next(by_row)
    table_term(place.bit(0))
    next(by_line)
    next(by_half)

    def ticks():
        while sums.ticks < chunks + sums.stages() - 1:
            sums.tick(chunks)
            for _ in range(2):
                yield

    interleave(
        ticks(),
        by_row,
        by_line,
        by_half,
        seldom(vector_reduce(place, links, vector_terms, vector_land, vector_sems), 3),
    )
    table_sum[...] = slab_at(place.dp, place.half)[...]
    vector_sum[0:16] = vector_terms[bits + 2]
    vector_sum[16:17] = vector_terms[bits + 2, pl.ds(8 + t, 1)]
    vector_sum[17:18] = vector_terms[bits + 2, pl.ds(12 + t, 1)]
    vector_sum[18:24] = jnp.zeros((6, width), F32)
    word_copy.wait()
    links.finish()
    sums.finish(chunks)


def backward_all(devices, owns, slab_rows, weights, vectors, boxes, segments, offsets, kept):
    bits = (devices // 4).bit_length() - 1
    dps = 2**bits
    tokens, width = kept[0].shape
    anywhere = pl.BlockSpec(memory_space=pl.ANY)
    in_vmem = pl.BlockSpec(memory_space=pltpu.VMEM)
    fourth, part = width // 4, width // PARTS
    chunks = 3 * PARTS
    landing = sum(ladder(part, bits)[1:])
    held_rows = max(8 * width, 2 * dps * slab_rows)
    shape = jax.ShapeDtypeStruct
    return pl.pallas_call(
        functools.partial(backward_kernel, bits, owns, slab_rows),
        out_shape=[
            shape((tokens, width), F32),
            shape((chunks, part, width), BF16),
            shape((slab_rows, width), BF16),
            shape((24, width), F32),
        ],
        in_specs=[anywhere]
        + [in_vmem] * 6
        + [anywhere] * 2
        + [in_vmem]
        + [anywhere] * 2
        + [in_vmem]
        + [anywhere] * 2
        + [in_vmem]
        + [anywhere] * 2,
        out_specs=[anywhere] + [in_vmem] * 3,
        scratch_shapes=[
            pltpu.VMEM((held_rows, width), BF16),
            pltpu.VMEM((tokens, width), BF16),
            pltpu.VMEM((tokens, width), BF16),
            pltpu.VMEM((4, 3 * fourth, tokens), BF16),
            pltpu.VMEM((4, fourth, tokens), BF16),
            pltpu.VMEM((tokens, width), BF16),
            pltpu.VMEM((tokens, width), BF16),
            pltpu.VMEM((4, tokens, width), BF16),
            pltpu.VMEM((4, tokens, width), BF16),
            pltpu.VMEM((SLOTS, 2, part, width), BF16),
            pltpu.VMEM((chunks, 2, part, width), BF16),
            pltpu.VMEM((SLOTS, 2, part, width), BF16),
            pltpu.VMEM((chunks, part, width), BF16),
            pltpu.VMEM((chunks, landing, width), BF16),
            pltpu.VMEM((3, 2 * dps - 1, slab_rows, width // 3), BF16),
            pltpu.VMEM((tokens, width), BF16),
            pltpu.VMEM((2, 8, tokens), jnp.int32),
            pltpu.VMEM((bits + 3, 16, width), F32),
            pltpu.VMEM((bits + 2, 16, width), F32),
            pltpu.VMEM((tokens, width), F32),
            pltpu.VMEM((tokens, width), BF16),
            pltpu.VMEM((2, tokens // 2 + 128, tokens // 2), BF16),
            pltpu.VMEM((4, fourth, tokens), BF16),
            pltpu.VMEM((4, 3 * fourth, tokens), BF16),
            pltpu.VMEM((2, 2 * slab_rows, tokens), BF16),
            pltpu.SemaphoreType.DMA((6 * dps + 40,)),
            pltpu.SemaphoreType.DMA((2 + 2 * bits, chunks)),
            pltpu.SemaphoreType.DMA((2 + 2 * bits, chunks)),
            pltpu.SemaphoreType.DMA((3, 2 * dps - 1)),
            pltpu.SemaphoreType.DMA((bits + 2,)),
            pltpu.SemaphoreType.DMA((2,)),
            pltpu.SemaphoreType.DMA((4, 4)),
            pltpu.SemaphoreType.DMA((6,)),
            pltpu.SemaphoreType.REGULAR,
        ],
        name="backward_all",
        compiler_params=pltpu.CompilerParams(
            collective_id=1, has_side_effects=True, vmem_limit_bytes=60 * 2**20
        ),
    )(weights, vectors, boxes, segments, offsets, *kept)


def body(
    devices,
    word_vectors,
    position_table,
    horizontal_table,
    vertical_table,
    height_table,
    width_table,
    embed_gain,
    embed_shift,
    w_query,
    b_query,
    w_key,
    w_value,
    b_value,
    w_out,
    b_out,
    attn_gain,
    attn_shift,
    w_in,
    b_in,
    w_down,
    b_down,
    ffn_gain,
    ffn_shift,
    boxes,
    segments,
    offsets,
    cotangent,
):
    own_rows, width = word_vectors.shape
    owned = (position_table, horizontal_table, vertical_table, height_table, width_table)
    slab_rows = sum(table.shape[0] for table in owned)
    slab_padded = -(-slab_rows // 16) * 16
    slabs = owned
    if slab_padded > slab_rows or any(table.shape[0] % 16 for table in owned):
        slab = jnp.concatenate(owned, axis=0)
        slabs = (jnp.pad(slab, ((0, slab_padded - slab_rows), (0, 0))),)
    fourth = w_query.shape[0]
    bias_rows = jnp.concatenate([b_query, b_value, jnp.zeros((2 * fourth,), F32)])
    vectors = jnp.concatenate(
        [embed_gain, embed_shift, b_out, attn_gain, attn_shift, b_down, ffn_gain, ffn_shift]
        + [b_in, bias_rows, jnp.zeros((6 * width,), F32)]
    ).reshape(16, width)
    owns = tuple(table.shape[0] for table in owned)
    layer_out, grad_ffn_sum, ffn_vectors, weights, *kept = forward_all(
        devices,
        owns,
        slab_padded,
        slabs,
        (w_query, w_key, w_value, w_out, w_in, w_down),
        vectors,
        word_vectors,
        boxes,
        segments,
        offsets,
        cotangent,
    )
    grad_word, weight_sums, table_sum, vector_sum = backward_all(
        devices,
        owns,
        slab_padded,
        weights,
        vectors,
        boxes,
        segments,
        offsets,
        (grad_ffn_sum, ffn_vectors, *kept),
    )
    tall_sum, wide_sum, square_sum = weight_sums.astype(F32).reshape(3, width, width)
    table_sum = table_sum.astype(F32)
    first = [0]
    for own in owns:
        first.append(first[-1] + own)
    bias_in, bias_row = vector_sum[16], vector_sum[17]
    bias_query, bias_value = bias_row[:fourth], bias_row[2 * fourth : 3 * fourth]
    return (
        layer_out,
        grad_word,
        *(table_sum[first[k] : first[k + 1]] for k in range(5)),
        vector_sum[0],
        vector_sum[1],
        square_sum[:fourth],
        bias_query,
        square_sum[fourth : 2 * fourth],
        square_sum[2 * fourth : 3 * fourth],
        bias_value,
        square_sum[3 * fourth :],
        vector_sum[6],
        vector_sum[2],
        vector_sum[3],
        wide_sum,
        bias_in,
        tall_sum,
        vector_sum[7],
        vector_sum[4],
        vector_sum[5],
    )


def solution(mesh):
    devices = mesh.shape["dp"] * mesh.shape["tensor"]
    both = P(("dp", "tensor"), None)
    rows = P("tensor", None)
    return jax.shard_map(
        functools.partial(body, devices),
        mesh=mesh,
        in_specs=(
            *(both,) * 6,
            P(),
            P(),
            rows,
            P("tensor"),
            rows,
            rows,
            P("tensor"),
            rows,
            P(),
            P(),
            P(),
            P(None, "tensor"),
            P("tensor"),
            rows,
            P(),
            P(),
            P(),
            P(None, ("dp", "tensor")),
            P("dp", None),
            P("dp", None),
            both,
        ),
        out_specs=(
            *(both,) * 7,
            P(),
            P(),
            rows,
            P("tensor"),
            rows,
            rows,
            P("tensor"),
            rows,
            P(),
            P(),
            P(),
            P(None, "tensor"),
            P("tensor"),
            rows,
            P(),
            P(),
            P(),
        ),
        check_vma=False,
    )
```
